256 devices in a mesh: depth: 16 (over y, x), area: 16 (over z, core).
Axes of the slice: x: 4, y: 4, z: 8, core: 2. Of those that a mesh axis runs over, the one named last changes fastest.
Arguments:
- states: float32 [8, 256, 256, 768], P(None, 'depth', 'area'), may hold values from 0 to 1
- tissue: int32 [64, 64, 192], P('depth', 'area'), may hold values 0 or 1
- fiber: int32 [64, 64, 192], P('depth', 'area'), may hold values from 0 to 7
Outputs:
- final_states: float32 [8, 256, 256, 768], P(None, 'depth', 'area')
- images: float32 [2, 2, 4, 256, 768], P(None, None, None, 'area', 'depth')
The draws below stay inside these ranges and needn't reach their ends.
All inputs are finite; a program needn't handle non-finite values. No bound on the sum of `tissue` on one device may be relied on, other than what follows from the above.
Results may differ from the reference program's by a relative error of at most 0.0002.
Values sent between devices are 32-bit elements; how exact they have to be, the bound alone decides.
No kernel may reach another device: no remote copies, remote signals or barrier semaphores. Data moves between devices by JAX's collectives and lax.ppermute only.
A program may use at most 128 MiB of HBM per device.

```python
import math
import jax
import jax.numpy as jnp

NZ = 768
STATES = 8
BLK = 4
CLASSES = 8
STEPS = 2
NX = 256
NY = 256


def plant(drawn, key, smallest, largest):
    shape = drawn.shape
    place = [jax.random.randint(jax.random.fold_in(key, axis), (), 0, shape[axis]) for axis in range(len(shape))]
    drawn = drawn.at[tuple(place)].set(smallest)
    longest = shape.index(max(shape))
    place[longest] = (place[longest] + 1) % shape[longest]
    return drawn.at[tuple(place)].set(largest)


def level_of(stream_key, extent, shards, least, largest):
    def one(dim, shards_of):
        draws = jax.random.uniform(jax.random.fold_in(jax.random.fold_in(stream_key, 6), dim), (shards_of,), jnp.float32, least / len(shards), largest / len(shards))
        return jnp.repeat(jnp.exp(draws), extent[dim] // shards_of).reshape((-1,) + (1,) * (len(extent) - dim - 1))

    factor_of = one(*shards[0])
    for cut in shards[1:]:
        factor_of = factor_of * one(*cut)
    return factor_of


def setup_inputs(seed: int = 0) -> dict:
    streams_of = jax.random.split(jax.random.key(seed), 4)
    return {
        "states": jnp.clip(1.0 * jax.random.uniform(streams_of[0], (STATES, NX, NY, NZ), jnp.float32) ** level_of(streams_of[0], (STATES, NX, NY, NZ), ((1, 16), (2, 16)), -0.2, 0.2), 0.0, 1.0),
        "tissue": plant((jax.random.randint(streams_of[1], (NX // BLK, NY // BLK, NZ // BLK), 0, 4) < 3).astype(jnp.int32), jax.random.fold_in(streams_of[1], 1), 0, 1),
        "fiber": plant(jax.random.randint(streams_of[2], (NX // BLK, NY // BLK, NZ // BLK), 0, CLASSES), jax.random.fold_in(streams_of[2], 1), 0, CLASSES - 1).astype(jnp.int32),
    }


TIME_STEP = 0.15
SIGMA_LONG = 1.0
SIGMA_CROSS = 0.3
SLOPES = (8.0, -8.0, 6.0, 5.0, -5.0, -3.0)
MIDDLES = (0.2, 0.4, 0.3, 0.5, 0.6, 0.5)
RATES = (3.0, 0.5, 1.0, 0.8, 0.3, 0.1)
OPACITY = (0.012, 0.010)


def expand(blocks):
    first, second, third = blocks.shape
    wide = jnp.broadcast_to(blocks[:, None, :, None, :, None], (first, BLK, second, BLK, third, BLK))
    return wide.reshape(first * BLK, second * BLK, third * BLK)


def tensor(fiber):
    kind = fiber.astype(jnp.float32)
    polar = math.pi * (kind + 0.5) / CLASSES
    azimuth = 2.3 * kind
    along_x = jnp.cos(polar)
    along_y = jnp.sin(polar) * jnp.cos(azimuth)
    along_z = jnp.sin(polar) * jnp.sin(azimuth)
    spread = SIGMA_LONG - SIGMA_CROSS
    parts = (SIGMA_CROSS + spread * along_x * along_x, SIGMA_CROSS + spread * along_y * along_y,
             SIGMA_CROSS + spread * along_z * along_z, spread * along_x * along_y,
             spread * along_x * along_z, spread * along_y * along_z)
    return tuple(expand(item) for item in parts)


def diffuse(padded, comps):
    centre = padded[1:-1, 1:-1, 1:-1]
    second_x = padded[2:, 1:-1, 1:-1] - 2.0 * centre + padded[:-2, 1:-1, 1:-1]
    second_y = padded[1:-1, 2:, 1:-1] - 2.0 * centre + padded[1:-1, :-2, 1:-1]
    second_z = padded[1:-1, 1:-1, 2:] - 2.0 * centre + padded[1:-1, 1:-1, :-2]
    cross_xy = 0.25 * (padded[2:, 2:, 1:-1] - padded[2:, :-2, 1:-1] - padded[:-2, 2:, 1:-1] + padded[:-2, :-2, 1:-1])
    cross_xz = 0.25 * (padded[2:, 1:-1, 2:] - padded[2:, 1:-1, :-2] - padded[:-2, 1:-1, 2:] + padded[:-2, 1:-1, :-2])
    cross_yz = 0.25 * (padded[1:-1, 2:, 2:] - padded[1:-1, 2:, :-2] - padded[1:-1, :-2, 2:] + padded[1:-1, :-2, :-2])
    dxx, dyy, dzz, dxy, dxz, dyz = comps
    return dxx * second_x + dyy * second_y + dzz * second_z + 2.0 * (dxy * cross_xy + dxz * cross_xz + dyz * cross_yz)


def ionic(voltage, gates, calcium):
    fresh = []
    for k in range(6):
        steady = jax.nn.sigmoid(SLOPES[k] * (voltage - MIDDLES[k]))
        fresh.append(steady + (gates[k] - steady) * math.exp(-TIME_STEP * RATES[k]))
    current = (2.0 * fresh[0] * fresh[0] * fresh[0] * fresh[1] * (voltage - 1.2)
               + fresh[2] * fresh[2] * (voltage + 0.1)
               + 0.6 * fresh[3] * fresh[4] * (voltage - 0.9)
               + 0.2 * (1.0 + fresh[5]) * (voltage - 0.05))
    volt_next = voltage - TIME_STEP * current
    calc_next = calcium + TIME_STEP * (1.5 * fresh[3] * fresh[4] * (1.0 - calcium) - 0.8 * calcium)
    return volt_next, fresh, calc_next


def emission(field, tissue_float, which):
    alpha = OPACITY[which] * tissue_float * jax.nn.sigmoid(6.0 * (field - 0.4))
    red = jax.nn.sigmoid(5.0 * (field - 0.5))
    green = jnp.exp(-6.0 * (field - 0.5) * (field - 0.5))
    return alpha, (red, green, 1.0 - red)


def march(alpha, colours):
    through = jnp.cumprod(1.0 - alpha, axis=0)
    before = jnp.concatenate([jnp.ones_like(through[:1]), through[:-1]], axis=0)
    weight = before * alpha
    colour = jnp.stack([jnp.sum(weight * item, axis=0) for item in colours])
    return colour, through[-1]


def advance(voltage, gates, calcium, tissue_float, padded, comps):
    diffused = voltage + TIME_STEP * diffuse(padded, comps)
    volt_next, fresh, calc_next = ionic(diffused, gates, calcium)
    keep = 1.0 - tissue_float
    voltage = tissue_float * volt_next + keep * voltage
    gates = [tissue_float * item + keep * old for item, old in zip(fresh, gates)]
    calcium = tissue_float * calc_next + keep * calcium
    return voltage, gates, calcium


def reference(states, tissue, fiber):
    comps = tensor(fiber)
    tissue_float = expand(tissue).astype(jnp.float32)
    voltage = states[0]
    gates = [states[k] for k in range(1, 7)]
    calcium = states[7]
    images = []
    for step in range(STEPS):
        padded = jnp.pad(voltage * tissue_float, 1)
        voltage, gates, calcium = advance(voltage, gates, calcium, tissue_float, padded, comps)
        pictures = []
        for which, field in enumerate((voltage, calcium)):
            alpha, colours = emission(field, tissue_float, which)
            colour, through = march(alpha, colours)
            pictures.append(jnp.concatenate([colour, (1.0 - through)[None]], axis=0))
        images.append(jnp.stack(pictures))
    final_states = jnp.stack([voltage] + gates + [calcium])
    return final_states, jnp.stack(images)
```

```python
import math

import jax
import jax.numpy as jnp
from jax import lax
from jax.experimental import pallas as pl
from jax.experimental.pallas import tpu as pltpu
from jax.sharding import PartitionSpec as P

BLK = 4
CLASSES = 8
NX = 16
NY = 16
NZ = 768
STRIP = 48
HALF = STRIP // 2
PLANES = 4
CHUNK = 128

TIME_STEP = 0.15
SIGMA_LONG = 1.0
SIGMA_CROSS = 0.3
SLOPES = (8.0, -8.0, 6.0, 5.0, -5.0, -3.0)
MIDDLES = (0.2, 0.4, 0.3, 0.5, 0.6, 0.5)
RATES = (3.0, 0.5, 1.0, 0.8, 0.3, 0.1)
OPACITY = (0.012, 0.01)

f32 = jnp.float32
HIGHEST = lax.Precision.HIGHEST


def params(mib):
    return pltpu.CompilerParams(vmem_limit_bytes=mib * 2**20)


def is_even(axis):
    return lax.rem(lax.axis_index(axis), 2) == 0


def lane_spread(count):
    row = lax.broadcasted_iota(jnp.int32, (count, count * BLK), 0)
    column = lax.broadcasted_iota(jnp.int32, (count, count * BLK), 1)
    return row == lax.shift_right_logical(column, 2)


def row_spread(blocks):
    row = lax.broadcasted_iota(jnp.int32, (64, 16), 0)
    column = lax.broadcasted_iota(jnp.int32, (64, 16), 1)
    return jnp.dot((lax.shift_right_logical(row, 2) == column).astype(f32), blocks,
                   precision=HIGHEST, preferred_element_type=f32)


def faces_kernel(tissue_ref, v_ref, ev_ref, od_ref, row_lo_ref, row_hi_ref):
    tissue = tissue_ref[...].astype(f32)
    wide = jnp.dot(tissue.astype(jnp.bfloat16), lane_spread(NZ // BLK).astype(jnp.bfloat16),
                   preferred_element_type=f32)
    even = is_even("depth")
    row = lax.broadcasted_iota(jnp.int32, (NY, 1), 0)

    def mask_of(block):
        out = jnp.broadcast_to(wide[4 * block:4 * block + 1], (NY, NZ))
        for k in range(1, 4):
            out = jnp.where(row >= 4 * k, wide[4 * block + k:4 * block + k + 1], out)
        return out

    low = v_ref[0, 0] * mask_of(0)
    high = v_ref[0, NX - 1] * mask_of(3)
    ev_ref[...] = jnp.where(even, high, low)
    od_ref[...] = jnp.where(even, low, high)
    for x in range(NX):
        block = x // BLK
        row_lo_ref[x:x + 1] = v_ref[0, x, 0:1] * wide[4 * block:4 * block + 1]
        row_hi_ref[x:x + 1] = v_ref[0, x, NY - 1:NY] * wide[4 * block + 3:4 * block + 4]


def coefs_kernel(tissue_ref, fiber_ref, out_ref):
    kind = fiber_ref[...].astype(f32)
    polar = math.pi * (kind + 0.5) / CLASSES
    azimuth = 2.3 * kind
    along_x = jnp.cos(polar)
    ring = jnp.sin(polar)
    along_y = ring * jnp.cos(azimuth)
    along_z = ring * jnp.sin(azimuth)
    spread = SIGMA_LONG - SIGMA_CROSS
    t = TIME_STEP
    parts = (
        tissue_ref[...].astype(f32),
        t * (SIGMA_CROSS + spread * along_x * along_x),
        t * (SIGMA_CROSS + spread * along_y * along_y),
        t * (SIGMA_CROSS + spread * along_z * along_z),
        (0.5 * t) * (spread * along_x * along_y),
        (0.5 * t) * (spread * along_x * along_z),
        (0.5 * t) * (spread * along_y * along_z),
    )
    onehot = lane_spread(NZ // BLK).astype(f32)
    for k, part in enumerate(parts):
        out_ref[k] = jnp.dot(row_spread(part), onehot, precision=HIGHEST, preferred_element_type=f32)


def message_kernel(rcv_ev_ref, rcv_od_ref, row_lo_ref, row_hi_ref, ev_ref, od_ref):
    depth_even = is_even("depth")
    area_even = is_even("area")

    def pick(flag, a, b):
        return jnp.where(flag, a, b)

    lo = row_lo_ref[...]
    hi = row_hi_ref[...]
    ev_ref[0:NX] = pick(area_even, hi, lo)
    od_ref[0:NX] = pick(area_even, lo, hi)
    for place, first, second in ((NX, rcv_od_ref, rcv_ev_ref), (NX + 1, rcv_ev_ref, rcv_od_ref)):
        low = pick(depth_even, first[0:1], second[0:1])
        high = pick(depth_even, first[NY - 1:NY], second[NY - 1:NY])
        ev_ref[place:place + 1] = pick(area_even, high, low)
        od_ref[place:place + 1] = pick(area_even, low, high)


def z_sides(u):
    lane = lax.broadcasted_iota(jnp.int32, (1, NZ), 1)
    after = jnp.where(lane == NZ - 1, 0.0, pltpu.roll(u, NZ - 1, axis=1))
    before = jnp.where(lane == 0, 0.0, pltpu.roll(u, 1, axis=1))
    return after, before


def y_sides(u, row_lo, row_hi):
    row = lax.broadcasted_iota(jnp.int32, (NY, 1), 0)
    after = jnp.where(row == NY - 1, row_hi, pltpu.roll(u, NY - 1, axis=0))
    before = jnp.where(row == 0, row_lo, pltpu.roll(u, 1, axis=0))
    return after, before


def derive(v_ref, coefs_ref, depth_refs, area_refs, u_s, uy_s, uz_s, w_s, lo_s, hi_s, loz_s, hiz_s):
    depth_even = is_even("depth")
    area_even = is_even("area")
    lo_s[0:18] = jnp.where(area_even, area_refs[1][...], area_refs[0][...])
    hi_s[0:18] = jnp.where(area_even, area_refs[0][...], area_refs[1][...])
    for source, target in ((lo_s, loz_s), (hi_s, hiz_s)):
        after, before = z_sides(source[...])
        target[...] = after - before
    for place, where, flip in ((NX, 0, 1), (NX + 1, NX + 1, 0)):
        u = jnp.where(depth_even, depth_refs[flip][...], depth_refs[1 - flip][...])
        after, before = z_sides(u)
        uz_s[where] = after - before
        after, before = y_sides(u, lo_s[place:place + 1], hi_s[place:place + 1])
        uy_s[where] = after - before
        u_s[where] = u

    def plane(x, carry):
        rows = pl.ds(pl.multiple_of(lax.shift_right_logical(x, 2) * NY, NY), NY)
        u = v_ref[0, x] * coefs_ref[0, rows]
        u_s[x + 1] = u
        after, before = z_sides(u)
        uz = after - before
        uz_s[x + 1] = uz
        w = 0.52 * u + coefs_ref[3, rows] * (after + before)
        after, before = y_sides(u, lo_s[pl.ds(x, 1)], hi_s[pl.ds(x, 1)])
        uy_s[x + 1] = after - before
        w = w + coefs_ref[2, rows] * (after + before)
        after, before = y_sides(uz, loz_s[pl.ds(x, 1)], hiz_s[pl.ds(x, 1)])
        w_s[x] = w + coefs_ref[6, rows] * (after - before)
        return carry

    lax.fori_loop(0, NX, plane, 0)


def ionic(w, gates, calcium):
    fresh = []
    for k in range(6):
        keep = math.exp(-TIME_STEP * RATES[k])
        half = 0.5 * (1.0 - keep)
        t = jnp.tanh((0.5 * SLOPES[k]) * w - (0.5 * SLOPES[k] * MIDDLES[k]))
        fresh.append(half * t + (keep * gates[k] + half))
    both = fresh[3] * fresh[4]
    cube = fresh[0] * fresh[0] * fresh[0]
    loss = (
        (2.0 * TIME_STEP) * (cube * fresh[1]) * (w - 1.2)
        + TIME_STEP * (fresh[2] * fresh[2]) * (w + 0.1)
        + (0.6 * TIME_STEP) * both * (w - 0.9)
        + (0.2 * TIME_STEP) * (1.0 + fresh[5]) * (w - 0.05)
    )
    gain = (1.5 * TIME_STEP) * both
    calc_next = (1.0 - 0.8 * TIME_STEP) * calcium + gain * (1.0 - calcium)
    return w - loss, fresh, calc_next


def march(q, opaque, state):
    passed, red, green = state
    alpha = opaque * jnp.tanh(3.0 * q - 1.2) + opaque
    weight = passed * alpha
    off = q - 0.5
    red = red + weight * jnp.tanh(2.5 * off)
    green = green + weight * jnp.exp(-6.0 * (off * off))
    return passed - weight, red, green


def step_body(last, refs):
    (states_ref, v_ref, coefs_ref, dev_ref, dod_ref, aev_ref, aod_ref) = refs[:7]
    if last:
        earlier_ref, out_ref, strips_ref = refs[7:10]
        scratch = refs[10:]
    else:
        out_ref, shown_ref, ev_ref, od_ref, row_lo_ref, row_hi_ref = refs[7:13]
        scratch = refs[13:]
    u_s, uy_s, uz_s, w_s, lo_s, hi_s, loz_s, hiz_s, acc_s = scratch
    i = pl.program_id(0)

    @pl.when(i == 0)
    def _():
        derive(v_ref, coefs_ref, (dev_ref, dod_ref), (aev_ref, aod_ref),
               u_s, uy_s, uz_s, w_s, lo_s, hi_s, loz_s, hiz_s)
        for k in range(6):
            acc_s[k] = jnp.full((NY, NZ), 1.0 if k % 3 == 0 else 0.0, f32)

    rows = pl.ds(pl.multiple_of(i * NY, NY), NY)

    def chunk(j, carry):
        cols = pl.ds(pl.multiple_of(j * CHUNK, CHUNK), CHUNK)
        m = coefs_ref[0, rows, cols]
        inside = m > 0.5
        opaque = (0.5 * OPACITY[0] * m, 0.5 * OPACITY[1] * m)
        cxx = coefs_ref[1, rows, cols]
        cxy = coefs_ref[4, rows, cols]
        cxz = coefs_ref[5, rows, cols]
        marches = [tuple(acc_s[3 * f + k, :, cols] for k in range(3)) for f in range(2)]
        for p in range(PLANES):
            x = i * PLANES + p
            w = (
                w_s[x, :, cols]
                + cxx * (u_s[x + 2, :, cols] + u_s[x, :, cols])
                + cxy * (uy_s[x + 2, :, cols] - uy_s[x, :, cols])
                + cxz * (uz_s[x + 2, :, cols] - uz_s[x, :, cols])
            )
            old = [states_ref[k, p, :, cols] for k in range(8)]
            volt, fresh, calc = ionic(w, old[1:7], old[7])
            new = [jnp.where(inside, a, b) for a, b in zip([volt] + fresh + [calc], old)]
            for k in range(8):
                out_ref[k, p, :, cols] = new[k]
            marches = [march(q, o, s) for q, o, s in zip((new[0], new[7]), opaque, marches)]
        for f in range(2):
            for k in range(3):
                acc_s[3 * f + k, :, cols] = marches[f][k]
        return carry

    lax.fori_loop(0, NZ // CHUNK, chunk, 0)

    if not last:
        even = is_even("depth")
        for block in range(NX // PLANES):
            @pl.when(i == block)
            def _():
                for p in range(PLANES):
                    x = block * PLANES + p
                    first, final = block * NY, block * NY + NY - 1
                    row_lo_ref[x:x + 1] = out_ref[0, p, 0:1] * coefs_ref[0, first:first + 1]
                    row_hi_ref[x:x + 1] = out_ref[0, p, NY - 1:NY] * coefs_ref[0, final:final + 1]

        @pl.when(i == 0)
        def _():
            u = out_ref[0, 0] * coefs_ref[0, 0:NY]
            ev_ref[...] = jnp.where(even, ev_ref[...], u)
            od_ref[...] = jnp.where(even, u, od_ref[...])

        @pl.when(i == NX // PLANES - 1)
        def _():
            u = out_ref[0, PLANES - 1] * coefs_ref[0, 3 * NY:4 * NY]
            ev_ref[...] = jnp.where(even, u, ev_ref[...])
            od_ref[...] = jnp.where(even, od_ref[...], u)
            shown_ref[...] = acc_s[...]
    else:
        @pl.when(i == NX // PLANES - 1)
        def _():
            for k in range(3):
                stack = jnp.concatenate(
                    [earlier_ref[k], earlier_ref[3 + k], acc_s[k], acc_s[3 + k]], axis=0)
                stack = jnp.concatenate([stack, pltpu.roll(stack, NZ - HALF, axis=1)], axis=0)
                turned = stack.T
                for d in range(NZ // STRIP):
                    strips_ref[d, HALF * k:HALF * (k + 1)] = turned[STRIP * d:STRIP * d + HALF]


def composite_kernel(strips_ref, out_ref):
    count = strips_ref.shape[0]
    passed = jnp.ones((HALF, 128), f32)
    red = jnp.zeros((HALF, 128), f32)
    green = jnp.zeros((HALF, 128), f32)
    for s in range(count):
        red = red + passed * strips_ref[s, HALF:2 * HALF]
        green = green + passed * strips_ref[s, 2 * HALF:3 * HALF]
        passed = passed * strips_ref[s, 0:HALF]
    solid = 1.0 - passed
    red = 0.5 * (solid + red)
    whole = jnp.concatenate([red, green, solid - red, solid, jnp.zeros((32, 128), f32)], axis=0)
    turned = whole.T
    first, second = turned[0:64], turned[64:128]
    lane = lax.broadcasted_iota(jnp.int32, (1, 128), 1)
    for c in range(4):
        a = pltpu.roll(first, (128 - HALF * c) % 128, axis=1) if c else first
        b = pltpu.roll(second, (128 + HALF - HALF * c) % 128, axis=1) if c != 1 else second
        o = jnp.where(lane < HALF, a, b)
        for k in range(4):
            out_ref[k // 2, k % 2, c] = o[NY * k:NY * (k + 1), 0:STRIP]


def full(shape):
    return pl.BlockSpec(shape, lambda i: (0,) * len(shape))


def run_step(last, states, coefs, depth, area, earlier=None):
    block = pl.BlockSpec((8, PLANES, NY, NZ), lambda i: (0, i, 0, 0))
    in_specs = [block, full((1, NX, NY, NZ)), full((7, 64, NZ)), full((NY, NZ)), full((NY, NZ)),
                full((18, NZ)), full((18, NZ))]
    args = [states, states, coefs, *depth, *area]
    out_specs = [block]
    out_shape = [jax.ShapeDtypeStruct((8, NX, NY, NZ), f32)]
    if last:
        in_specs.append(full((6, NY, NZ)))
        args.append(earlier)
        shapes = [(NZ // STRIP, 3 * HALF, 128)]
    else:
        shapes = [(6, NY, NZ)] + [(NY, NZ)] * 4
    out_specs += [full(s) for s in shapes]
    out_shape += [jax.ShapeDtypeStruct(s, f32) for s in shapes]
    scratch = [pltpu.VMEM((NX + 2, NY, NZ), f32)] * 3 + [pltpu.VMEM((NX, NY, NZ), f32)]
    scratch += [pltpu.VMEM((24, NZ), f32)] * 4 + [pltpu.VMEM((6, NY, NZ), f32)]
    return pl.pallas_call(
        lambda *refs: step_body(last, refs),
        grid=(NX // PLANES,),
        in_specs=in_specs,
        out_specs=out_specs,
        out_shape=out_shape,
        scratch_shapes=scratch,
        compiler_params=params(24),
        name="step_last" if last else "step_first",
    )(*args)


def swaps(axis):
    count = lax.axis_size(axis)
    even = [(i, i ^ 1) for i in range(count) if i ^ 1 < count]
    odd = [(i, ((i - 1) ^ 1) + 1) for i in range(1, count) if ((i - 1) ^ 1) + 1 < count]
    return even, odd


def exchange(axis, pair):
    even, odd = swaps(axis)
    return lax.ppermute(pair[0], axis, even), lax.ppermute(pair[1], axis, odd)


def halos(pair, row_lo, row_hi):
    depth = exchange("depth", pair)
    messages = pl.pallas_call(
        message_kernel,
        out_shape=[jax.ShapeDtypeStruct((18, NZ), f32)] * 2,
        compiler_params=params(1),
        name="area_message",
    )(*depth, row_lo, row_hi)
    return depth, exchange("area", messages)


def per_device(states, tissue, fiber):
    tissue = tissue.reshape(16, NZ // BLK)
    fiber = fiber.reshape(16, NZ // BLK)
    plane = jax.ShapeDtypeStruct((NY, NZ), f32)
    ev, od, row_lo, row_hi = pl.pallas_call(
        faces_kernel,
        grid=(1,),
        in_specs=[full((16, NZ // BLK)), full((1, NX, NY, NZ))],
        out_specs=[full((NY, NZ))] * 4,
        out_shape=[plane] * 4,
        compiler_params=params(4),
        name="faces",
    )(tissue, states)
    depth, area = halos((ev, od), row_lo, row_hi)
    coefs = pl.pallas_call(
        coefs_kernel,
        out_shape=jax.ShapeDtypeStruct((7, 64, NZ), f32),
        compiler_params=params(8),
        name="coefficients",
    )(tissue, fiber)
    states, shown, ev, od, row_lo, row_hi = run_step(False, states, coefs, depth, area)
    depth, area = halos((ev, od), row_lo, row_hi)
    states, strips = run_step(True, states, coefs, depth, area, shown)
    strips = lax.all_to_all(strips, "depth", split_axis=0, concat_axis=0, tiled=True)
    images = pl.pallas_call(
        composite_kernel,
        out_shape=jax.ShapeDtypeStruct((2, 2, 4, NY, STRIP), f32),
        compiler_params=params(4),
        name="composite",
    )(strips)
    return states, images


def solution(mesh):
    return jax.shard_map(
        per_device,
        mesh=mesh,
        in_specs=(
            P(None, "depth", "area", None),
            P("depth", "area", None),
            P("depth", "area", None),
        ),
        out_specs=(P(None, "depth", "area", None), P(None, None, None, "area", "depth")),
        check_vma=False,
    )
```

```python
import math

import jax
import jax.numpy as jnp
from jax import lax
from jax.experimental import pallas as pl
from jax.experimental.pallas import tpu as pltpu
from jax.sharding import PartitionSpec as P

BLK = 4
CLASSES = 8
NX = 16
NY = 16
NZ = 768
STRIP = 48
HALF = STRIP // 2
GROUP = 7
CHUNK = 128

TIME_STEP = 0.15
SIGMA_LONG = 1.0
SIGMA_CROSS = 0.3
SLOPES = (8.0, -8.0, 6.0, 5.0, -5.0, -3.0)
MIDDLES = (0.2, 0.4, 0.3, 0.5, 0.6, 0.5)
RATES = (3.0, 0.5, 1.0, 0.8, 0.3, 0.1)
OPACITY = (0.012, 0.01)

f32 = jnp.float32


def params(mib):
    return pltpu.CompilerParams(vmem_limit_bytes=mib * 2**20)


def is_even(axis):
    return lax.rem(lax.axis_index(axis), 2) == 0


def lane_spread(count):
    row = lax.broadcasted_iota(jnp.int32, (count, count * BLK), 0)
    column = lax.broadcasted_iota(jnp.int32, (count, count * BLK), 1)
    return row == lax.shift_right_logical(column, 2)


def flat(ref):
    return jnp.concatenate([ref[k] for k in range(NX // BLK)], axis=0)


def spread_y(wide, start):
    row = lax.broadcasted_iota(jnp.int32, (NY, 1), 0)
    out = jnp.broadcast_to(wide[start:start + 1], (NY, wide.shape[1]))
    for k in range(1, NY // BLK):
        out = jnp.where(row >= BLK * k, wide[start + k:start + k + 1], out)
    return out


def choose(first, a, b):
    return jnp.where(first, a, b)


def faces_kernel(tissue_ref, v_ref, ev_ref, od_ref, ends_ref):
    wide = jnp.dot(flat(tissue_ref).astype(f32).astype(jnp.bfloat16),
                   lane_spread(NZ // BLK).astype(jnp.bfloat16), preferred_element_type=f32)
    even = is_even("area")
    for x in range(NX):
        row = x // BLK * BLK
        low = v_ref[0, x, 0:1] * wide[row:row + 1]
        high = v_ref[0, x, NY - 1:NY] * wide[row + 3:row + 4]
        ev_ref[x:x + 1] = choose(even, high, low)
        od_ref[x:x + 1] = choose(even, low, high)
    ends_ref[0] = v_ref[0, 0] * spread_y(wide, 0)
    ends_ref[1] = v_ref[0, NX - 1] * spread_y(wide, 12)


def class_tables():
    spread = SIGMA_LONG - SIGMA_CROSS
    tables = [[] for _ in range(6)]
    for kind in range(CLASSES):
        polar = math.pi * (kind + 0.5) / CLASSES
        azimuth = 2.3 * kind
        f = (math.cos(polar), math.sin(polar) * math.cos(azimuth), math.sin(polar) * math.sin(azimuth))
        for k in range(3):
            tables[k].append(TIME_STEP * (SIGMA_CROSS + spread * f[k] * f[k]))
        for k, (a, b) in enumerate(((0, 1), (0, 2), (1, 2))):
            tables[3 + k].append(0.5 * TIME_STEP * spread * f[a] * f[b])
    return tables


def coefs_kernel(tissue_ref, fiber_ref, out_ref):
    kind = flat(fiber_ref)
    parts = [flat(tissue_ref).astype(f32)]
    for table in class_tables():
        part = jnp.full(kind.shape, table[0], f32)
        for c in range(1, CLASSES):
            part = jnp.where(kind == c, table[c], part)
        parts.append(part)
    rest = jnp.concatenate(parts, axis=0)
    onehot = lane_spread(NZ // BLK).astype(jnp.bfloat16)
    wide = None
    for _ in range(3):
        piece = rest.astype(jnp.bfloat16)
        rest = rest - piece.astype(f32)
        product = jnp.dot(piece, onehot, preferred_element_type=f32)
        wide = product if wide is None else wide + product
    for k in range(7):
        for block in range(4):
            out_ref[k, NY * block:NY * (block + 1)] = spread_y(wide, 16 * k + 4 * block)


def message_kernel(area_ev_ref, area_od_ref, ends_ref, ev_ref, od_ref):
    area_even = is_even("area")
    depth_even = is_even("depth")
    ev_ref[0:NY] = choose(depth_even, ends_ref[1], ends_ref[0])
    od_ref[0:NY] = choose(depth_even, ends_ref[0], ends_ref[1])
    for place, first, second in ((NY, area_od_ref, area_ev_ref), (NY + 1, area_ev_ref, area_od_ref)):
        low = choose(area_even, first[0:1], second[0:1])
        high = choose(area_even, first[NX - 1:NX], second[NX - 1:NX])
        ev_ref[place:place + 1] = choose(depth_even, high, low)
        od_ref[place:place + 1] = choose(depth_even, low, high)


def z_sides(u):
    lane = lax.broadcasted_iota(jnp.int32, (1, NZ), 1)
    after = jnp.where(lane == NZ - 1, 0.0, pltpu.roll(u, NZ - 1, axis=1))
    before = jnp.where(lane == 0, 0.0, pltpu.roll(u, 1, axis=1))
    return after, before


def y_sides(u, row_lo, row_hi):
    row = lax.broadcasted_iota(jnp.int32, (NY, 1), 0)
    after = jnp.where(row == NY - 1, row_hi, pltpu.roll(u, NY - 1, axis=0))
    before = jnp.where(row == 0, row_lo, pltpu.roll(u, 1, axis=0))
    return after, before


def derive(v_ref, coefs_ref, ev_ref, od_ref, u_s, uy_s, uz_s, w_s, lo_s, hi_s, loz_s, hiz_s):
    even = is_even("area")
    lo_s[...] = choose(even, od_ref[...], ev_ref[...])
    hi_s[...] = choose(even, ev_ref[...], od_ref[...])
    for source, target in ((lo_s, loz_s), (hi_s, hiz_s)):
        after, before = z_sides(source[...])
        target[...] = after - before

    def plane(x, carry):
        rows = pl.ds(pl.multiple_of(lax.shift_right_logical(x, 2) * NY, NY), NY)
        u = v_ref[0, x] * coefs_ref[0, rows]
        u_s[x] = u
        after, before = z_sides(u)
        uz = after - before
        uz_s[x] = uz
        w = 0.52 * u + coefs_ref[3, rows] * (after + before)
        after, before = y_sides(u, lo_s[pl.ds(x, 1)], hi_s[pl.ds(x, 1)])
        uy_s[x] = after - before
        w = w + coefs_ref[2, rows] * (after + before)
        after, before = y_sides(uz, loz_s[pl.ds(x, 1)], hiz_s[pl.ds(x, 1)])
        w_s[x] = w + coefs_ref[6, rows] * (after - before)
        return carry

    lax.fori_loop(0, NX, plane, 0)


def ionic(w, gates, calcium):
    fresh = []
    for k in range(6):
        keep = math.exp(-TIME_STEP * RATES[k])
        half = 0.5 * (1.0 - keep)
        t = jnp.tanh((0.5 * SLOPES[k]) * w - (0.5 * SLOPES[k] * MIDDLES[k]))
        fresh.append(half * t + (keep * gates[k] + half))
    both = fresh[3] * fresh[4]
    cube = fresh[0] * fresh[0] * fresh[0]
    loss = (
        (2.0 * TIME_STEP) * (cube * fresh[1]) * (w - 1.2)
        + TIME_STEP * (fresh[2] * fresh[2]) * (w + 0.1)
        + (0.6 * TIME_STEP) * both * (w - 0.9)
        + (0.2 * TIME_STEP) * (1.0 + fresh[5]) * (w - 0.05)
    )
    gain = (1.5 * TIME_STEP) * both
    calc_next = (1.0 - 0.8 * TIME_STEP) * calcium + gain * (1.0 - calcium)
    return w - loss, fresh, calc_next


def march(q, opaque, state):
    passed, red, green = state
    alpha = opaque * jnp.tanh(3.0 * q - 1.2) + opaque
    weight = passed * alpha
    off = q - 0.5
    red = red + weight * jnp.tanh(2.5 * off)
    green = green + weight * jnp.exp(-6.0 * (off * off))
    return passed - weight, red, green


def advance(w, old, inside):
    volt, fresh, calc = ionic(w, old[1:7], old[7])
    return [jnp.where(inside, a, b) for a, b in zip([volt] + fresh + [calc], old)]


def show(new, m, marches):
    return [march(q, (0.5 * OPACITY[f]) * m, marches[f]) for f, q in enumerate((new[0], new[7]))]


def interior_kernel(states_ref, v_ref, coefs_ref, area_ev_ref, area_od_ref,
                    out_ref, shown_ref, base_ref, row_lo_ref, row_hi_ref,
                    u_s, uy_s, uz_s, w_s, lo_s, hi_s, loz_s, hiz_s):
    j = pl.program_id(0)

    @pl.when(j == 0)
    def _():
        derive(v_ref, coefs_ref, area_ev_ref, area_od_ref,
               u_s, uy_s, uz_s, w_s, lo_s, hi_s, loz_s, hiz_s)

    cols = pl.ds(pl.multiple_of(j * CHUNK, CHUNK), CHUNK)
    for end, x, beside, sign in ((0, 0, 1, 1.0), (1, NX - 1, NX - 2, -1.0)):
        rows = pl.ds(x // BLK * NY, NY)
        base_ref[end] = (
            w_s[x, :, cols]
            + coefs_ref[1, rows, cols] * u_s[beside, :, cols]
            + sign * (coefs_ref[4, rows, cols] * uy_s[beside, :, cols]
                      + coefs_ref[5, rows, cols] * uz_s[beside, :, cols])
        )

    def planes(g, carry):
        marches = carry
        for p in range(GROUP):
            x = 1 + g * GROUP + p
            rows = pl.ds(pl.multiple_of(lax.shift_right_logical(x, 2) * NY, NY), NY)
            m = coefs_ref[0, rows, cols]
            w = (
                w_s[x, :, cols]
                + coefs_ref[1, rows, cols] * (u_s[x + 1, :, cols] + u_s[x - 1, :, cols])
                + coefs_ref[4, rows, cols] * (uy_s[x + 1, :, cols] - uy_s[x - 1, :, cols])
                + coefs_ref[5, rows, cols] * (uz_s[x + 1, :, cols] - uz_s[x - 1, :, cols])
            )
            new = advance(w, [states_ref[k, x] for k in range(8)], m > 0.5)
            for k in range(8):
                out_ref[k, x] = new[k]
            marches = show(new, m, marches)
        return marches

    one = jnp.ones((NY, CHUNK), f32)
    zero = jnp.zeros((NY, CHUNK), f32)
    marches = lax.fori_loop(0, (NX - 2) // GROUP, planes, [(one, zero, zero)] * 2)
    for f in range(2):
        for k in range(3):
            shown_ref[3 * f + k] = marches[f][k]
    for x in range(1, NX - 1):
        first = x // BLK * NY
        final = first + NY - 1
        row_lo_ref[x:x + 1] = out_ref[0, x, 0:1] * coefs_ref[0, first:first + 1, cols]
        row_hi_ref[x:x + 1] = out_ref[0, x, NY - 1:NY] * coefs_ref[0, final:final + 1, cols]


def ends_body(last, refs):
    states_ref, base_ref, coefs_ref, depth_ev_ref, depth_od_ref, shown_ref = refs[:6]
    if last:
        earlier_ref, _, out_ref, strips_ref, acc_s, uy_s, uz_s = refs[6:]
    else:
        (row_lo_ref, row_hi_ref, _, out_ref, images_ref, ev_ref, od_ref, ends_ref,
         acc_s, uy_s, uz_s) = refs[6:]
    i = pl.program_id(0)
    back = i == 1
    sign = jnp.where(back, 1.0, -1.0)
    use_ev = is_even("depth") == back
    halo = choose(use_ev, depth_ev_ref[...], depth_od_ref[...])
    u = halo[0:NY]
    after, before = z_sides(u)
    uz_s[...] = sign * (after - before)
    after, before = y_sides(u, halo[NY:NY + 1], halo[NY + 1:NY + 2])
    uy_s[...] = sign * (after - before)

    @pl.when(i == 0)
    def _():
        for k in range(6):
            acc_s[k] = jnp.full((NY, NZ), 1.0 if k % 3 == 0 else 0.0, f32)

    for j in range(NZ // CHUNK):
        cols = slice(j * CHUNK, (j + 1) * CHUNK)
        m = coefs_ref[0, :, cols]
        w = (
            base_ref[0, :, cols]
            + coefs_ref[1, :, cols] * u[:, cols]
            + coefs_ref[4, :, cols] * uy_s[:, cols]
            + coefs_ref[5, :, cols] * uz_s[:, cols]
        )
        new = advance(w, [states_ref[k, 0, :, cols] for k in range(8)], m > 0.5)
        for k in range(8):
            out_ref[k, 0, :, cols] = new[k]
        marches = [tuple(acc_s[3 * f + k, :, cols] for k in range(3)) for f in range(2)]
        marches = show(new, m, marches)
        for f in range(2):
            for k in range(3):
                acc_s[3 * f + k, :, cols] = marches[f][k]
        if not last:
            ends_ref[0, :, cols] = m * new[0]

    @pl.when(i == 0)
    def _():
        for f in range(2):
            passed = acc_s[3 * f]
            for k in (1, 2):
                acc_s[3 * f + k] = acc_s[3 * f + k] + passed * shown_ref[3 * f + k]
            acc_s[3 * f] = passed * shown_ref[3 * f]

    if not last:
        even = is_even("area")

        @pl.when(i == 0)
        def _():
            lo, hi = row_lo_ref[...], row_hi_ref[...]
            ev_ref[...] = choose(even, hi, lo)
            od_ref[...] = choose(even, lo, hi)

        for end, x in ((0, 0), (1, NX - 1)):
            @pl.when(i == end)
            def _():
                lo, hi = ends_ref[0, 0:1], ends_ref[0, NY - 1:NY]
                ev_ref[x:x + 1] = choose(even, hi, lo)
                od_ref[x:x + 1] = choose(even, lo, hi)

        @pl.when(back)
        def _():
            images_ref[...] = acc_s[...]
    else:
        @pl.when(back)
        def _():
            for k in range(3):
                stack = jnp.concatenate(
                    [earlier_ref[k], earlier_ref[3 + k], acc_s[k], acc_s[3 + k]], axis=0)
                stack = jnp.concatenate([stack, pltpu.roll(stack, NZ - HALF, axis=1)], axis=0)
                turned = stack.T
                for d in range(NZ // STRIP):
                    strips_ref[d, HALF * k:HALF * (k + 1)] = turned[STRIP * d:STRIP * d + HALF]


def composite_kernel(strips_ref, out_ref):
    count = strips_ref.shape[0]
    passed = jnp.ones((HALF, 128), f32)
    red = jnp.zeros((HALF, 128), f32)
    green = jnp.zeros((HALF, 128), f32)
    for s in range(count):
        red = red + passed * strips_ref[s, HALF:2 * HALF]
        green = green + passed * strips_ref[s, 2 * HALF:3 * HALF]
        passed = passed * strips_ref[s, 0:HALF]
    solid = 1.0 - passed
    red = 0.5 * (solid + red)
    whole = jnp.concatenate([red, green, solid - red, solid, jnp.zeros((32, 128), f32)], axis=0)
    turned = whole.T
    first, second = turned[0:64], turned[64:128]
    lane = lax.broadcasted_iota(jnp.int32, (1, 128), 1)
    for c in range(4):
        a = pltpu.roll(first, (128 - HALF * c) % 128, axis=1) if c else first
        b = pltpu.roll(second, (128 + HALF - HALF * c) % 128, axis=1) if c != 1 else second
        o = jnp.where(lane < HALF, a, b)
        for k in range(4):
            out_ref[k // 2, k % 2, c] = o[NY * k:NY * (k + 1), 0:STRIP]


def full(shape):
    return pl.BlockSpec(shape, lambda *_: (0,) * len(shape))


def interior(states, coefs, area):
    block = pl.BlockSpec((8, NX, NY, CHUNK), lambda j: (0, 0, 0, j))
    row = pl.BlockSpec((NX, CHUNK), lambda j: (0, j))
    voxels = NX * NY * NZ
    return pl.pallas_call(
        interior_kernel,
        grid=(NZ // CHUNK,),
        in_specs=[block, full((1, NX, NY, NZ)), full((7, 64, NZ)), full((NX, NZ)), full((NX, NZ))],
        out_specs=[block, pl.BlockSpec((6, NY, CHUNK), lambda j: (0, 0, j)),
                   pl.BlockSpec((2, NY, CHUNK), lambda j: (0, 0, j)), row, row],
        out_shape=[jax.ShapeDtypeStruct(s, f32) for s in
                   ((8, NX, NY, NZ), (6, NY, NZ), (2, NY, NZ), (NX, NZ), (NX, NZ))],
        scratch_shapes=[pltpu.VMEM((NX, NY, NZ), f32)] * 4 + [pltpu.VMEM((NX, NZ), f32)] * 4,
        compiler_params=params(24),
        cost_estimate=pl.CostEstimate(flops=400 * voxels, bytes_accessed=64 * voxels,
                                      transcendentals=12 * voxels),
        name="interior",
    )(states, states, coefs, *area)


def ends(last, states, base, coefs, depth, shown, extra, new):
    plane = pl.BlockSpec((8, 1, NY, NZ), lambda i: (0, (NX - 1) * i, 0, 0))
    end = pl.BlockSpec((1, NY, NZ), lambda i: (i, 0, 0))
    in_specs = [plane, end, pl.BlockSpec((7, NY, NZ), lambda i: (0, 3 * i, 0)),
                full((NY + 2, NZ)), full((NY + 2, NZ)), full((6, NY, NZ))]
    in_specs += [full(item.shape) for item in extra] + [pl.BlockSpec(memory_space=pl.ANY)]
    args = [states, base, coefs, *depth, shown, *extra, new]
    out_specs = [plane]
    out_shape = [new.shape]
    if last:
        out_shape += [(NZ // STRIP, 3 * HALF, 128)]
        out_specs += [full(out_shape[1])]
    else:
        out_shape += [(6, NY, NZ), (NX, NZ), (NX, NZ), (2, NY, NZ)]
        out_specs += [full((6, NY, NZ)), full((NX, NZ)), full((NX, NZ)), end]
    return pl.pallas_call(
        lambda *refs: ends_body(last, refs),
        grid=(2,),
        in_specs=in_specs,
        out_specs=out_specs,
        out_shape=[jax.ShapeDtypeStruct(s, f32) for s in out_shape],
        scratch_shapes=[pltpu.VMEM((6, NY, NZ), f32)] + [pltpu.VMEM((NY, NZ), f32)] * 2,
        input_output_aliases={len(args) - 1: 0},
        compiler_params=params(16),
        name="ends_last" if last else "ends_first",
    )(*args)


def swaps(axis):
    count = lax.axis_size(axis)
    even = [(i, i ^ 1) for i in range(count) if i ^ 1 < count]
    odd = [(i, ((i - 1) ^ 1) + 1) for i in range(1, count) if ((i - 1) ^ 1) + 1 < count]
    return even, odd


def exchange(axis, pair):
    even, odd = swaps(axis)
    return lax.ppermute(pair[0], axis, even), lax.ppermute(pair[1], axis, odd)


def depth_halo(area, ends_planes):
    messages = pl.pallas_call(
        message_kernel,
        out_shape=[jax.ShapeDtypeStruct((NY + 2, NZ), f32)] * 2,
        compiler_params=params(1),
        name="depth_message",
    )(*area, ends_planes)
    return exchange("depth", messages)


def per_device(states, tissue, fiber):
    blocks = (NX // BLK, NY // BLK, NZ // BLK)
    ev, od, planes = pl.pallas_call(
        faces_kernel,
        grid=(1,),
        in_specs=[full(blocks), full((1, NX, NY, NZ))],
        out_specs=[full((NX, NZ)), full((NX, NZ)), full((2, NY, NZ))],
        out_shape=[jax.ShapeDtypeStruct(s, f32) for s in ((NX, NZ), (NX, NZ), (2, NY, NZ))],
        compiler_params=params(58),
        name="faces",
    )(tissue, states)
    area = exchange("area", (ev, od))
    coefs = pl.pallas_call(
        coefs_kernel,
        out_shape=jax.ShapeDtypeStruct((7, 64, NZ), f32),
        compiler_params=params(8),
        name="coefficients",
    )(tissue, fiber)
    depth = depth_halo(area, planes)
    new, shown, base, row_lo, row_hi = interior(states, coefs, area)
    states, images, ev, od, planes = ends(
        False, states, base, coefs, depth, shown, (row_lo, row_hi), new)
    area = exchange("area", (ev, od))
    depth = depth_halo(area, planes)
    new, shown, base, _, _ = interior(states, coefs, area)
    states, strips = ends(True, states, base, coefs, depth, shown, (images,), new)
    strips = lax.all_to_all(strips, "depth", split_axis=0, concat_axis=0, tiled=True)
    images = pl.pallas_call(
        composite_kernel,
        out_shape=jax.ShapeDtypeStruct((2, 2, 4, NY, STRIP), f32),
        compiler_params=params(4),
        name="composite",
    )(strips)
    return states, images


def solution(mesh):
    return jax.shard_map(
        per_device,
        mesh=mesh,
        in_specs=(
            P(None, "depth", "area", None),
            P("depth", "area", None),
            P("depth", "area", None),
        ),
        out_specs=(P(None, "depth", "area", None), P(None, None, None, "area", "depth")),
        check_vma=False,
    )
```

```python
import math

import jax
import jax.numpy as jnp
from jax import lax
from jax.experimental import pallas as pl
from jax.experimental.pallas import tpu as pltpu
from jax.sharding import PartitionSpec as P

BLK = 4
CLASSES = 8
NX = 16
NY = 16
NZ = 768
STRIP = 48
HALF = STRIP // 2
CHUNK = 128
MID = 8
FACES_MIB = 4
INTERIOR_MIB = 4

TIME_STEP = 0.15
SIGMA_LONG = 1.0
SIGMA_CROSS = 0.3
SLOPES = (8.0, -8.0, 6.0, 5.0, -5.0, -3.0)
MIDDLES = (0.2, 0.4, 0.3, 0.5, 0.6, 0.5)
RATES = (3.0, 0.5, 1.0, 0.8, 0.3, 0.1)
OPACITY = (0.012, 0.01)

f32 = jnp.float32


def params(mib):
    return pltpu.CompilerParams(vmem_limit_bytes=mib * 2**20)


def is_even(axis):
    return lax.rem(lax.axis_index(axis), 2) == 0


def lane_spread(count):
    row = lax.broadcasted_iota(jnp.int32, (count, count * BLK), 0)
    column = lax.broadcasted_iota(jnp.int32, (count, count * BLK), 1)
    return row == lax.shift_right_logical(column, 2)


def flat(ref):
    return jnp.concatenate([ref[k] for k in range(NX // BLK)], axis=0)


def spread_y(wide, start):
    row = lax.broadcasted_iota(jnp.int32, (NY, 1), 0)
    out = jnp.broadcast_to(wide[start:start + 1], (NY, wide.shape[1]))
    for k in range(1, NY // BLK):
        out = jnp.where(row >= BLK * k, wide[start + k:start + k + 1], out)
    return out


def choose(first, a, b):
    return jnp.where(first, a, b)


def faces_kernel(tissue_ref, states_ref, u_ref, ev_ref, od_ref, v_s, sem):
    load = pltpu.make_async_copy(states_ref.at[0], v_s, sem)
    load.start()
    wide = jnp.dot(flat(tissue_ref).astype(f32).astype(jnp.bfloat16),
                   lane_spread(NZ // BLK).astype(jnp.bfloat16), preferred_element_type=f32)
    masks = [spread_y(wide, BLK * block) for block in range(NX // BLK)]
    load.wait()
    for x in range(NX):
        u_ref[x] = v_s[x] * masks[x // BLK]
    area_rows(u_ref, ev_ref, od_ref)


def area_rows(u_ref, ev_ref, od_ref):
    even = is_even("area")
    for x in range(NX):
        low = u_ref[x, 0:1]
        high = u_ref[x, NY - 1:NY]
        ev_ref[x:x + 1] = choose(even, high, low)
        od_ref[x:x + 1] = choose(even, low, high)


def class_tables():
    spread = SIGMA_LONG - SIGMA_CROSS
    tables = [[] for _ in range(6)]
    for kind in range(CLASSES):
        polar = math.pi * (kind + 0.5) / CLASSES
        azimuth = 2.3 * kind
        f = (math.cos(polar), math.sin(polar) * math.cos(azimuth), math.sin(polar) * math.sin(azimuth))
        for k in range(3):
            tables[k].append(TIME_STEP * (SIGMA_CROSS + spread * f[k] * f[k]))
        for k, (a, b) in enumerate(((0, 1), (0, 2), (1, 2))):
            tables[3 + k].append(0.5 * TIME_STEP * spread * f[a] * f[b])
    return tables


def coefs_kernel(tissue_ref, fiber_ref, out_ref):
    kind = flat(fiber_ref)
    parts = [flat(tissue_ref).astype(f32)]
    for table in class_tables():
        part = jnp.full(kind.shape, table[0], f32)
        for c in range(1, CLASSES):
            part = jnp.where(kind == c, table[c], part)
        parts.append(part)
    rest = jnp.concatenate(parts, axis=0)
    onehot = lane_spread(NZ // BLK).astype(jnp.bfloat16)
    wide = None
    for _ in range(3):
        piece = rest.astype(jnp.bfloat16)
        rest = rest - piece.astype(f32)
        product = jnp.dot(piece, onehot, preferred_element_type=f32)
        wide = product if wide is None else wide + product
    for k in range(7):
        for block in range(4):
            out_ref[k, NY * block:NY * (block + 1)] = spread_y(wide, 16 * k + 4 * block)


def message_kernel(area_ev_ref, area_od_ref, u_ref, ev_ref, od_ref):
    area_even = is_even("area")
    depth_even = is_even("depth")
    ev_ref[0:NY] = choose(depth_even, u_ref[NX - 1], u_ref[0])
    od_ref[0:NY] = choose(depth_even, u_ref[0], u_ref[NX - 1])
    for place, first, second in ((NY, area_od_ref, area_ev_ref), (NY + 1, area_ev_ref, area_od_ref)):
        low = choose(area_even, first[0:1], second[0:1])
        high = choose(area_even, first[NX - 1:NX], second[NX - 1:NX])
        ev_ref[place:place + 1] = choose(depth_even, high, low)
        od_ref[place:place + 1] = choose(depth_even, low, high)


def z_sides(u):
    lane = lax.broadcasted_iota(jnp.int32, (1, NZ), 1)
    after = jnp.where(lane == NZ - 1, 0.0, pltpu.roll(u, NZ - 1, axis=1))
    before = jnp.where(lane == 0, 0.0, pltpu.roll(u, 1, axis=1))
    return after, before


def y_sides(u, row_lo, row_hi):
    row = lax.broadcasted_iota(jnp.int32, (NY, 1), 0)
    after = jnp.where(row == NY - 1, row_hi, pltpu.roll(u, NY - 1, axis=0))
    before = jnp.where(row == 0, row_lo, pltpu.roll(u, 1, axis=0))
    return after, before


def derive(planes, u_ref, coefs_ref, ev_ref, od_ref, uy_ref, uz_ref, w_ref):
    even = is_even("area")
    row_lo = choose(even, od_ref[...], ev_ref[...])
    row_hi = choose(even, ev_ref[...], od_ref[...])
    after, before = z_sides(row_lo)
    rowz_lo = after - before
    after, before = z_sides(row_hi)
    rowz_hi = after - before
    for x in planes:
        rows = slice(x // BLK * NY, x // BLK * NY + NY)
        row = slice(x, x + 1)
        u = u_ref[x]
        after, before = z_sides(u)
        uz = after - before
        uz_ref[x] = uz
        w = 0.52 * u + coefs_ref[3, rows] * (after + before)
        after, before = y_sides(u, row_lo[row], row_hi[row])
        uy_ref[x] = after - before
        w = w + coefs_ref[2, rows] * (after + before)
        after, before = y_sides(uz, rowz_lo[row], rowz_hi[row])
        w_ref[x] = w + coefs_ref[6, rows] * (after - before)


def ionic(w, gates, calcium):
    fresh = []
    for k in range(6):
        keep = math.exp(-TIME_STEP * RATES[k])
        half = 0.5 * (1.0 - keep)
        t = jnp.tanh((0.5 * SLOPES[k]) * w - (0.5 * SLOPES[k] * MIDDLES[k]))
        fresh.append(half * t + (keep * gates[k] + half))
    both = fresh[3] * fresh[4]
    cube = fresh[0] * fresh[0] * fresh[0]
    loss = (
        (2.0 * TIME_STEP) * (cube * fresh[1]) * (w - 1.2)
        + TIME_STEP * (fresh[2] * fresh[2]) * (w + 0.1)
        + (0.6 * TIME_STEP) * both * (w - 0.9)
        + (0.2 * TIME_STEP) * (1.0 + fresh[5]) * (w - 0.05)
    )
    gain = (1.5 * TIME_STEP) * both
    calc_next = (1.0 - 0.8 * TIME_STEP) * calcium + gain * (1.0 - calcium)
    return w - loss, fresh, calc_next


def march(q, opaque, state):
    passed, red, green = state
    alpha = opaque * jnp.tanh(3.0 * q - 1.2) + opaque
    weight = passed * alpha
    off = q - 0.5
    red = red + weight * jnp.tanh(2.5 * off)
    green = green + weight * jnp.exp(-6.0 * (off * off))
    return passed - weight, red, green


def advance(w, old, inside):
    volt, fresh, calc = ionic(w, old[1:7], old[7])
    return [jnp.where(inside, a, b) for a, b in zip([volt] + fresh + [calc], old)]


def show(new, m, marches):
    return [march(q, (0.5 * OPACITY[f]) * m, marches[f]) for f, q in enumerate((new[0], new[7]))]


def interior_planes(planes, marches_of, s_ref, u_ref, next_ref, coefs_ref, uy_ref, uz_ref, w_ref, shown_ref):
    def chunk(j, carry):
        cols = pl.ds(pl.multiple_of(j * CHUNK, CHUNK), CHUNK)
        marches = marches_of(cols)
        for x in planes:
            rows = slice(x // BLK * NY, x // BLK * NY + NY)
            m = coefs_ref[0, rows, cols]
            w = (
                w_ref[x, :, cols]
                + coefs_ref[1, rows, cols] * (u_ref[x + 1, :, cols] + u_ref[x - 1, :, cols])
                + coefs_ref[4, rows, cols] * (uy_ref[x + 1, :, cols] - uy_ref[x - 1, :, cols])
                + coefs_ref[5, rows, cols] * (uz_ref[x + 1, :, cols] - uz_ref[x - 1, :, cols])
            )
            new = advance(w, [s_ref[k, x, :, cols] for k in range(8)], m > 0.5)
            for k in range(8):
                s_ref[k, x, :, cols] = new[k]
            next_ref[x, :, cols] = m * new[0]
            marches = show(new, m, marches)
        for f in range(2):
            for k in range(3):
                shown_ref[3 * f + k, :, cols] = marches[f][k]
        return carry

    lax.fori_loop(0, NZ // CHUNK, chunk, 0)


def base_of(x, beside, sign, u_ref, coefs_ref, uy_ref, uz_ref, w_ref):
    rows = slice(x // BLK * NY, x // BLK * NY + NY)
    return (
        w_ref[x]
        + coefs_ref[1, rows] * u_ref[beside]
        + sign * (coefs_ref[4, rows] * uy_ref[beside] + coefs_ref[5, rows] * uz_ref[beside])
    )


def front_body(last, refs):
    states_ref, u_ref, coefs_ref, area_ev_ref, area_od_ref, _ = refs[:6]
    s_ref, next_ref, uy_ref, uz_ref, w_ref, shown_ref, base_ref, _ = refs[6:14]
    loads = []
    if last:
        final_ref, sem = refs[14:]
    else:
        (sem,) = refs[14:]
        for k in range(2):
            half = pl.ds(k * MID, MID)
            loads.append(pltpu.make_async_copy(states_ref.at[:, half], s_ref.at[:, half], sem.at[k]))
            loads[k].start()
    derive(range(MID + 1), u_ref, coefs_ref, area_ev_ref, area_od_ref, uy_ref, uz_ref, w_ref)
    base_ref[...] = base_of(0, 1, 1.0, u_ref, coefs_ref, uy_ref, uz_ref, w_ref)
    if not last:
        loads[0].wait()
    one = jnp.ones((NY, CHUNK), f32)
    zero = jnp.zeros((NY, CHUNK), f32)
    interior_planes(range(1, MID), lambda cols: [(one, zero, zero)] * 2,
                    s_ref, u_ref, next_ref, coefs_ref, uy_ref, uz_ref, w_ref, shown_ref)
    if last:
        done = pl.ds(1, MID - 1)
        store = pltpu.make_async_copy(s_ref.at[:, done], final_ref.at[:, done], sem)
        store.start()
        store.wait()
    else:
        loads[1].wait()


def back_body(last, refs):
    u_ref, coefs_ref, area_ev_ref, area_od_ref = refs[:4]
    outs = refs[11:] if last else refs[10:]
    s_ref, next_ref, uy_ref, uz_ref, w_ref, shown_ref, base_ref = outs[:7]
    derive(range(MID + 1, NX), u_ref, coefs_ref, area_ev_ref, area_od_ref, uy_ref, uz_ref, w_ref)
    base_ref[...] = base_of(NX - 1, NX - 2, -1.0, u_ref, coefs_ref, uy_ref, uz_ref, w_ref)
    interior_planes(range(MID, NX - 1),
                    lambda cols: [tuple(shown_ref[3 * f + k, :, cols] for k in range(3)) for f in range(2)],
                    s_ref, u_ref, next_ref, coefs_ref, uy_ref, uz_ref, w_ref, shown_ref)
    if last:
        final_ref, sem = outs[7:]
        done = pl.ds(MID, NX - 1 - MID)
        store = pltpu.make_async_copy(s_ref.at[:, done], final_ref.at[:, done], sem)
        store.start()
        store.wait()


def ends_body(last, refs):
    base_lo_ref, base_hi_ref, coefs_ref, depth_ev_ref, depth_od_ref, shown_ref = refs[:6]
    if last:
        earlier_ref, _, _, s_ref, final_ref, strips_ref, acc_s, uy_s, uz_s, sem = refs[6:]
    else:
        _, _, s_ref, next_ref, acc_s, ev_ref, od_ref, uy_s, uz_s = refs[6:]
    even = is_even("depth")
    stores = []
    for end, x, base_ref, sign in ((0, 0, base_lo_ref, -1.0), (1, NX - 1, base_hi_ref, 1.0)):
        if end == 1:
            use_ev = even
        else:
            use_ev = jnp.logical_not(even)
        rows = slice(x // BLK * NY, x // BLK * NY + NY)
        halo = choose(use_ev, depth_ev_ref[...], depth_od_ref[...])
        u = halo[0:NY]
        after, before = z_sides(u)
        uz_s[...] = sign * (after - before)
        after, before = y_sides(u, halo[NY:NY + 1], halo[NY + 1:NY + 2])
        uy_s[...] = sign * (after - before)
        for j in range(NZ // CHUNK):
            cols = slice(j * CHUNK, (j + 1) * CHUNK)
            m = coefs_ref[0, rows, cols]
            w = (
                base_ref[:, cols]
                + coefs_ref[1, rows, cols] * u[:, cols]
                + coefs_ref[4, rows, cols] * uy_s[:, cols]
                + coefs_ref[5, rows, cols] * uz_s[:, cols]
            )
            new = advance(w, [s_ref[k, x, :, cols] for k in range(8)], m > 0.5)
            for k in range(8):
                s_ref[k, x, :, cols] = new[k]
            if not last:
                next_ref[x, :, cols] = m * new[0]
            if end == 0:
                one = jnp.ones((NY, CHUNK), f32)
                zero = jnp.zeros((NY, CHUNK), f32)
                marches = show(new, m, [(one, zero, zero)] * 2)
            else:
                marches = [tuple(acc_s[3 * f + k, :, cols] for k in range(3)) for f in range(2)]
                marches = show(new, m, marches)
            for f in range(2):
                passed, red, green = marches[f]
                if end == 0:
                    red = red + passed * shown_ref[3 * f + 1, :, cols]
                    green = green + passed * shown_ref[3 * f + 2, :, cols]
                    passed = passed * shown_ref[3 * f, :, cols]
                for k, item in enumerate((passed, red, green)):
                    acc_s[3 * f + k, :, cols] = item
        if last:
            stores.append(pltpu.make_async_copy(s_ref.at[:, x], final_ref.at[:, x], sem.at[end]))
            stores[end].start()
    if not last:
        area_rows(next_ref, ev_ref, od_ref)
    else:
        for k in range(3):
            stack = jnp.concatenate(
                [earlier_ref[k], earlier_ref[3 + k], acc_s[k], acc_s[3 + k]], axis=0)
            stack = jnp.concatenate([stack, pltpu.roll(stack, NZ - HALF, axis=1)], axis=0)
            turned = stack.T
            for d in range(NZ // STRIP):
                strips_ref[d, HALF * k:HALF * (k + 1)] = turned[STRIP * d:STRIP * d + HALF]
        for store in stores:
            store.wait()


def composite_kernel(strips_ref, out_ref):
    count = strips_ref.shape[0]
    passed = jnp.ones((HALF, 128), f32)
    red = jnp.zeros((HALF, 128), f32)
    green = jnp.zeros((HALF, 128), f32)
    for s in range(count):
        red = red + passed * strips_ref[s, HALF:2 * HALF]
        green = green + passed * strips_ref[s, 2 * HALF:3 * HALF]
        passed = passed * strips_ref[s, 0:HALF]
    solid = 1.0 - passed
    red = 0.5 * (solid + red)
    whole = jnp.concatenate([red, green, solid - red, solid, jnp.zeros((32, 128), f32)], axis=0)
    turned = whole.T
    first, second = turned[0:64], turned[64:128]
    lane = lax.broadcasted_iota(jnp.int32, (1, 128), 1)
    for c in range(4):
        a = pltpu.roll(first, (128 - HALF * c) % 128, axis=1) if c else first
        b = pltpu.roll(second, (128 + HALF - HALF * c) % 128, axis=1) if c != 1 else second
        o = jnp.where(lane < HALF, a, b)
        for k in range(4):
            out_ref[k // 2, k % 2, c] = o[NY * k:NY * (k + 1), 0:STRIP]


VOLUME = (8, NX, NY, NZ)
FIELD = (NX, NY, NZ)
PLANE = (NY, NZ)
SHOWN = (6, NY, NZ)
COPY = pltpu.SemaphoreType.DMA


def shapes_of(*shapes):
    return [jax.ShapeDtypeStruct(s, f32) for s in shapes]


def kept_in(space, *shapes):
    return [space(s, f32) for s in shapes]


def anywhere():
    return pl.BlockSpec(memory_space=pl.ANY)


def inside():
    return pl.BlockSpec(memory_space=pltpu.VMEM)


def cost():
    voxels = NX * NY * NZ // 2
    return pl.CostEstimate(flops=400 * voxels, bytes_accessed=32 * voxels, transcendentals=12 * voxels)


def interior_front(last, states, u, coefs, area, passing):
    out_shape = kept_in(pltpu.VMEM, VOLUME, FIELD, FIELD, FIELD, FIELD, SHOWN, PLANE) + shapes_of(passing.shape)
    out_specs = [inside()] * 7 + [anywhere()]
    aliases = {5: 7}
    if last:
        aliases[0] = 0
        out_shape += kept_in(pltpu.HBM, VOLUME)
        out_specs += [anywhere()]
        scratch = [COPY]
    else:
        scratch = [COPY((2,))]
    return pl.pallas_call(
        lambda *refs: front_body(last, refs),
        in_specs=[inside() if last else anywhere()] + [inside()] * 4 + [anywhere()],
        out_specs=out_specs,
        out_shape=out_shape,
        scratch_shapes=scratch,
        input_output_aliases=aliases,
        compiler_params=params(INTERIOR_MIB),
        cost_estimate=cost(),
        name="front_last" if last else "front_first",
    )(states, u, coefs, *area, passing)


def interior_back(last, u, coefs, area, kept):
    out_shape = kept_in(pltpu.VMEM, VOLUME, FIELD, FIELD, FIELD, FIELD, SHOWN, PLANE)
    out_specs = [inside()] * 7
    in_specs = [inside()] * 10
    aliases = {4 + k: k for k in range(6)}
    scratch = []
    if last:
        in_specs += [anywhere()]
        out_shape += kept_in(pltpu.HBM, VOLUME)
        out_specs += [anywhere()]
        aliases[10] = 7
        scratch = [COPY]
    return pl.pallas_call(
        lambda *refs: back_body(last, refs),
        in_specs=in_specs,
        out_specs=out_specs,
        out_shape=out_shape,
        scratch_shapes=scratch,
        input_output_aliases=aliases,
        compiler_params=params(INTERIOR_MIB),
        cost_estimate=cost(),
        name="back_last" if last else "back_first",
    )(u, coefs, *area, *kept)


def ends(last, bases, coefs, depth, shown, rest):
    args = [*bases, coefs, *depth, shown, *rest]
    in_specs = [inside()] * len(args)
    if last:
        in_specs[-1] = anywhere()
        out_shape = kept_in(pltpu.VMEM, VOLUME) + kept_in(pltpu.HBM, VOLUME) + shapes_of((NZ // STRIP, 3 * HALF, 128))
        out_specs = [inside(), anywhere(), inside()]
        scratch = [pltpu.VMEM(SHOWN, f32)]
    else:
        out_shape = kept_in(pltpu.VMEM, VOLUME, FIELD, SHOWN, (NX, NZ), (NX, NZ))
        out_specs = [inside()] * 5
        scratch = []
    scratch += [pltpu.VMEM(PLANE, f32)] * 2
    if last:
        scratch += [COPY((2,))]
    return pl.pallas_call(
        lambda *refs: ends_body(last, refs),
        in_specs=in_specs,
        out_specs=out_specs,
        out_shape=out_shape,
        scratch_shapes=scratch,
        input_output_aliases={len(args) - 2: 0, len(args) - 1: 1},
        compiler_params=params(4),
        name="ends_last" if last else "ends_first",
    )(*args)


def depth_messages(area, u):
    return pl.pallas_call(
        message_kernel,
        out_shape=shapes_of((NY + 2, NZ), (NY + 2, NZ)),
        compiler_params=params(1),
        name="depth_message",
    )(*area, u)


def swaps(axis):
    count = lax.axis_size(axis)
    even = [(i, i ^ 1) for i in range(count) if i ^ 1 < count]
    odd = [(i, ((i - 1) ^ 1) + 1) for i in range(1, count) if ((i - 1) ^ 1) + 1 < count]
    return even, odd


def swap(axis, which, message):
    return lax.ppermute(message, axis, swaps(axis)[which])


def half_step(last, states, u, coefs, area):
    messages = depth_messages(area, u)
    even = swap("depth", 0, messages[0])
    states, after, uy, uz, w, shown, low, passing, *final = interior_front(
        last, states, u, coefs, area, messages[1])
    odd = swap("depth", 1, passing)
    kept = (states, after, uy, uz, w, shown, *final)
    states, after, _, _, _, shown, high, *final = interior_back(last, u, coefs, area, kept)
    return states, after, shown, (low, high), (even, odd), final


def per_device(states, tissue, fiber):
    states = pltpu.with_memory_space_constraint(states, pltpu.HBM)
    u, ev, od = pl.pallas_call(
        faces_kernel,
        in_specs=[inside(), anywhere()],
        out_shape=kept_in(pltpu.VMEM, FIELD, (NX, NZ), (NX, NZ)),
        scratch_shapes=[pltpu.VMEM(FIELD, f32), COPY],
        compiler_params=params(FACES_MIB),
        name="faces",
    )(tissue, states)
    area = swap("area", 0, ev), swap("area", 1, od)
    coefs = pl.pallas_call(
        coefs_kernel,
        out_shape=jax.ShapeDtypeStruct((7, 64, NZ), f32),
        compiler_params=params(4),
        name="coefficients",
    )(tissue, fiber)
    states, u, shown, bases, depth, _ = half_step(False, states, u, coefs, area)
    states, u, images, ev, od = ends(False, bases, coefs, depth, shown, (states, u))
    area = swap("area", 0, ev), swap("area", 1, od)
    states, _, shown, bases, depth, final = half_step(True, states, u, coefs, area)
    _, states, strips = ends(True, bases, coefs, depth, shown, (images, states, final[0]))
    strips = lax.all_to_all(strips, "depth", split_axis=0, concat_axis=0, tiled=True)
    images = pl.pallas_call(
        composite_kernel,
        out_shape=jax.ShapeDtypeStruct((2, 2, 4, NY, STRIP), f32),
        compiler_params=params(4),
        name="composite",
    )(strips)
    return states, images


def solution(mesh):
    return jax.shard_map(
        per_device,
        mesh=mesh,
        in_specs=(
            P(None, "depth", "area", None),
            P("depth", "area", None),
            P("depth", "area", None),
        ),
        out_specs=(P(None, "depth", "area", None), P(None, None, None, "area", "depth")),
        check_vma=False,
    )
```

```python
import math

import jax
import jax.numpy as jnp
from jax import lax
from jax.experimental import pallas as pl
from jax.experimental.pallas import tpu as pltpu
from jax.sharding import PartitionSpec as P

BLK = 4
CLASSES = 8
NX = 16
NY = 16
NZ = 768
STRIP = 48
HALF = STRIP // 2
CHUNK = 128
MID = 8
GATES = 6
RECORD = GATES * NX + 2 * (NX // BLK)

TIME_STEP = 0.15
SIGMA_LONG = 1.0
SIGMA_CROSS = 0.3
SLOPES = (8.0, -8.0, 6.0, 5.0, -5.0, -3.0)
MIDDLES = (0.2, 0.4, 0.3, 0.5, 0.6, 0.5)
RATES = (3.0, 0.5, 1.0, 0.8, 0.3, 0.1)
OPACITY = (0.012, 0.01)

f32 = jnp.float32


def params(mib):
    return pltpu.CompilerParams(vmem_limit_bytes=mib * 2**20)


def is_even(axis):
    return lax.rem(lax.axis_index(axis), 2) == 0


def lane_spread(count):
    row = lax.broadcasted_iota(jnp.int32, (count, count * BLK), 0)
    column = lax.broadcasted_iota(jnp.int32, (count, count * BLK), 1)
    return row == lax.shift_right_logical(column, 2)


def flat(ref):
    return jnp.concatenate([ref[k] for k in range(NX // BLK)], axis=0)


def spread_y(wide, start):
    row = lax.broadcasted_iota(jnp.int32, (NY, 1), 0)
    out = jnp.broadcast_to(wide[start:start + 1], (NY, wide.shape[1]))
    for k in range(1, NY // BLK):
        out = jnp.where(row >= BLK * k, wide[start + k:start + k + 1], out)
    return out


def choose(first, a, b):
    return jnp.where(first, a, b)


def neighbours(axis, ev, od):
    even = is_even(axis)
    place = lax.axis_index(axis)
    below = jnp.where(place == 0, 0.0, choose(even, od, ev))
    above = jnp.where(place == lax.axis_size(axis) - 1, 0.0, choose(even, ev, od))
    return below, above


def faces_kernel(tissue_ref, states_ref, u_ref, ev_ref, od_ref, own_ref, tissue_s, v_s, sem):
    loads = [pltpu.make_async_copy(tissue_ref, tissue_s, sem.at[0]),
             pltpu.make_async_copy(states_ref.at[0], v_s, sem.at[1])]
    for load in loads:
        load.start()
    onehot = lane_spread(NZ // BLK).astype(jnp.bfloat16)
    loads[0].wait()
    wide = jnp.dot(flat(tissue_s).astype(f32).astype(jnp.bfloat16), onehot, preferred_element_type=f32)
    masks = [spread_y(wide, BLK * block) for block in range(NX // BLK)]
    even = is_even("area")
    loads[1].wait()
    for x in range(NX):
        u = v_s[x] * masks[x // BLK]
        u_ref[x] = u
        own_ref[0, x:x + 1] = u[0:1]
        own_ref[1, x:x + 1] = u[NY - 1:NY]
        ev_ref[NX + x:NX + x + 1] = choose(even, u[NY - 2:NY - 1], u[1:2])
        od_ref[NX + x:NX + x + 1] = choose(even, u[1:2], u[NY - 2:NY - 1])
    ev_ref[0:NX] = choose(even, own_ref[1], own_ref[0])
    od_ref[0:NX] = choose(even, own_ref[0], own_ref[1])


def class_tables():
    spread = SIGMA_LONG - SIGMA_CROSS
    tables = [[] for _ in range(6)]
    for kind in range(CLASSES):
        polar = math.pi * (kind + 0.5) / CLASSES
        azimuth = 2.3 * kind
        f = (math.cos(polar), math.sin(polar) * math.cos(azimuth), math.sin(polar) * math.sin(azimuth))
        for k in range(3):
            tables[k].append(TIME_STEP * (SIGMA_CROSS + spread * f[k] * f[k]))
        for k, (a, b) in enumerate(((0, 1), (0, 2), (1, 2))):
            tables[3 + k].append(0.5 * TIME_STEP * spread * f[a] * f[b])
    return tables


def load_kernel(tissue_ref, fiber_ref, states_ref, _after, s_ref, coefs_ref, ev_ref, od_ref, sem):
    load = pltpu.make_async_copy(states_ref, s_ref, sem)
    load.start()
    kind = flat(fiber_ref)
    parts = [flat(tissue_ref).astype(f32)]
    for table in class_tables():
        part = jnp.full(kind.shape, table[0], f32)
        for c in range(1, CLASSES):
            part = jnp.where(kind == c, table[c], part)
        parts.append(part)
    parts.append(kind.astype(f32))
    rest = jnp.concatenate(parts, axis=0)
    onehot = lane_spread(NZ // BLK).astype(jnp.bfloat16)
    wide = None
    for _ in range(3):
        piece = rest.astype(jnp.bfloat16)
        rest = rest - piece.astype(f32)
        product = jnp.dot(piece, onehot, preferred_element_type=f32)
        wide = product if wide is None else wide + product
    for k in range(7):
        for block in range(4):
            coefs_ref[k, NY * block:NY * (block + 1)] = spread_y(wide, 16 * k + 4 * block)
    even = is_even("area")
    for place, part in ((GATES * NX, 0), (GATES * NX + 4, 7)):
        for block in range(4):
            low = wide[16 * part + 4 * block:16 * part + 4 * block + 1]
            high = wide[16 * part + 4 * block + 3:16 * part + 4 * block + 4]
            ev_ref[place + block:place + block + 1] = choose(even, high, low)
            od_ref[place + block:place + block + 1] = choose(even, low, high)
    load.wait()
    for k in range(GATES):
        for x in range(NX):
            place = NX * k + x
            low = s_ref[k + 1, x, 0:1]
            high = s_ref[k + 1, x, NY - 1:NY]
            ev_ref[place:place + 1] = choose(even, high, low)
            od_ref[place:place + 1] = choose(even, low, high)


def message_kernel(area_ev_ref, area_od_ref, u_ref, _e, _o, ev_ref, od_ref, rows_ref, _gates_ev, _gates_od):
    even = is_even("depth")
    below, above = neighbours("area", area_ev_ref[...], area_od_ref[...])
    rows_ref[0], rows_ref[2] = below[0:NX], below[NX:2 * NX]
    rows_ref[1], rows_ref[3] = above[0:NX], above[NX:2 * NX]
    depth_messages(even, u_ref, rows_ref, ev_ref, od_ref)


def depth_messages(even, u_ref, rows_ref, ev_ref, od_ref):
    low, high = u_ref[0], u_ref[NX - 1]
    ev_ref[0:NY] = choose(even, high, low)
    od_ref[0:NY] = choose(even, low, high)
    for k in range(rows_ref.shape[0]):
        place = NY + k
        low, high = rows_ref[k, 0:1], rows_ref[k, NX - 1:NX]
        ev_ref[place:place + 1] = choose(even, high, low)
        od_ref[place:place + 1] = choose(even, low, high)


def z_sides(u):
    lane = lax.broadcasted_iota(jnp.int32, (1, NZ), 1)
    after = jnp.where(lane == NZ - 1, 0.0, pltpu.roll(u, NZ - 1, axis=1))
    before = jnp.where(lane == 0, 0.0, pltpu.roll(u, 1, axis=1))
    return after, before


def y_sides(u, row_lo, row_hi):
    row = lax.broadcasted_iota(jnp.int32, (NY, 1), 0)
    after = jnp.where(row == NY - 1, row_hi, pltpu.roll(u, NY - 1, axis=0))
    before = jnp.where(row == 0, row_lo, pltpu.roll(u, 1, axis=0))
    return after, before


def z_slope(u):
    after, before = z_sides(u)
    return after - before


def y_slope(u, row_lo, row_hi):
    after, before = y_sides(u, row_lo, row_hi)
    return after - before


def derive(planes, u_ref, coefs_ref, rows_ref, uy_ref, uz_ref, w_ref):
    row_lo = rows_ref[0]
    row_hi = rows_ref[1]
    rowz_lo = z_slope(row_lo)
    rowz_hi = z_slope(row_hi)
    for x in planes:
        rows = slice(x // BLK * NY, x // BLK * NY + NY)
        row = slice(x, x + 1)
        u = u_ref[x]
        after, before = z_sides(u)
        uz = after - before
        uz_ref[x] = uz
        w = 0.52 * u + coefs_ref[3, rows] * (after + before)
        after, before = y_sides(u, row_lo[row], row_hi[row])
        uy_ref[x] = after - before
        w = w + coefs_ref[2, rows] * (after + before)
        after, before = y_sides(uz, rowz_lo[row], rowz_hi[row])
        w_ref[x] = w + coefs_ref[6, rows] * (after - before)


def ionic(w, gates, calcium):
    fresh = []
    for k in range(6):
        keep = math.exp(-TIME_STEP * RATES[k])
        half = 0.5 * (1.0 - keep)
        t = jnp.tanh((0.5 * SLOPES[k]) * w - (0.5 * SLOPES[k] * MIDDLES[k]))
        fresh.append(half * t + (keep * gates[k] + half))
    both = fresh[3] * fresh[4]
    cube = fresh[0] * fresh[0] * fresh[0]
    loss = (
        (2.0 * TIME_STEP) * (cube * fresh[1]) * (w - 1.2)
        + TIME_STEP * (fresh[2] * fresh[2]) * (w + 0.1)
        + (0.6 * TIME_STEP) * both * (w - 0.9)
        + (0.2 * TIME_STEP) * (1.0 + fresh[5]) * (w - 0.05)
    )
    gain = (1.5 * TIME_STEP) * both
    calc_next = (1.0 - 0.8 * TIME_STEP) * calcium + gain * (1.0 - calcium)
    return w - loss, fresh, calc_next


def march(q, opaque, state):
    passed, red, green = state
    alpha = opaque * jnp.tanh(3.0 * q - 1.2) + opaque
    weight = passed * alpha
    off = q - 0.5
    red = red + weight * jnp.tanh(2.5 * off)
    green = green + weight * jnp.exp(-6.0 * (off * off))
    return passed - weight, red, green


def advance(w, old, inside):
    volt, fresh, calc = ionic(w, old[1:7], old[7])
    return [jnp.where(inside, a, b) for a, b in zip([volt] + fresh + [calc], old)]


def show(new, m, marches):
    return [march(q, (0.5 * OPACITY[f]) * m, marches[f]) for f, q in enumerate((new[0], new[7]))]


def interior_planes(planes, marches_of, s_ref, u_ref, next_ref, coefs_ref, uy_ref, uz_ref, w_ref, shown_ref):
    def chunk(j, carry):
        cols = pl.ds(pl.multiple_of(j * CHUNK, CHUNK), CHUNK)
        marches = marches_of(cols)
        for x in planes:
            rows = slice(x // BLK * NY, x // BLK * NY + NY)
            m = coefs_ref[0, rows, cols]
            w = (
                w_ref[x, :, cols]
                + coefs_ref[1, rows, cols] * (u_ref[x + 1, :, cols] + u_ref[x - 1, :, cols])
                + coefs_ref[4, rows, cols] * (uy_ref[x + 1, :, cols] - uy_ref[x - 1, :, cols])
                + coefs_ref[5, rows, cols] * (uz_ref[x + 1, :, cols] - uz_ref[x - 1, :, cols])
            )
            new = advance(w, [s_ref[k, x, :, cols] for k in range(8)], m > 0.5)
            for k in range(8):
                s_ref[k, x, :, cols] = new[k]
            next_ref[x, :, cols] = m * new[0]
            marches = show(new, m, marches)
        for f in range(2):
            for k in range(3):
                shown_ref[3 * f + k, :, cols] = marches[f][k]
        return carry

    lax.fori_loop(0, NZ // CHUNK, chunk, 0)


def base_of(x, beside, sign, u_ref, coefs_ref, uy_ref, uz_ref, w_ref):
    rows = slice(x // BLK * NY, x // BLK * NY + NY)
    return (
        w_ref[x]
        + coefs_ref[1, rows] * u_ref[beside]
        + sign * (coefs_ref[4, rows] * uy_ref[beside] + coefs_ref[5, rows] * uz_ref[beside])
    )


def front_kernel(_s, u_ref, coefs_ref, rows_ref, _p,
                 s_ref, next_ref, uy_ref, uz_ref, w_ref, shown_ref, base_ref, _passing):
    derive(range(MID + 1), u_ref, coefs_ref, rows_ref, uy_ref, uz_ref, w_ref)
    base_ref[...] = base_of(0, 1, 1.0, u_ref, coefs_ref, uy_ref, uz_ref, w_ref)
    one = jnp.ones((NY, CHUNK), f32)
    zero = jnp.zeros((NY, CHUNK), f32)
    interior_planes(range(1, MID), lambda cols: [(one, zero, zero)] * 2,
                    s_ref, u_ref, next_ref, coefs_ref, uy_ref, uz_ref, w_ref, shown_ref)


def back_kernel(u_ref, coefs_ref, rows_ref, _s, _n, _y, _z, _w, _a,
                s_ref, next_ref, uy_ref, uz_ref, w_ref, shown_ref, base_ref, *storing):
    if storing:
        final_ref, sem = storing
        done = pl.ds(1, MID - 1)
        store = pltpu.make_async_copy(s_ref.at[:, done], final_ref.at[:, done], sem)
        store.start()
    derive(range(MID + 1, NX), u_ref, coefs_ref, rows_ref, uy_ref, uz_ref, w_ref)
    base_ref[...] = base_of(NX - 1, NX - 2, -1.0, u_ref, coefs_ref, uy_ref, uz_ref, w_ref)
    interior_planes(range(MID, NX - 1),
                    lambda cols: [tuple(shown_ref[3 * f + k, :, cols] for k in range(3)) for f in range(2)],
                    s_ref, u_ref, next_ref, coefs_ref, uy_ref, uz_ref, w_ref, shown_ref)
    if storing:
        store.wait()


def outer_row(side, halos, rows_ref, own_ref, record):
    near, far, own = rows_ref[side], rows_ref[2 + side], own_ref[side]
    turn = 1.0 if side else -1.0
    near_place, far_place = NY + side, NY + 2 + side
    own_place = NY - 1 if side else 0

    def across(halo, place):
        return halo[place:place + 1]

    slope = turn * (far - own)
    slopes = [turn * (across(h, far_place) - across(h, own_place)) for h in halos]
    zs = [across(z_slope(h), near_place) for h in halos]
    mask = spread_y(record[GATES * NX:GATES * NX + 4], 0)
    kind = spread_y(record[GATES * NX + 4:GATES * NX + 8], 0)
    coefs = []
    for table in class_tables():
        coef = jnp.full(kind.shape, table[0], f32)
        for c in range(1, CLASSES):
            coef = jnp.where(kind == float(c), table[c], coef)
        coefs.append(coef)
    x_after, x_before = y_sides(near, across(halos[0], near_place), across(halos[1], near_place))
    z_after, z_before = z_sides(near)
    w = (
        0.52 * near
        + coefs[0] * (x_after + x_before)
        + coefs[1] * (own + far)
        + coefs[2] * (z_after + z_before)
        + coefs[3] * y_slope(slope, *slopes)
        + coefs[4] * y_slope(z_after - z_before, *zs)
        + coefs[5] * z_slope(slope)
    )
    gates = [record[NX * k:NX * (k + 1)] for k in range(GATES)]
    return mask * ionic(w, gates, jnp.zeros_like(w))[0]


def ends_body(last, refs):
    base_lo_ref, base_hi_ref, coefs_ref, depth_ev_ref, depth_od_ref, shown_ref = refs[:6]
    if last:
        earlier_ref, _, _, s_ref, final_ref, strips_ref, acc_s, uy_s, uz_s, sem = refs[6:]
        done = pl.ds(MID, NX - 1 - MID)
        stores = [pltpu.make_async_copy(s_ref.at[:, done], final_ref.at[:, done], sem.at[2])]
        stores[0].start()
    else:
        (gates_ev_ref, gates_od_ref, rows_ref, own_ref, _, _,
         s_ref, next_ref, acc_s, ahead_ref, ev_ref, od_ref, uy_s, uz_s) = refs[6:]
    even = is_even("depth")
    halos = neighbours("depth", depth_ev_ref[...], depth_od_ref[...])
    if not last:
        records = neighbours("area", gates_ev_ref[...], gates_od_ref[...])
        for side in range(2):
            ahead_ref[side] = outer_row(side, halos, rows_ref, own_ref, records[side])
    for end, x, base_ref, sign in ((0, 0, base_lo_ref, -1.0), (1, NX - 1, base_hi_ref, 1.0)):
        rows = slice(x // BLK * NY, x // BLK * NY + NY)
        halo = halos[end]
        u = halo[0:NY]
        uz_s[...] = sign * z_slope(u)
        uy_s[...] = sign * y_slope(u, halo[NY:NY + 1], halo[NY + 1:NY + 2])
        for j in range(NZ // CHUNK):
            cols = slice(j * CHUNK, (j + 1) * CHUNK)
            m = coefs_ref[0, rows, cols]
            w = (
                base_ref[:, cols]
                + coefs_ref[1, rows, cols] * u[:, cols]
                + coefs_ref[4, rows, cols] * uy_s[:, cols]
                + coefs_ref[5, rows, cols] * uz_s[:, cols]
            )
            new = advance(w, [s_ref[k, x, :, cols] for k in range(8)], m > 0.5)
            for k in range(8):
                s_ref[k, x, :, cols] = new[k]
            if not last:
                next_ref[x, :, cols] = m * new[0]
            if end == 0:
                one = jnp.ones((NY, CHUNK), f32)
                zero = jnp.zeros((NY, CHUNK), f32)
                marches = show(new, m, [(one, zero, zero)] * 2)
            else:
                marches = [tuple(acc_s[3 * f + k, :, cols] for k in range(3)) for f in range(2)]
                marches = show(new, m, marches)
            for f in range(2):
                passed, red, green = marches[f]
                if end == 0:
                    red = red + passed * shown_ref[3 * f + 1, :, cols]
                    green = green + passed * shown_ref[3 * f + 2, :, cols]
                    passed = passed * shown_ref[3 * f, :, cols]
                for k, item in enumerate((passed, red, green)):
                    acc_s[3 * f + k, :, cols] = item
        if last:
            stores.append(pltpu.make_async_copy(s_ref.at[:, x], final_ref.at[:, x], sem.at[end]))
            stores[-1].start()
    if not last:
        depth_messages(even, next_ref, ahead_ref, ev_ref, od_ref)
    else:
        for k in range(3):
            stack = jnp.concatenate(
                [earlier_ref[k], earlier_ref[3 + k], acc_s[k], acc_s[3 + k]], axis=0)
            stack = jnp.concatenate([stack, pltpu.roll(stack, NZ - HALF, axis=1)], axis=0)
            turned = stack.T
            for d in range(NZ // STRIP):
                strips_ref[d, HALF * k:HALF * (k + 1)] = turned[STRIP * d:STRIP * d + HALF]
        for store in stores:
            store.wait()


def composite_kernel(strips_ref, out_ref):
    count = strips_ref.shape[0]
    passed = jnp.ones((HALF, 128), f32)
    red = jnp.zeros((HALF, 128), f32)
    green = jnp.zeros((HALF, 128), f32)
    for s in range(count):
        red = red + passed * strips_ref[s, HALF:2 * HALF]
        green = green + passed * strips_ref[s, 2 * HALF:3 * HALF]
        passed = passed * strips_ref[s, 0:HALF]
    solid = 1.0 - passed
    red = 0.5 * (solid + red)
    whole = jnp.concatenate([red, green, solid - red, solid, jnp.zeros((32, 128), f32)], axis=0)
    turned = whole.T
    first, second = turned[0:64], turned[64:128]
    lane = lax.broadcasted_iota(jnp.int32, (1, 128), 1)
    for c in range(4):
        a = pltpu.roll(first, (128 - HALF * c) % 128, axis=1) if c else first
        b = pltpu.roll(second, (128 + HALF - HALF * c) % 128, axis=1) if c != 1 else second
        o = jnp.where(lane < HALF, a, b)
        for k in range(4):
            out_ref[k // 2, k % 2, c] = o[NY * k:NY * (k + 1), 0:STRIP]


VOLUME = (8, NX, NY, NZ)
FIELD = (NX, NY, NZ)
PLANE = (NY, NZ)
SHOWN = (6, NY, NZ)
COPY = pltpu.SemaphoreType.DMA


def shapes_of(*shapes):
    return [jax.ShapeDtypeStruct(s, f32) for s in shapes]


def kept_in(space, *shapes):
    return [space(s, f32) for s in shapes]


def anywhere():
    return pl.BlockSpec(memory_space=pl.ANY)


def inside():
    return pl.BlockSpec(memory_space=pltpu.VMEM)


def cost():
    voxels = NX * NY * NZ // 2
    return pl.CostEstimate(flops=400 * voxels, bytes_accessed=32 * voxels, transcendentals=12 * voxels)


def interior_front(states, u, coefs, rows, passing):
    return pl.pallas_call(
        front_kernel,
        in_specs=[inside()] * 4 + [anywhere()],
        out_specs=[inside()] * 7 + [anywhere()],
        out_shape=kept_in(pltpu.VMEM, VOLUME, FIELD, FIELD, FIELD, FIELD, SHOWN, PLANE) + shapes_of(passing.shape),
        input_output_aliases={0: 0, 4: 7},
        compiler_params=params(4),
        cost_estimate=cost(),
        name="front",
    )(states, u, coefs, rows, passing)


def interior_back(last, u, coefs, rows, kept):
    out_specs = [inside()] * 7
    out_shape = kept_in(pltpu.VMEM, VOLUME, FIELD, FIELD, FIELD, FIELD, SHOWN, PLANE)
    if last:
        out_specs += [anywhere()]
        out_shape += kept_in(pltpu.HBM, VOLUME)
    return pl.pallas_call(
        back_kernel,
        in_specs=[inside()] * 9,
        out_specs=out_specs,
        out_shape=out_shape,
        scratch_shapes=[COPY] if last else [],
        input_output_aliases={3 + k: k for k in range(6)},
        compiler_params=params(4),
        cost_estimate=cost(),
        name="back",
    )(u, coefs, rows, *kept)


def ends(last, bases, coefs, depth, shown, rest):
    args = [*bases, coefs, *depth, shown, *rest]
    in_specs = [inside()] * len(args)
    aliases = {len(args) - 2: 0, len(args) - 1: 1}
    scratch = [pltpu.VMEM(PLANE, f32)] * 2
    if last:
        out_shape = kept_in(pltpu.VMEM, VOLUME) + kept_in(pltpu.HBM, VOLUME)
        out_shape += kept_in(pltpu.VMEM, (NZ // STRIP, 3 * HALF, 128))
        scratch = [pltpu.VMEM(SHOWN, f32), *scratch, COPY((3,))]
        in_specs[-1] = anywhere()
        out_specs = [inside(), anywhere(), inside()]
    else:
        out_shape = kept_in(pltpu.VMEM, VOLUME, FIELD, SHOWN, (2, NX, NZ), (NY + 2, NZ), (NY + 2, NZ))
        out_specs = [inside()] * 6
    return pl.pallas_call(
        lambda *refs: ends_body(last, refs),
        in_specs=in_specs,
        out_specs=out_specs,
        out_shape=out_shape,
        scratch_shapes=scratch,
        input_output_aliases=aliases,
        compiler_params=params(4),
        name="ends_last" if last else "ends_first",
    )(*args)


def swaps(axis):
    count = lax.axis_size(axis)
    return [(i, i ^ 1) for i in range(count)], [(i, (((i - 1) ^ 1) + 1) % count) for i in range(count)]


def swap(axis, which, message):
    return lax.ppermute(message, axis, swaps(axis)[which])


def half_step(last, states, u, coefs, rows, messages):
    even = swap("depth", 0, messages[0])
    *kept, low, passing = interior_front(states, u, coefs, rows, messages[1])
    odd = swap("depth", 1, passing)
    states, after, _, _, _, shown, high, *final = interior_back(last, u, coefs, rows, kept)
    return states, after, shown, (low, high), (even, odd), final


def per_device(states, tissue, fiber):
    blocks = (NX // BLK, NY // BLK, NZ // BLK)
    states = pltpu.with_memory_space_constraint(states, pltpu.HBM)
    tissue = pltpu.with_memory_space_constraint(tissue, pltpu.HBM)
    u, ev, od, own = pl.pallas_call(
        faces_kernel,
        in_specs=[anywhere(), anywhere()],
        out_shape=kept_in(pltpu.VMEM, FIELD, (2 * NX, NZ), (2 * NX, NZ), (2, NX, NZ)),
        scratch_shapes=[pltpu.VMEM(blocks, jnp.int32), pltpu.VMEM(FIELD, f32), COPY((2,))],
        compiler_params=params(4),
        name="faces",
    )(tissue, states)
    area = swap("area", 0, ev), swap("area", 1, od)
    states, coefs, ev, od = pl.pallas_call(
        load_kernel,
        in_specs=[inside(), inside(), anywhere(), anywhere()],
        out_shape=kept_in(pltpu.VMEM, VOLUME, (7, 64, NZ), (RECORD, NZ), (RECORD, NZ)),
        scratch_shapes=[COPY],
        compiler_params=params(4),
        cost_estimate=pl.CostEstimate(flops=10**7, bytes_accessed=8 * 10**6, transcendentals=0),
        name="load",
    )(tissue, fiber, states, own)
    ev, od, rows, gates_ev, gates_od = pl.pallas_call(
        message_kernel,
        in_specs=[inside()] * 3 + [anywhere()] * 2,
        out_specs=[inside()] * 3 + [anywhere()] * 2,
        out_shape=kept_in(pltpu.VMEM, (NY + 4, NZ), (NY + 4, NZ), (4, NX, NZ), (RECORD, NZ), (RECORD, NZ)),
        input_output_aliases={3: 3, 4: 4},
        compiler_params=params(1),
        name="depth_message",
    )(*area, u, ev, od)
    gates = swap("area", 0, gates_ev), swap("area", 1, gates_od)
    states, after, shown, bases, depth, _ = half_step(False, states, u, coefs, rows, (ev, od))
    states, u, images, rows, ev, od = ends(
        False, bases, coefs, depth, shown, (*gates, rows, own, states, after))
    states, _, shown, bases, depth, final = half_step(True, states, u, coefs, rows, (ev, od))
    _, states, strips = ends(True, bases, coefs, depth, shown, (images, states, *final))
    strips = lax.all_to_all(strips, "depth", split_axis=0, concat_axis=0, tiled=True)
    images = pl.pallas_call(
        composite_kernel,
        out_shape=jax.ShapeDtypeStruct((2, 2, 4, NY, STRIP), f32),
        compiler_params=params(4),
        name="composite",
    )(strips)
    return states, images


def solution(mesh):
    return jax.shard_map(
        per_device,
        mesh=mesh,
        in_specs=(
            P(None, "depth", "area", None),
            P("depth", "area", None),
            P("depth", "area", None),
        ),
        out_specs=(P(None, "depth", "area", None), P(None, None, None, "area", "depth")),
        check_vma=False,
    )
```

```python
import math

import jax
import jax.numpy as jnp
from jax import lax
from jax.experimental import pallas as pl
from jax.experimental.pallas import tpu as pltpu
from jax.sharding import PartitionSpec as P

BLK = 4
CLASSES = 8
NX = 16
NY = 16
NZ = 768
STRIP = 48
HALF = STRIP // 2
CHUNK = 128
MID = 8
GATES = 6
RECORD = GATES * NX + 2 * (NX // BLK)

TIME_STEP = 0.15
SIGMA_LONG = 1.0
SIGMA_CROSS = 0.3
SLOPES = (8.0, -8.0, 6.0, 5.0, -5.0, -3.0)
MIDDLES = (0.2, 0.4, 0.3, 0.5, 0.6, 0.5)
RATES = (3.0, 0.5, 1.0, 0.8, 0.3, 0.1)
OPACITY = (0.012, 0.01)

f32 = jnp.float32


def params(mib):
    return pltpu.CompilerParams(vmem_limit_bytes=mib * 2**20)


def is_even(axis):
    return lax.rem(lax.axis_index(axis), 2) == 0


def lane_spread(count):
    row = lax.broadcasted_iota(jnp.int32, (count, count * BLK), 0)
    column = lax.broadcasted_iota(jnp.int32, (count, count * BLK), 1)
    return row == lax.shift_right_logical(column, 2)


def flat(ref):
    return jnp.concatenate([ref[k] for k in range(NX // BLK)], axis=0)


def spread_y(wide, start):
    row = lax.broadcasted_iota(jnp.int32, (NY, 1), 0)
    out = jnp.broadcast_to(wide[start:start + 1], (NY, wide.shape[1]))
    for k in range(1, NY // BLK):
        out = jnp.where(row >= BLK * k, wide[start + k:start + k + 1], out)
    return out


def choose(first, a, b):
    return jnp.where(first, a, b)


def neighbours(axis, ev, od):
    even = is_even(axis)
    place = lax.axis_index(axis)
    below = jnp.where(place == 0, 0.0, choose(even, od, ev))
    above = jnp.where(place == lax.axis_size(axis) - 1, 0.0, choose(even, ev, od))
    return below, above


def faces_kernel(tissue_ref, states_ref, u_ref, ev_ref, od_ref, own_ref, tissue_s, v_s, sem):
    loads = [pltpu.make_async_copy(tissue_ref, tissue_s, sem.at[0]),
             pltpu.make_async_copy(states_ref.at[0], v_s, sem.at[1])]
    for load in loads:
        load.start()
    onehot = lane_spread(NZ // BLK).astype(jnp.bfloat16)
    loads[0].wait()
    wide = jnp.dot(flat(tissue_s).astype(f32).astype(jnp.bfloat16), onehot, preferred_element_type=f32)
    masks = [spread_y(wide, BLK * block) for block in range(NX // BLK)]
    even = is_even("area")
    loads[1].wait()
    for x in range(NX):
        u = v_s[x] * masks[x // BLK]
        u_ref[x] = u
        own_ref[0, x:x + 1] = u[0:1]
        own_ref[1, x:x + 1] = u[NY - 1:NY]
        ev_ref[NX + x:NX + x + 1] = choose(even, u[NY - 2:NY - 1], u[1:2])
        od_ref[NX + x:NX + x + 1] = choose(even, u[1:2], u[NY - 2:NY - 1])
    ev_ref[0:NX] = choose(even, own_ref[1], own_ref[0])
    od_ref[0:NX] = choose(even, own_ref[0], own_ref[1])


def class_tables():
    spread = SIGMA_LONG - SIGMA_CROSS
    tables = [[] for _ in range(6)]
    for kind in range(CLASSES):
        polar = math.pi * (kind + 0.5) / CLASSES
        azimuth = 2.3 * kind
        f = (math.cos(polar), math.sin(polar) * math.cos(azimuth), math.sin(polar) * math.sin(azimuth))
        for k in range(3):
            tables[k].append(TIME_STEP * (SIGMA_CROSS + spread * f[k] * f[k]))
        for k, (a, b) in enumerate(((0, 1), (0, 2), (1, 2))):
            tables[3 + k].append(0.5 * TIME_STEP * spread * f[a] * f[b])
    return tables


def load_kernel(tissue_ref, fiber_ref, states_ref, _after, s_ref, coefs_ref, ev_ref, od_ref, sem):
    loads = [pltpu.make_async_copy(states_ref.at[k], s_ref.at[k], sem.at[k]) for k in range(8)]
    for k in (1, 2, 3, 4, 5, 6, 0, 7):
        loads[k].start()
    kind = flat(fiber_ref)
    parts = [flat(tissue_ref).astype(f32)]
    for table in class_tables():
        part = jnp.full(kind.shape, table[0], f32)
        for c in range(1, CLASSES):
            part = jnp.where(kind == c, table[c], part)
        parts.append(part)
    parts.append(kind.astype(f32))
    rest = jnp.concatenate(parts, axis=0)
    onehot = lane_spread(NZ // BLK).astype(jnp.bfloat16)
    wide = None
    for _ in range(3):
        piece = rest.astype(jnp.bfloat16)
        rest = rest - piece.astype(f32)
        product = jnp.dot(piece, onehot, preferred_element_type=f32)
        wide = product if wide is None else wide + product
    for k in range(7):
        for block in range(4):
            coefs_ref[k, NY * block:NY * (block + 1)] = spread_y(wide, 16 * k + 4 * block)
    even = is_even("area")
    for place, part in ((GATES * NX, 0), (GATES * NX + 4, 7)):
        for block in range(4):
            low = wide[16 * part + 4 * block:16 * part + 4 * block + 1]
            high = wide[16 * part + 4 * block + 3:16 * part + 4 * block + 4]
            ev_ref[place + block:place + block + 1] = choose(even, high, low)
            od_ref[place + block:place + block + 1] = choose(even, low, high)
    for k in range(GATES):
        loads[k + 1].wait()
        for x in range(NX):
            place = NX * k + x
            low = s_ref[k + 1, x, 0:1]
            high = s_ref[k + 1, x, NY - 1:NY]
            ev_ref[place:place + 1] = choose(even, high, low)
            od_ref[place:place + 1] = choose(even, low, high)
    loads[0].wait()
    loads[7].wait()


def message_kernel(area_ev_ref, area_od_ref, u_ref, _e, _o, ev_ref, od_ref, rows_ref, _gates_ev, _gates_od):
    even = is_even("depth")
    below, above = neighbours("area", area_ev_ref[...], area_od_ref[...])
    rows_ref[0], rows_ref[2] = below[0:NX], below[NX:2 * NX]
    rows_ref[1], rows_ref[3] = above[0:NX], above[NX:2 * NX]
    depth_messages(even, u_ref, rows_ref, ev_ref, od_ref)


def depth_messages(even, u_ref, rows_ref, ev_ref, od_ref):
    low, high = u_ref[0], u_ref[NX - 1]
    ev_ref[0:NY] = choose(even, high, low)
    od_ref[0:NY] = choose(even, low, high)
    for k in range(rows_ref.shape[0]):
        place = NY + k
        low, high = rows_ref[k, 0:1], rows_ref[k, NX - 1:NX]
        ev_ref[place:place + 1] = choose(even, high, low)
        od_ref[place:place + 1] = choose(even, low, high)


def z_sides(u):
    lane = lax.broadcasted_iota(jnp.int32, (1, NZ), 1)
    after = jnp.where(lane == NZ - 1, 0.0, pltpu.roll(u, NZ - 1, axis=1))
    before = jnp.where(lane == 0, 0.0, pltpu.roll(u, 1, axis=1))
    return after, before


def y_sides(u, row_lo, row_hi):
    row = lax.broadcasted_iota(jnp.int32, (NY, 1), 0)
    after = jnp.where(row == NY - 1, row_hi, pltpu.roll(u, NY - 1, axis=0))
    before = jnp.where(row == 0, row_lo, pltpu.roll(u, 1, axis=0))
    return after, before


def z_slope(u):
    after, before = z_sides(u)
    return after - before


def y_slope(u, row_lo, row_hi):
    after, before = y_sides(u, row_lo, row_hi)
    return after - before


def derive(planes, u_ref, coefs_ref, rows_ref, uy_ref, uz_ref, w_ref):
    row_lo = rows_ref[0]
    row_hi = rows_ref[1]
    rowz_lo = z_slope(row_lo)
    rowz_hi = z_slope(row_hi)
    for x in planes:
        rows = slice(x // BLK * NY, x // BLK * NY + NY)
        row = slice(x, x + 1)
        u = u_ref[x]
        after, before = z_sides(u)
        uz = after - before
        uz_ref[x] = uz
        w = 0.52 * u + coefs_ref[3, rows] * (after + before)
        after, before = y_sides(u, row_lo[row], row_hi[row])
        uy_ref[x] = after - before
        w = w + coefs_ref[2, rows] * (after + before)
        after, before = y_sides(uz, rowz_lo[row], rowz_hi[row])
        w_ref[x] = w + coefs_ref[6, rows] * (after - before)


def ionic(w, gates, calcium):
    fresh = []
    for k in range(6):
        keep = math.exp(-TIME_STEP * RATES[k])
        half = 0.5 * (1.0 - keep)
        t = jnp.tanh((0.5 * SLOPES[k]) * w - (0.5 * SLOPES[k] * MIDDLES[k]))
        fresh.append(half * t + (keep * gates[k] + half))
    both = fresh[3] * fresh[4]
    cube = fresh[0] * fresh[0] * fresh[0]
    loss = (
        (2.0 * TIME_STEP) * (cube * fresh[1]) * (w - 1.2)
        + TIME_STEP * (fresh[2] * fresh[2]) * (w + 0.1)
        + (0.6 * TIME_STEP) * both * (w - 0.9)
        + (0.2 * TIME_STEP) * (1.0 + fresh[5]) * (w - 0.05)
    )
    gain = (1.5 * TIME_STEP) * both
    calc_next = (1.0 - 0.8 * TIME_STEP) * calcium + gain * (1.0 - calcium)
    return w - loss, fresh, calc_next


def march(q, opaque, state):
    passed, red, green = state
    alpha = opaque * jnp.tanh(3.0 * q - 1.2) + opaque
    weight = passed * alpha
    off = q - 0.5
    red = red + weight * jnp.tanh(2.5 * off)
    green = green + weight * jnp.exp(-6.0 * (off * off))
    return passed - weight, red, green


def advance(w, old, inside):
    volt, fresh, calc = ionic(w, old[1:7], old[7])
    return [jnp.where(inside, a, b) for a, b in zip([volt] + fresh + [calc], old)]


def show(new, m, marches):
    return [march(q, (0.5 * OPACITY[f]) * m, marches[f]) for f, q in enumerate((new[0], new[7]))]


def interior_planes(planes, marches_of, s_ref, u_ref, next_ref, coefs_ref, uy_ref, uz_ref, w_ref, shown_ref):
    def chunk(j, carry):
        cols = pl.ds(pl.multiple_of(j * CHUNK, CHUNK), CHUNK)
        marches = marches_of(cols)
        for x in planes:
            rows = slice(x // BLK * NY, x // BLK * NY + NY)
            m = coefs_ref[0, rows, cols]
            w = (
                w_ref[x, :, cols]
                + coefs_ref[1, rows, cols] * (u_ref[x + 1, :, cols] + u_ref[x - 1, :, cols])
                + coefs_ref[4, rows, cols] * (uy_ref[x + 1, :, cols] - uy_ref[x - 1, :, cols])
                + coefs_ref[5, rows, cols] * (uz_ref[x + 1, :, cols] - uz_ref[x - 1, :, cols])
            )
            new = advance(w, [s_ref[k, x, :, cols] for k in range(8)], m > 0.5)
            for k in range(8):
                s_ref[k, x, :, cols] = new[k]
            if next_ref is not None:
                next_ref[x, :, cols] = m * new[0]
            marches = show(new, m, marches)
        for f in range(2):
            for k in range(3):
                shown_ref[3 * f + k, :, cols] = marches[f][k]
        return carry

    lax.fori_loop(0, NZ // CHUNK, chunk, 0)


def base_of(x, beside, sign, u_ref, coefs_ref, uy_ref, uz_ref, w_ref):
    rows = slice(x // BLK * NY, x // BLK * NY + NY)
    return (
        w_ref[x]
        + coefs_ref[1, rows] * u_ref[beside]
        + sign * (coefs_ref[4, rows] * uy_ref[beside] + coefs_ref[5, rows] * uz_ref[beside])
    )


def interior_kernel(last, refs):
    u_ref, coefs_ref, rows_ref = refs[1:4]
    s_ref, shown_ref, base_ref = refs[4:7]
    if last:
        next_ref = None
        final_ref, uy_s, uz_s, w_s, sem = refs[7:]
    else:
        next_ref, uy_s, uz_s, w_s = refs[7:]
    derive(range(NX), u_ref, coefs_ref, rows_ref, uy_s, uz_s, w_s)
    base_ref[0] = base_of(0, 1, 1.0, u_ref, coefs_ref, uy_s, uz_s, w_s)
    base_ref[1] = base_of(NX - 1, NX - 2, -1.0, u_ref, coefs_ref, uy_s, uz_s, w_s)
    one = jnp.ones((NY, CHUNK), f32)
    zero = jnp.zeros((NY, CHUNK), f32)
    interior_planes(range(1, MID), lambda cols: [(one, zero, zero)] * 2,
                    s_ref, u_ref, next_ref, coefs_ref, uy_s, uz_s, w_s, shown_ref)
    if last:
        done = pl.ds(1, MID - 1)
        store = pltpu.make_async_copy(s_ref.at[:, done], final_ref.at[:, done], sem)
        store.start()
    interior_planes(range(MID, NX - 1),
                    lambda cols: [tuple(shown_ref[3 * f + k, :, cols] for k in range(3)) for f in range(2)],
                    s_ref, u_ref, next_ref, coefs_ref, uy_s, uz_s, w_s, shown_ref)
    if last:
        store.wait()


def outer_row(side, halos, rows_ref, own_ref, record):
    near, far, own = rows_ref[side], rows_ref[2 + side], own_ref[side]
    turn = 1.0 if side else -1.0
    near_place, far_place = NY + side, NY + 2 + side
    own_place = NY - 1 if side else 0

    def across(halo, place):
        return halo[place:place + 1]

    slope = turn * (far - own)
    slopes = [turn * (across(h, far_place) - across(h, own_place)) for h in halos]
    zs = [across(z_slope(h), near_place) for h in halos]
    mask = spread_y(record[GATES * NX:GATES * NX + 4], 0)
    kind = spread_y(record[GATES * NX + 4:GATES * NX + 8], 0)
    coefs = []
    for table in class_tables():
        coef = jnp.full(kind.shape, table[0], f32)
        for c in range(1, CLASSES):
            coef = jnp.where(kind == float(c), table[c], coef)
        coefs.append(coef)
    x_after, x_before = y_sides(near, across(halos[0], near_place), across(halos[1], near_place))
    z_after, z_before = z_sides(near)
    w = (
        0.52 * near
        + coefs[0] * (x_after + x_before)
        + coefs[1] * (own + far)
        + coefs[2] * (z_after + z_before)
        + coefs[3] * y_slope(slope, *slopes)
        + coefs[4] * y_slope(z_after - z_before, *zs)
        + coefs[5] * z_slope(slope)
    )
    gates = [record[NX * k:NX * (k + 1)] for k in range(GATES)]
    return mask * ionic(w, gates, jnp.zeros_like(w))[0]


def ends_body(last, refs):
    bases_ref, coefs_ref, depth_ev_ref, depth_od_ref, shown_ref = refs[:5]
    if last:
        earlier_ref, _, _, s_ref, final_ref, strips_ref, acc_s, uy_s, uz_s, sem = refs[5:]
        done = pl.ds(MID, NX - 1 - MID)
        stores = [pltpu.make_async_copy(s_ref.at[:, done], final_ref.at[:, done], sem.at[2])]
        stores[0].start()
    else:
        (gates_ev_ref, gates_od_ref, rows_ref, own_ref, _, _,
         s_ref, next_ref, acc_s, ahead_ref, ev_ref, od_ref, uy_s, uz_s) = refs[5:]
    even = is_even("depth")
    halos = neighbours("depth", depth_ev_ref[...], depth_od_ref[...])
    if not last:
        records = neighbours("area", gates_ev_ref[...], gates_od_ref[...])
        for side in range(2):
            ahead_ref[side] = outer_row(side, halos, rows_ref, own_ref, records[side])
    for end, x, sign in ((0, 0, -1.0), (1, NX - 1, 1.0)):
        rows = slice(x // BLK * NY, x // BLK * NY + NY)
        halo = halos[end]
        u = halo[0:NY]
        uz_s[...] = sign * z_slope(u)
        uy_s[...] = sign * y_slope(u, halo[NY:NY + 1], halo[NY + 1:NY + 2])
        for j in range(NZ // CHUNK):
            cols = slice(j * CHUNK, (j + 1) * CHUNK)
            m = coefs_ref[0, rows, cols]
            w = (
                bases_ref[end, :, cols]
                + coefs_ref[1, rows, cols] * u[:, cols]
                + coefs_ref[4, rows, cols] * uy_s[:, cols]
                + coefs_ref[5, rows, cols] * uz_s[:, cols]
            )
            new = advance(w, [s_ref[k, x, :, cols] for k in range(8)], m > 0.5)
            for k in range(8):
                s_ref[k, x, :, cols] = new[k]
            if not last:
                next_ref[x, :, cols] = m * new[0]
            if end == 0:
                one = jnp.ones((NY, CHUNK), f32)
                zero = jnp.zeros((NY, CHUNK), f32)
                marches = show(new, m, [(one, zero, zero)] * 2)
            else:
                marches = [tuple(acc_s[3 * f + k, :, cols] for k in range(3)) for f in range(2)]
                marches = show(new, m, marches)
            for f in range(2):
                passed, red, green = marches[f]
                if end == 0:
                    red = red + passed * shown_ref[3 * f + 1, :, cols]
                    green = green + passed * shown_ref[3 * f + 2, :, cols]
                    passed = passed * shown_ref[3 * f, :, cols]
                for k, item in enumerate((passed, red, green)):
                    acc_s[3 * f + k, :, cols] = item
        if last:
            stores.append(pltpu.make_async_copy(s_ref.at[:, x], final_ref.at[:, x], sem.at[end]))
            stores[-1].start()
    if not last:
        depth_messages(even, next_ref, ahead_ref, ev_ref, od_ref)
    else:
        for k in range(3):
            stack = jnp.concatenate(
                [earlier_ref[k], earlier_ref[3 + k], acc_s[k], acc_s[3 + k]], axis=0)
            stack = jnp.concatenate([stack, pltpu.roll(stack, NZ - HALF, axis=1)], axis=0)
            turned = stack.T
            for d in range(NZ // STRIP):
                strips_ref[d, HALF * k:HALF * (k + 1)] = turned[STRIP * d:STRIP * d + HALF]
        for store in stores:
            store.wait()


def composite_kernel(strips_ref, out_ref):
    count = strips_ref.shape[0]
    passed = jnp.ones((HALF, 128), f32)
    red = jnp.zeros((HALF, 128), f32)
    green = jnp.zeros((HALF, 128), f32)
    for s in range(count):
        red = red + passed * strips_ref[s, HALF:2 * HALF]
        green = green + passed * strips_ref[s, 2 * HALF:3 * HALF]
        passed = passed * strips_ref[s, 0:HALF]
    solid = 1.0 - passed
    red = 0.5 * (solid + red)
    whole = jnp.concatenate([red, green, solid - red, solid, jnp.zeros((32, 128), f32)], axis=0)
    turned = whole.T
    first, second = turned[0:64], turned[64:128]
    lane = lax.broadcasted_iota(jnp.int32, (1, 128), 1)
    for c in range(4):
        a = pltpu.roll(first, (128 - HALF * c) % 128, axis=1) if c else first
        b = pltpu.roll(second, (128 + HALF - HALF * c) % 128, axis=1) if c != 1 else second
        o = jnp.where(lane < HALF, a, b)
        for k in range(4):
            out_ref[k // 2, k % 2, c] = o[NY * k:NY * (k + 1), 0:STRIP]


VOLUME = (8, NX, NY, NZ)
FIELD = (NX, NY, NZ)
PLANE = (NY, NZ)
SHOWN = (6, NY, NZ)
COPY = pltpu.SemaphoreType.DMA


def shapes_of(*shapes):
    return [jax.ShapeDtypeStruct(s, f32) for s in shapes]


def kept_in(space, *shapes):
    return [space(s, f32) for s in shapes]


def anywhere():
    return pl.BlockSpec(memory_space=pl.ANY)


def inside():
    return pl.BlockSpec(memory_space=pltpu.VMEM)


def cost():
    voxels = NX * NY * NZ
    return pl.CostEstimate(flops=400 * voxels, bytes_accessed=32 * voxels, transcendentals=12 * voxels)


def interior(last, states, u, coefs, rows):
    out_specs = [inside()] * 3
    out_shape = kept_in(pltpu.VMEM, VOLUME, SHOWN, (2, NY, NZ))
    scratch = [pltpu.VMEM(FIELD, f32)] * 3
    if last:
        out_specs += [anywhere()]
        out_shape += kept_in(pltpu.HBM, VOLUME)
        scratch += [COPY]
    else:
        out_specs += [inside()]
        out_shape += kept_in(pltpu.VMEM, FIELD)
    return pl.pallas_call(
        lambda *refs: interior_kernel(last, refs),
        in_specs=[inside()] * 4,
        out_specs=out_specs,
        out_shape=out_shape,
        scratch_shapes=scratch,
        input_output_aliases={0: 0},
        compiler_params=params(8),
        cost_estimate=cost(),
        name="interior_last" if last else "interior_first",
    )(states, u, coefs, rows)


def ends(last, bases, coefs, depth, shown, rest):
    args = [bases, coefs, *depth, shown, *rest]
    in_specs = [inside()] * len(args)
    aliases = {len(args) - 2: 0, len(args) - 1: 1}
    scratch = [pltpu.VMEM(PLANE, f32)] * 2
    if last:
        out_shape = kept_in(pltpu.VMEM, VOLUME) + kept_in(pltpu.HBM, VOLUME)
        out_shape += kept_in(pltpu.VMEM, (NZ // STRIP, 3 * HALF, 128))
        scratch = [pltpu.VMEM(SHOWN, f32), *scratch, COPY((3,))]
        in_specs[-1] = anywhere()
        out_specs = [inside(), anywhere(), inside()]
    else:
        out_shape = kept_in(pltpu.VMEM, VOLUME, FIELD, SHOWN, (2, NX, NZ), (NY + 2, NZ), (NY + 2, NZ))
        out_specs = [inside()] * 6
    return pl.pallas_call(
        lambda *refs: ends_body(last, refs),
        in_specs=in_specs,
        out_specs=out_specs,
        out_shape=out_shape,
        scratch_shapes=scratch,
        input_output_aliases=aliases,
        compiler_params=params(4),
        name="ends_last" if last else "ends_first",
    )(*args)


def swaps(axis):
    count = lax.axis_size(axis)
    return [(i, i ^ 1) for i in range(count)], [(i, (((i - 1) ^ 1) + 1) % count) for i in range(count)]


def swap(axis, which, message):
    return lax.ppermute(message, axis, swaps(axis)[which])


def per_device(states, tissue, fiber):
    blocks = (NX // BLK, NY // BLK, NZ // BLK)
    states = pltpu.with_memory_space_constraint(states, pltpu.HBM)
    tissue = pltpu.with_memory_space_constraint(tissue, pltpu.HBM)
    u, ev, od, own = pl.pallas_call(
        faces_kernel,
        in_specs=[anywhere(), anywhere()],
        out_shape=kept_in(pltpu.VMEM, FIELD, (2 * NX, NZ), (2 * NX, NZ), (2, NX, NZ)),
        scratch_shapes=[pltpu.VMEM(blocks, jnp.int32), pltpu.VMEM(FIELD, f32), COPY((2,))],
        compiler_params=params(4),
        name="faces",
    )(tissue, states)
    area = swap("area", 0, ev), swap("area", 1, od)
    states, coefs, ev, od = pl.pallas_call(
        load_kernel,
        in_specs=[inside(), inside(), anywhere(), anywhere()],
        out_shape=kept_in(pltpu.VMEM, VOLUME, (7, 64, NZ), (RECORD, NZ), (RECORD, NZ)),
        scratch_shapes=[COPY((8,))],
        compiler_params=params(4),
        cost_estimate=pl.CostEstimate(flops=10**7, bytes_accessed=8 * 10**6, transcendentals=0),
        name="load",
    )(tissue, fiber, states, own)
    ev, od, rows, gates_ev, gates_od = pl.pallas_call(
        message_kernel,
        in_specs=[inside()] * 3 + [anywhere()] * 2,
        out_specs=[inside()] * 3 + [anywhere()] * 2,
        out_shape=kept_in(pltpu.VMEM, (NY + 4, NZ), (NY + 4, NZ), (4, NX, NZ), (RECORD, NZ), (RECORD, NZ)),
        input_output_aliases={3: 3, 4: 4},
        compiler_params=params(1),
        name="depth_message",
    )(*area, u, ev, od)
    gates = swap("area", 0, gates_ev), swap("area", 1, gates_od)
    depth = swap("depth", 0, ev), swap("depth", 1, od)
    states, shown, bases, after = interior(False, states, u, coefs, rows)
    states, u, images, rows, ev, od = ends(
        False, bases, coefs, depth, shown, (*gates, rows, own, states, after))
    depth = swap("depth", 0, ev), swap("depth", 1, od)
    states, shown, bases, final = interior(True, states, u, coefs, rows)
    _, states, strips = ends(True, bases, coefs, depth, shown, (images, states, final))
    strips = lax.all_to_all(strips, "depth", split_axis=0, concat_axis=0, tiled=True)
    images = pl.pallas_call(
        composite_kernel,
        out_shape=jax.ShapeDtypeStruct((2, 2, 4, NY, STRIP), f32),
        compiler_params=params(4),
        name="composite",
    )(strips)
    return states, images


def solution(mesh):
    return jax.shard_map(
        per_device,
        mesh=mesh,
        in_specs=(
            P(None, "depth", "area", None),
            P("depth", "area", None),
            P("depth", "area", None),
        ),
        out_specs=(P(None, "depth", "area", None), P(None, None, None, "area", "depth")),
        check_vma=False,
    )
```

```python
import math

import jax
import jax.numpy as jnp
from jax import lax
from jax.experimental import pallas as pl
from jax.experimental.pallas import tpu as pltpu
from jax.sharding import PartitionSpec as P

BLK = 4
CLASSES = 8
NX = 16
NY = 16
NZ = 768
STRIP = 48
HALF = STRIP // 2
CHUNK = 128
GROUPS = (1, 7, 10, 15)
GATES = 6
RECORD = GATES * NX + 2 * (NX // BLK)

TIME_STEP = 0.15
SIGMA_LONG = 1.0
SIGMA_CROSS = 0.3
SLOPES = (8.0, -8.0, 6.0, 5.0, -5.0, -3.0)
MIDDLES = (0.2, 0.4, 0.3, 0.5, 0.6, 0.5)
RATES = (3.0, 0.5, 1.0, 0.8, 0.3, 0.1)
OPACITY = (0.012, 0.01)

f32 = jnp.float32


def params(mib):
    return pltpu.CompilerParams(vmem_limit_bytes=mib * 2**20)


def is_even(axis):
    return lax.rem(lax.axis_index(axis), 2) == 0


def lane_spread(count):
    row = lax.broadcasted_iota(jnp.int32, (count, count * BLK), 0)
    column = lax.broadcasted_iota(jnp.int32, (count, count * BLK), 1)
    return row == lax.shift_right_logical(column, 2)


def flat(ref):
    return jnp.concatenate([ref[k] for k in range(NX // BLK)], axis=0)


def spread_y(wide, start):
    row = lax.broadcasted_iota(jnp.int32, (NY, 1), 0)
    out = jnp.broadcast_to(wide[start:start + 1], (NY, wide.shape[1]))
    for k in range(1, NY // BLK):
        out = jnp.where(row >= BLK * k, wide[start + k:start + k + 1], out)
    return out


def choose(first, a, b):
    return jnp.where(first, a, b)


def neighbours(axis, ev, od):
    even = is_even(axis)
    place = lax.axis_index(axis)
    below = jnp.where(place == 0, 0.0, choose(even, od, ev))
    above = jnp.where(place == lax.axis_size(axis) - 1, 0.0, choose(even, ev, od))
    return below, above


def faces_kernel(tissue_ref, states_ref, s_ref, u_ref, ev_ref, od_ref, own_ref, tissue_s, sem):
    loads = [pltpu.make_async_copy(tissue_ref, tissue_s, sem.at[0]),
             pltpu.make_async_copy(states_ref.at[0], s_ref.at[0], sem.at[1])]
    for load in loads:
        load.start()
    onehot = lane_spread(NZ // BLK).astype(jnp.bfloat16)
    loads[0].wait()
    wide = jnp.dot(flat(tissue_s).astype(f32).astype(jnp.bfloat16), onehot, preferred_element_type=f32)
    masks = [spread_y(wide, BLK * block) for block in range(NX // BLK)]
    even = is_even("area")
    loads[1].wait()
    for x in range(NX):
        u = s_ref[0, x] * masks[x // BLK]
        u_ref[x] = u
        own_ref[0, x:x + 1] = u[0:1]
        own_ref[1, x:x + 1] = u[NY - 1:NY]
        ev_ref[NX + x:NX + x + 1] = choose(even, u[NY - 2:NY - 1], u[1:2])
        od_ref[NX + x:NX + x + 1] = choose(even, u[1:2], u[NY - 2:NY - 1])
    ev_ref[0:NX] = choose(even, own_ref[1], own_ref[0])
    od_ref[0:NX] = choose(even, own_ref[0], own_ref[1])


def class_tables():
    spread = SIGMA_LONG - SIGMA_CROSS
    tables = [[] for _ in range(6)]
    for kind in range(CLASSES):
        polar = math.pi * (kind + 0.5) / CLASSES
        azimuth = 2.3 * kind
        f = (math.cos(polar), math.sin(polar) * math.cos(azimuth), math.sin(polar) * math.sin(azimuth))
        for k in range(3):
            tables[k].append(TIME_STEP * (SIGMA_CROSS + spread * f[k] * f[k]))
        for k, (a, b) in enumerate(((0, 1), (0, 2), (1, 2))):
            tables[3 + k].append(0.5 * TIME_STEP * spread * f[a] * f[b])
    return tables


def load_kernel(tissue_ref, fiber_ref, states_ref, _kept, s_ref, coefs_ref, ev_ref, od_ref, sem):
    loads = [pltpu.make_async_copy(states_ref.at[k + 1], s_ref.at[k + 1], sem.at[k]) for k in range(7)]
    for load in loads:
        load.start()
    kind = flat(fiber_ref)
    parts = [flat(tissue_ref).astype(f32)]
    for table in class_tables():
        part = jnp.full(kind.shape, table[0], f32)
        for c in range(1, CLASSES):
            part = jnp.where(kind == c, table[c], part)
        parts.append(part)
    parts.append(kind.astype(f32))
    rest = jnp.concatenate(parts, axis=0)
    onehot = lane_spread(NZ // BLK).astype(jnp.bfloat16)
    wide = None
    for _ in range(3):
        piece = rest.astype(jnp.bfloat16)
        rest = rest - piece.astype(f32)
        product = jnp.dot(piece, onehot, preferred_element_type=f32)
        wide = product if wide is None else wide + product
    for k in range(7):
        for block in range(4):
            coefs_ref[k, NY * block:NY * (block + 1)] = spread_y(wide, 16 * k + 4 * block)
    even = is_even("area")
    for place, part in ((GATES * NX, 0), (GATES * NX + 4, 7)):
        for block in range(4):
            low = wide[16 * part + 4 * block:16 * part + 4 * block + 1]
            high = wide[16 * part + 4 * block + 3:16 * part + 4 * block + 4]
            ev_ref[place + block:place + block + 1] = choose(even, high, low)
            od_ref[place + block:place + block + 1] = choose(even, low, high)
    for k in range(GATES):
        loads[k].wait()
        for x in range(NX):
            place = NX * k + x
            low = s_ref[k + 1, x, 0:1]
            high = s_ref[k + 1, x, NY - 1:NY]
            ev_ref[place:place + 1] = choose(even, high, low)
            od_ref[place:place + 1] = choose(even, low, high)
    loads[6].wait()


def message_kernel(area_ev_ref, area_od_ref, u_ref, _e, _o, ev_ref, od_ref, rows_ref, _gates_ev, _gates_od):
    even = is_even("depth")
    below, above = neighbours("area", area_ev_ref[...], area_od_ref[...])
    rows_ref[0], rows_ref[2] = below[0:NX], below[NX:2 * NX]
    rows_ref[1], rows_ref[3] = above[0:NX], above[NX:2 * NX]
    depth_messages(even, u_ref, rows_ref, ev_ref, od_ref)


def depth_messages(even, u_ref, rows_ref, ev_ref, od_ref):
    low, high = u_ref[0], u_ref[NX - 1]
    ev_ref[0:NY] = choose(even, high, low)
    od_ref[0:NY] = choose(even, low, high)
    for k in range(rows_ref.shape[0]):
        place = NY + k
        low, high = rows_ref[k, 0:1], rows_ref[k, NX - 1:NX]
        ev_ref[place:place + 1] = choose(even, high, low)
        od_ref[place:place + 1] = choose(even, low, high)


def z_sides(u):
    lane = lax.broadcasted_iota(jnp.int32, (1, NZ), 1)
    after = jnp.where(lane == NZ - 1, 0.0, pltpu.roll(u, NZ - 1, axis=1))
    before = jnp.where(lane == 0, 0.0, pltpu.roll(u, 1, axis=1))
    return after, before


def y_sides(u, row_lo, row_hi):
    row = lax.broadcasted_iota(jnp.int32, (NY, 1), 0)
    after = jnp.where(row == NY - 1, row_hi, pltpu.roll(u, NY - 1, axis=0))
    before = jnp.where(row == 0, row_lo, pltpu.roll(u, 1, axis=0))
    return after, before


def z_slope(u):
    after, before = z_sides(u)
    return after - before


def y_slope(u, row_lo, row_hi):
    after, before = y_sides(u, row_lo, row_hi)
    return after - before


def derive(planes, u_ref, coefs_ref, rows_ref, uy_ref, uz_ref, w_ref):
    row_lo = rows_ref[0]
    row_hi = rows_ref[1]
    rowz_lo = z_slope(row_lo)
    rowz_hi = z_slope(row_hi)
    for x in planes:
        rows = slice(x // BLK * NY, x // BLK * NY + NY)
        row = slice(x, x + 1)
        u = u_ref[x]
        after, before = z_sides(u)
        uz = after - before
        uz_ref[x] = uz
        w = 0.52 * u + coefs_ref[3, rows] * (after + before)
        after, before = y_sides(u, row_lo[row], row_hi[row])
        uy_ref[x] = after - before
        w = w + coefs_ref[2, rows] * (after + before)
        after, before = y_sides(uz, rowz_lo[row], rowz_hi[row])
        w_ref[x] = w + coefs_ref[6, rows] * (after - before)


def ionic(w, gates, calcium):
    fresh = []
    for k in range(6):
        keep = math.exp(-TIME_STEP * RATES[k])
        half = 0.5 * (1.0 - keep)
        t = jnp.tanh((0.5 * SLOPES[k]) * w - (0.5 * SLOPES[k] * MIDDLES[k]))
        fresh.append(half * t + (keep * gates[k] + half))
    both = fresh[3] * fresh[4]
    cube = fresh[0] * fresh[0] * fresh[0]
    loss = (
        (2.0 * TIME_STEP) * (cube * fresh[1]) * (w - 1.2)
        + TIME_STEP * (fresh[2] * fresh[2]) * (w + 0.1)
        + (0.6 * TIME_STEP) * both * (w - 0.9)
        + (0.2 * TIME_STEP) * (1.0 + fresh[5]) * (w - 0.05)
    )
    gain = (1.5 * TIME_STEP) * both
    calc_next = (1.0 - 0.8 * TIME_STEP) * calcium + gain * (1.0 - calcium)
    return w - loss, fresh, calc_next


def march(q, opaque, state):
    passed, red, green = state
    alpha = opaque * jnp.tanh(3.0 * q - 1.2) + opaque
    weight = passed * alpha
    off = q - 0.5
    red = red + weight * jnp.tanh(2.5 * off)
    green = green + weight * jnp.exp(-6.0 * (off * off))
    return passed - weight, red, green


def advance(w, old, inside):
    volt, fresh, calc = ionic(w, old[1:7], old[7])
    return [jnp.where(inside, a, b) for a, b in zip([volt] + fresh + [calc], old)]


def show(new, m, marches):
    return [march(q, (0.5 * OPACITY[f]) * m, marches[f]) for f, q in enumerate((new[0], new[7]))]


def interior_planes(planes, marches_of, s_ref, u_ref, next_ref, coefs_ref, uy_ref, uz_ref, w_ref, shown_ref):
    def chunk(j, carry):
        cols = pl.ds(pl.multiple_of(j * CHUNK, CHUNK), CHUNK)
        marches = marches_of(cols)
        for x in planes:
            rows = slice(x // BLK * NY, x // BLK * NY + NY)
            m = coefs_ref[0, rows, cols]
            w = (
                w_ref[x, :, cols]
                + coefs_ref[1, rows, cols] * (u_ref[x + 1, :, cols] + u_ref[x - 1, :, cols])
                + coefs_ref[4, rows, cols] * (uy_ref[x + 1, :, cols] - uy_ref[x - 1, :, cols])
                + coefs_ref[5, rows, cols] * (uz_ref[x + 1, :, cols] - uz_ref[x - 1, :, cols])
            )
            new = advance(w, [s_ref[k, x, :, cols] for k in range(8)], m > 0.5)
            for k in range(8):
                s_ref[k, x, :, cols] = new[k]
            if next_ref is not None:
                next_ref[x, :, cols] = m * new[0]
            marches = show(new, m, marches)
        for f in range(2):
            for k in range(3):
                shown_ref[3 * f + k, :, cols] = marches[f][k]
        return carry

    lax.fori_loop(0, NZ // CHUNK, chunk, 0)


def base_of(x, beside, sign, u_ref, coefs_ref, uy_ref, uz_ref, w_ref):
    rows = slice(x // BLK * NY, x // BLK * NY + NY)
    return (
        w_ref[x]
        + coefs_ref[1, rows] * u_ref[beside]
        + sign * (coefs_ref[4, rows] * uy_ref[beside] + coefs_ref[5, rows] * uz_ref[beside])
    )


def interior_kernel(last, refs):
    u_ref, coefs_ref, rows_ref = refs[1:4]
    if last:
        next_ref = None
        s_ref, shown_ref, base_ref, final_ref, uy_s, uz_s, w_s, sem = refs[4:]
    else:
        s_ref, shown_ref, base_ref, next_ref, uy_s, uz_s, w_s = refs[4:]
    derive(range(NX), u_ref, coefs_ref, rows_ref, uy_s, uz_s, w_s)
    base_ref[0] = base_of(0, 1, 1.0, u_ref, coefs_ref, uy_s, uz_s, w_s)
    base_ref[1] = base_of(NX - 1, NX - 2, -1.0, u_ref, coefs_ref, uy_s, uz_s, w_s)
    copies = []
    one = jnp.ones((NY, CHUNK), f32)
    zero = jnp.zeros((NY, CHUNK), f32)
    for n in range(len(GROUPS) - 1):
        def marches_of(cols):
            if n == 0:
                return [(one, zero, zero)] * 2
            return [tuple(shown_ref[3 * f + k, :, cols] for k in range(3)) for f in range(2)]

        interior_planes(range(GROUPS[n], GROUPS[n + 1]), marches_of,
                        s_ref, u_ref, next_ref, coefs_ref, uy_s, uz_s, w_s, shown_ref)
        if last and n < len(GROUPS) - 2:
            done = pl.ds(GROUPS[n], GROUPS[n + 1] - GROUPS[n])
            copies.append(pltpu.make_async_copy(s_ref.at[:, done], final_ref.at[:, done], sem.at[n]))
            copies[n].start()
    for copy in copies:
        copy.wait()


def outer_row(side, halos, rows_ref, own_ref, record):
    near, far, own = rows_ref[side], rows_ref[2 + side], own_ref[side]
    turn = 1.0 if side else -1.0
    near_place, far_place = NY + side, NY + 2 + side
    own_place = NY - 1 if side else 0

    def across(halo, place):
        return halo[place:place + 1]

    slope = turn * (far - own)
    slopes = [turn * (across(h, far_place) - across(h, own_place)) for h in halos]
    zs = [across(z_slope(h), near_place) for h in halos]
    mask = spread_y(record[GATES * NX:GATES * NX + 4], 0)
    kind = spread_y(record[GATES * NX + 4:GATES * NX + 8], 0)
    coefs = []
    for table in class_tables():
        coef = jnp.full(kind.shape, table[0], f32)
        for c in range(1, CLASSES):
            coef = jnp.where(kind == float(c), table[c], coef)
        coefs.append(coef)
    x_after, x_before = y_sides(near, across(halos[0], near_place), across(halos[1], near_place))
    z_after, z_before = z_sides(near)
    w = (
        0.52 * near
        + coefs[0] * (x_after + x_before)
        + coefs[1] * (own + far)
        + coefs[2] * (z_after + z_before)
        + coefs[3] * y_slope(slope, *slopes)
        + coefs[4] * y_slope(z_after - z_before, *zs)
        + coefs[5] * z_slope(slope)
    )
    gates = [record[NX * k:NX * (k + 1)] for k in range(GATES)]
    return mask * ionic(w, gates, jnp.zeros_like(w))[0]


def ends_body(last, refs):
    bases_ref, coefs_ref, depth_ev_ref, depth_od_ref, shown_ref = refs[:5]
    if last:
        earlier_ref, _, _, s_ref, final_ref, strips_ref, acc_s, uy_s, uz_s, sem = refs[5:]
        done = pl.ds(GROUPS[-2], GROUPS[-1] - GROUPS[-2])
        stores = [pltpu.make_async_copy(s_ref.at[:, done], final_ref.at[:, done], sem.at[2])]
        stores[0].start()
    else:
        (gates_ev_ref, gates_od_ref, rows_ref, own_ref, _, _,
         s_ref, next_ref, acc_s, ahead_ref, ev_ref, od_ref, uy_s, uz_s) = refs[5:]
    even = is_even("depth")
    halos = neighbours("depth", depth_ev_ref[...], depth_od_ref[...])
    if not last:
        records = neighbours("area", gates_ev_ref[...], gates_od_ref[...])
        for side in range(2):
            ahead_ref[side] = outer_row(side, halos, rows_ref, own_ref, records[side])
    for end, x, sign in ((0, 0, -1.0), (1, NX - 1, 1.0)):
        rows = slice(x // BLK * NY, x // BLK * NY + NY)
        halo = halos[end]
        u = halo[0:NY]
        uz_s[...] = sign * z_slope(u)
        uy_s[...] = sign * y_slope(u, halo[NY:NY + 1], halo[NY + 1:NY + 2])
        for j in range(NZ // CHUNK):
            cols = slice(j * CHUNK, (j + 1) * CHUNK)
            m = coefs_ref[0, rows, cols]
            w = (
                bases_ref[end, :, cols]
                + coefs_ref[1, rows, cols] * u[:, cols]
                + coefs_ref[4, rows, cols] * uy_s[:, cols]
                + coefs_ref[5, rows, cols] * uz_s[:, cols]
            )
            new = advance(w, [s_ref[k, x, :, cols] for k in range(8)], m > 0.5)
            for k in range(8):
                s_ref[k, x, :, cols] = new[k]
            if not last:
                next_ref[x, :, cols] = m * new[0]
            if end == 0:
                one = jnp.ones((NY, CHUNK), f32)
                zero = jnp.zeros((NY, CHUNK), f32)
                marches = show(new, m, [(one, zero, zero)] * 2)
            else:
                marches = [tuple(acc_s[3 * f + k, :, cols] for k in range(3)) for f in range(2)]
                marches = show(new, m, marches)
            for f in range(2):
                passed, red, green = marches[f]
                if end == 0:
                    red = red + passed * shown_ref[3 * f + 1, :, cols]
                    green = green + passed * shown_ref[3 * f + 2, :, cols]
                    passed = passed * shown_ref[3 * f, :, cols]
                for k, item in enumerate((passed, red, green)):
                    acc_s[3 * f + k, :, cols] = item
        if last:
            stores.append(pltpu.make_async_copy(s_ref.at[:, x], final_ref.at[:, x], sem.at[end]))
            stores[-1].start()
    if not last:
        depth_messages(even, next_ref, ahead_ref, ev_ref, od_ref)
    else:
        stacks = [jnp.concatenate([earlier_ref[k], earlier_ref[3 + k], acc_s[k], acc_s[3 + k]], axis=0)
                  for k in range(3)]
        turned = jnp.concatenate(stacks[:2], axis=0).T
        greens = jnp.concatenate([stacks[2], pltpu.roll(stacks[2], NZ - HALF, axis=1)], axis=0).T
        left = lax.broadcasted_iota(jnp.int32, (1, 128), 1) < 64
        for d in range(NZ // STRIP):
            start = STRIP * d
            a, b = turned[start:start + HALF], turned[start + HALF:start + STRIP]
            strips_ref[d, 0:HALF] = jnp.where(left, a, pltpu.roll(b, 64, axis=1))
            strips_ref[d, HALF:2 * HALF] = jnp.where(left, pltpu.roll(a, 64, axis=1), b)
            strips_ref[d, 2 * HALF:3 * HALF] = greens[start:start + HALF]
        for store in stores:
            store.wait()


def composite_kernel(strips_ref, out_ref):
    count = strips_ref.shape[0]
    passed = jnp.ones((HALF, 128), f32)
    red = jnp.zeros((HALF, 128), f32)
    green = jnp.zeros((HALF, 128), f32)
    for s in range(count):
        red = red + passed * strips_ref[s, HALF:2 * HALF]
        green = green + passed * strips_ref[s, 2 * HALF:3 * HALF]
        passed = passed * strips_ref[s, 0:HALF]
    solid = 1.0 - passed
    red = 0.5 * (solid + red)
    whole = jnp.concatenate([red, green, solid - red, solid, jnp.zeros((32, 128), f32)], axis=0)
    turned = whole.T
    first, second = turned[0:64], turned[64:128]
    lane = lax.broadcasted_iota(jnp.int32, (1, 128), 1)
    for c in range(4):
        a = pltpu.roll(first, (128 - HALF * c) % 128, axis=1) if c else first
        b = pltpu.roll(second, (128 + HALF - HALF * c) % 128, axis=1) if c != 1 else second
        o = jnp.where(lane < HALF, a, b)
        for k in range(4):
            out_ref[k // 2, k % 2, c] = o[NY * k:NY * (k + 1), 0:STRIP]


VOLUME = (8, NX, NY, NZ)
FIELD = (NX, NY, NZ)
PLANE = (NY, NZ)
SHOWN = (6, NY, NZ)
COPY = pltpu.SemaphoreType.DMA


def shapes_of(*shapes):
    return [jax.ShapeDtypeStruct(s, f32) for s in shapes]


def kept_in(space, *shapes):
    return [space(s, f32) for s in shapes]


def anywhere():
    return pl.BlockSpec(memory_space=pl.ANY)


def inside():
    return pl.BlockSpec(memory_space=pltpu.VMEM)


def cost():
    voxels = NX * NY * NZ
    return pl.CostEstimate(flops=400 * voxels, bytes_accessed=32 * voxels, transcendentals=12 * voxels)


def interior(last, states, u, coefs, rows):
    out_specs = [inside()] * 3
    out_shape = kept_in(pltpu.VMEM, VOLUME, SHOWN, (2, NY, NZ))
    scratch = [pltpu.VMEM(FIELD, f32)] * 3
    if last:
        out_specs += [anywhere()]
        out_shape += kept_in(pltpu.HBM, VOLUME)
        scratch += [COPY((len(GROUPS) - 2,))]
    else:
        out_specs += [inside()]
        out_shape += kept_in(pltpu.VMEM, FIELD)
    return pl.pallas_call(
        lambda *refs: interior_kernel(last, refs),
        in_specs=[inside()] * 4,
        out_specs=out_specs,
        out_shape=out_shape,
        scratch_shapes=scratch,
        input_output_aliases={0: 0},
        compiler_params=params(8),
        cost_estimate=cost(),
        name="interior_last" if last else "interior_first",
    )(states, u, coefs, rows)


def ends(last, bases, coefs, depth, shown, rest):
    args = [bases, coefs, *depth, shown, *rest]
    in_specs = [inside()] * len(args)
    aliases = {len(args) - 2: 0, len(args) - 1: 1}
    scratch = [pltpu.VMEM(PLANE, f32)] * 2
    if last:
        out_shape = kept_in(pltpu.VMEM, VOLUME) + kept_in(pltpu.HBM, VOLUME)
        out_shape += kept_in(pltpu.VMEM, (NZ // STRIP, 3 * HALF, 128))
        scratch = [pltpu.VMEM(SHOWN, f32), *scratch, COPY((3,))]
        in_specs[-1] = anywhere()
        out_specs = [inside(), anywhere(), inside()]
    else:
        out_shape = kept_in(pltpu.VMEM, VOLUME, FIELD, SHOWN, (2, NX, NZ), (NY + 2, NZ), (NY + 2, NZ))
        out_specs = [inside()] * 6
    return pl.pallas_call(
        lambda *refs: ends_body(last, refs),
        in_specs=in_specs,
        out_specs=out_specs,
        out_shape=out_shape,
        scratch_shapes=scratch,
        input_output_aliases=aliases,
        compiler_params=params(4),
        name="ends_last" if last else "ends_first",
    )(*args)


def swaps(axis):
    count = lax.axis_size(axis)
    return [(i, i ^ 1) for i in range(count)], [(i, (((i - 1) ^ 1) + 1) % count) for i in range(count)]


def swap(axis, which, message):
    return lax.ppermute(message, axis, swaps(axis)[which])


def per_device(states, tissue, fiber):
    blocks = (NX // BLK, NY // BLK, NZ // BLK)
    states = pltpu.with_memory_space_constraint(states, pltpu.HBM)
    tissue = pltpu.with_memory_space_constraint(tissue, pltpu.HBM)
    kept, u, ev, od, own = pl.pallas_call(
        faces_kernel,
        in_specs=[anywhere(), anywhere()],
        out_shape=kept_in(pltpu.VMEM, VOLUME, FIELD, (2 * NX, NZ), (2 * NX, NZ), (2, NX, NZ)),
        scratch_shapes=[pltpu.VMEM(blocks, jnp.int32), COPY((2,))],
        compiler_params=params(4),
        name="faces",
    )(tissue, states)
    area = swap("area", 0, ev), swap("area", 1, od)
    states, coefs, ev, od = pl.pallas_call(
        load_kernel,
        in_specs=[inside(), inside(), anywhere(), inside()],
        out_shape=kept_in(pltpu.VMEM, VOLUME, (7, 64, NZ), (RECORD, NZ), (RECORD, NZ)),
        scratch_shapes=[COPY((7,))],
        input_output_aliases={3: 0},
        compiler_params=params(4),
        cost_estimate=pl.CostEstimate(flops=10**7, bytes_accessed=8 * 10**6, transcendentals=0),
        name="load",
    )(tissue, fiber, states, kept)
    ev, od, rows, gates_ev, gates_od = pl.pallas_call(
        message_kernel,
        in_specs=[inside()] * 3 + [anywhere()] * 2,
        out_specs=[inside()] * 3 + [anywhere()] * 2,
        out_shape=kept_in(pltpu.VMEM, (NY + 4, NZ), (NY + 4, NZ), (4, NX, NZ), (RECORD, NZ), (RECORD, NZ)),
        input_output_aliases={3: 3, 4: 4},
        compiler_params=params(1),
        name="depth_message",
    )(*area, u, ev, od)
    gates = swap("area", 0, gates_ev), swap("area", 1, gates_od)
    depth = swap("depth", 0, ev), swap("depth", 1, od)
    states, shown, bases, after = interior(False, states, u, coefs, rows)
    states, u, images, rows, ev, od = ends(
        False, bases, coefs, depth, shown, (*gates, rows, own, states, after))
    depth = swap("depth", 0, ev), swap("depth", 1, od)
    states, shown, bases, final = interior(True, states, u, coefs, rows)
    _, states, strips = ends(True, bases, coefs, depth, shown, (images, states, final))
    strips = lax.all_to_all(strips, "depth", split_axis=0, concat_axis=0, tiled=True)
    images = pl.pallas_call(
        composite_kernel,
        out_shape=jax.ShapeDtypeStruct((2, 2, 4, NY, STRIP), f32),
        compiler_params=params(4),
        name="composite",
    )(strips)
    return states, images


def solution(mesh):
    return jax.shard_map(
        per_device,
        mesh=mesh,
        in_specs=(
            P(None, "depth", "area", None),
            P("depth", "area", None),
            P("depth", "area", None),
        ),
        out_specs=(P(None, "depth", "area", None), P(None, None, None, "area", "depth")),
        check_vma=False,
    )
```

```python
import math

import jax
import jax.numpy as jnp
from jax import lax
from jax.experimental import pallas as pl
from jax.experimental.pallas import tpu as pltpu
from jax.sharding import PartitionSpec as P

BLK = 4
CLASSES = 8
NX = 16
NY = 16
NZ = 768
STRIP = 48
HALF = STRIP // 2
CHUNK = 128
GROUPS = (1, 7, 10, 15)
GATES = 6
RECORD = GATES * NX + 8 * (NX // BLK)

TIME_STEP = 0.15
SIGMA_LONG = 1.0
SIGMA_CROSS = 0.3
SLOPES = (8.0, -8.0, 6.0, 5.0, -5.0, -3.0)
MIDDLES = (0.2, 0.4, 0.3, 0.5, 0.6, 0.5)
RATES = (3.0, 0.5, 1.0, 0.8, 0.3, 0.1)
OPACITY = (0.012, 0.01)

f32 = jnp.float32


def params(mib):
    return pltpu.CompilerParams(vmem_limit_bytes=mib * 2**20)


def is_even(axis):
    return lax.rem(lax.axis_index(axis), 2) == 0


def lane_spread(count):
    row = lax.broadcasted_iota(jnp.int32, (count, count * BLK), 0)
    column = lax.broadcasted_iota(jnp.int32, (count, count * BLK), 1)
    return row == lax.shift_right_logical(column, 2)


def flat(ref):
    return jnp.concatenate([ref[k] for k in range(NX // BLK)], axis=0)


def spread_y(wide, start):
    row = lax.broadcasted_iota(jnp.int32, (NY, 1), 0)
    out = jnp.broadcast_to(wide[start:start + 1], (NY, wide.shape[1]))
    for k in range(1, NY // BLK):
        out = jnp.where(row >= BLK * k, wide[start + k:start + k + 1], out)
    return out


def choose(first, a, b):
    return jnp.where(first, a, b)


def neighbours(axis, ev, od):
    even = is_even(axis)
    place = lax.axis_index(axis)
    below = jnp.where(place == 0, 0.0, choose(even, od, ev))
    above = jnp.where(place == lax.axis_size(axis) - 1, 0.0, choose(even, ev, od))
    return below, above


def faces_kernel(tissue_ref, states_ref, s_ref, u_ref, ev_ref, od_ref, own_ref, tissue_s, sem):
    loads = [pltpu.make_async_copy(tissue_ref, tissue_s, sem.at[0])]
    for block in range(NX // BLK):
        part = pl.ds(BLK * block, BLK)
        loads.append(pltpu.make_async_copy(states_ref.at[0, part], s_ref.at[0, part], sem.at[1 + block]))
    for load in loads:
        load.start()
    onehot = lane_spread(NZ // BLK).astype(jnp.bfloat16)
    loads[0].wait()
    wide = jnp.dot(flat(tissue_s).astype(f32).astype(jnp.bfloat16), onehot, preferred_element_type=f32)
    masks = [spread_y(wide, BLK * block) for block in range(NX // BLK)]
    even = is_even("area")
    for x in range(NX):
        if x % BLK == 0:
            loads[1 + x // BLK].wait()
        u = s_ref[0, x] * masks[x // BLK]
        u_ref[x] = u
        own_ref[0, x:x + 1] = u[0:1]
        own_ref[1, x:x + 1] = u[NY - 1:NY]
        ev_ref[NX + x:NX + x + 1] = choose(even, u[NY - 2:NY - 1], u[1:2])
        od_ref[NX + x:NX + x + 1] = choose(even, u[1:2], u[NY - 2:NY - 1])
    ev_ref[0:NX] = choose(even, own_ref[1], own_ref[0])
    od_ref[0:NX] = choose(even, own_ref[0], own_ref[1])


def class_tables():
    spread = SIGMA_LONG - SIGMA_CROSS
    tables = [[] for _ in range(6)]
    for kind in range(CLASSES):
        polar = math.pi * (kind + 0.5) / CLASSES
        azimuth = 2.3 * kind
        f = (math.cos(polar), math.sin(polar) * math.cos(azimuth), math.sin(polar) * math.sin(azimuth))
        for k in range(3):
            tables[k].append(TIME_STEP * (SIGMA_CROSS + spread * f[k] * f[k]))
        for k, (a, b) in enumerate(((0, 1), (0, 2), (1, 2))):
            tables[3 + k].append(0.5 * TIME_STEP * spread * f[a] * f[b])
    return tables


def load_kernel(tissue_ref, fiber_ref, states_ref, _kept, s_ref, coefs_ref, ev_ref, od_ref, sem):
    loads = [pltpu.make_async_copy(states_ref.at[k + 1], s_ref.at[k + 1], sem.at[k]) for k in range(7)]
    for load in loads:
        load.start()
    kind = flat(fiber_ref)
    parts = [flat(tissue_ref).astype(f32)]
    for table in class_tables():
        part = jnp.full(kind.shape, table[0], f32)
        for c in range(1, CLASSES):
            part = jnp.where(kind == c, table[c], part)
        parts.append(part)
    rest = jnp.concatenate(parts, axis=0)
    onehot = lane_spread(NZ // BLK).astype(jnp.bfloat16)
    wide = None
    for _ in range(3):
        piece = rest.astype(jnp.bfloat16)
        rest = rest - piece.astype(f32)
        product = jnp.dot(piece, onehot, preferred_element_type=f32)
        wide = product if wide is None else wide + product
    for k in range(7):
        for block in range(4):
            coefs_ref[k, NY * block:NY * (block + 1)] = spread_y(wide, 16 * k + 4 * block)
    even = is_even("area")
    for part in range(7):
        place = GATES * NX + BLK * part
        for block in range(4):
            low = wide[16 * part + 4 * block:16 * part + 4 * block + 1]
            high = wide[16 * part + 4 * block + 3:16 * part + 4 * block + 4]
            ev_ref[place + block:place + block + 1] = choose(even, high, low)
            od_ref[place + block:place + block + 1] = choose(even, low, high)
    for k in range(GATES):
        loads[k].wait()
        for x in range(NX):
            place = NX * k + x
            low = s_ref[k + 1, x, 0:1]
            high = s_ref[k + 1, x, NY - 1:NY]
            ev_ref[place:place + 1] = choose(even, high, low)
            od_ref[place:place + 1] = choose(even, low, high)
    spare = pl.ds(GATES * NX + 7 * BLK, BLK)
    ev_ref[spare] = jnp.zeros((BLK, NZ), f32)
    od_ref[spare] = jnp.zeros((BLK, NZ), f32)
    loads[6].wait()


def message_kernel(area_ev_ref, area_od_ref, u_ref, _e, _o, ev_ref, od_ref, rows_ref, _gates_ev, _gates_od):
    even = is_even("depth")
    below, above = neighbours("area", area_ev_ref[...], area_od_ref[...])
    rows_ref[0], rows_ref[2] = below[0:NX], below[NX:2 * NX]
    rows_ref[1], rows_ref[3] = above[0:NX], above[NX:2 * NX]
    depth_messages(even, u_ref, rows_ref, ev_ref, od_ref)


def depth_messages(even, u_ref, rows_ref, ev_ref, od_ref):
    low, high = u_ref[0], u_ref[NX - 1]
    ev_ref[0:NY] = choose(even, high, low)
    od_ref[0:NY] = choose(even, low, high)
    for k in range(rows_ref.shape[0]):
        place = NY + k
        low, high = rows_ref[k, 0:1], rows_ref[k, NX - 1:NX]
        ev_ref[place:place + 1] = choose(even, high, low)
        od_ref[place:place + 1] = choose(even, low, high)


def z_sides(u):
    lane = lax.broadcasted_iota(jnp.int32, (1, NZ), 1)
    after = jnp.where(lane == NZ - 1, 0.0, pltpu.roll(u, NZ - 1, axis=1))
    before = jnp.where(lane == 0, 0.0, pltpu.roll(u, 1, axis=1))
    return after, before


def y_sides(u, row_lo, row_hi):
    row = lax.broadcasted_iota(jnp.int32, (NY, 1), 0)
    after = jnp.where(row == NY - 1, row_hi, pltpu.roll(u, NY - 1, axis=0))
    before = jnp.where(row == 0, row_lo, pltpu.roll(u, 1, axis=0))
    return after, before


def z_slope(u):
    after, before = z_sides(u)
    return after - before


def y_slope(u, row_lo, row_hi):
    after, before = y_sides(u, row_lo, row_hi)
    return after - before


def derive(planes, u_ref, coefs_ref, rows_ref, uy_ref, uz_ref, w_ref):
    row_lo = rows_ref[0]
    row_hi = rows_ref[1]
    rowz_lo = z_slope(row_lo)
    rowz_hi = z_slope(row_hi)
    for x in planes:
        rows = slice(x // BLK * NY, x // BLK * NY + NY)
        row = slice(x, x + 1)
        u = u_ref[x]
        after, before = z_sides(u)
        uz = after - before
        uz_ref[x] = uz
        w = 0.52 * u + coefs_ref[3, rows] * (after + before)
        after, before = y_sides(u, row_lo[row], row_hi[row])
        uy_ref[x] = after - before
        w = w + coefs_ref[2, rows] * (after + before)
        after, before = y_sides(uz, rowz_lo[row], rowz_hi[row])
        w_ref[x] = w + coefs_ref[6, rows] * (after - before)


def ionic(w, gates, calcium):
    fresh = []
    for k in range(6):
        keep = math.exp(-TIME_STEP * RATES[k])
        half = 0.5 * (1.0 - keep)
        t = jnp.tanh((0.5 * SLOPES[k]) * w - (0.5 * SLOPES[k] * MIDDLES[k]))
        fresh.append(half * t + (keep * gates[k] + half))
    both = fresh[3] * fresh[4]
    cube = fresh[0] * fresh[0] * fresh[0]
    loss = (
        (2.0 * TIME_STEP) * (cube * fresh[1]) * (w - 1.2)
        + TIME_STEP * (fresh[2] * fresh[2]) * (w + 0.1)
        + (0.6 * TIME_STEP) * both * (w - 0.9)
        + (0.2 * TIME_STEP) * (1.0 + fresh[5]) * (w - 0.05)
    )
    gain = (1.5 * TIME_STEP) * both
    calc_next = (1.0 - 0.8 * TIME_STEP) * calcium + gain * (1.0 - calcium)
    return w - loss, fresh, calc_next


def march(q, opaque, state):
    passed, red, green = state
    alpha = opaque * jnp.tanh(3.0 * q - 1.2) + opaque
    weight = passed * alpha
    off = q - 0.5
    red = red + weight * jnp.tanh(2.5 * off)
    green = green + weight * jnp.exp(-6.0 * (off * off))
    return passed - weight, red, green


def advance(w, old, inside):
    volt, fresh, calc = ionic(w, old[1:7], old[7])
    return [jnp.where(inside, a, b) for a, b in zip([volt] + fresh + [calc], old)]


def show(new, m, marches):
    return [march(q, (0.5 * OPACITY[f]) * m, marches[f]) for f, q in enumerate((new[0], new[7]))]


def interior_planes(planes, marches_of, s_ref, u_ref, next_ref, coefs_ref, uy_ref, uz_ref, w_ref, shown_ref):
    def chunk(j, carry):
        cols = pl.ds(pl.multiple_of(j * CHUNK, CHUNK), CHUNK)
        marches = marches_of(cols)
        for x in planes:
            rows = slice(x // BLK * NY, x // BLK * NY + NY)
            m = coefs_ref[0, rows, cols]
            w = (
                w_ref[x, :, cols]
                + coefs_ref[1, rows, cols] * (u_ref[x + 1, :, cols] + u_ref[x - 1, :, cols])
                + coefs_ref[4, rows, cols] * (uy_ref[x + 1, :, cols] - uy_ref[x - 1, :, cols])
                + coefs_ref[5, rows, cols] * (uz_ref[x + 1, :, cols] - uz_ref[x - 1, :, cols])
            )
            new = advance(w, [s_ref[k, x, :, cols] for k in range(8)], m > 0.5)
            for k in range(8):
                s_ref[k, x, :, cols] = new[k]
            if next_ref is not None:
                next_ref[x, :, cols] = m * new[0]
            marches = show(new, m, marches)
        for f in range(2):
            for k in range(3):
                shown_ref[3 * f + k, :, cols] = marches[f][k]
        return carry

    lax.fori_loop(0, NZ // CHUNK, chunk, 0)


def base_of(x, beside, sign, u_ref, coefs_ref, uy_ref, uz_ref, w_ref):
    rows = slice(x // BLK * NY, x // BLK * NY + NY)
    return (
        w_ref[x]
        + coefs_ref[1, rows] * u_ref[beside]
        + sign * (coefs_ref[4, rows] * uy_ref[beside] + coefs_ref[5, rows] * uz_ref[beside])
    )


def interior_kernel(last, refs):
    u_ref, coefs_ref, rows_ref = refs[1:4]
    if last:
        next_ref = None
        s_ref, shown_ref, base_ref, final_ref, uy_s, uz_s, w_s, sem = refs[4:]
    else:
        s_ref, shown_ref, base_ref, next_ref, uy_s, uz_s, w_s = refs[4:]
    derive(range(NX), u_ref, coefs_ref, rows_ref, uy_s, uz_s, w_s)
    base_ref[0] = base_of(0, 1, 1.0, u_ref, coefs_ref, uy_s, uz_s, w_s)
    base_ref[1] = base_of(NX - 1, NX - 2, -1.0, u_ref, coefs_ref, uy_s, uz_s, w_s)
    copies = []
    one = jnp.ones((NY, CHUNK), f32)
    zero = jnp.zeros((NY, CHUNK), f32)
    for n in range(len(GROUPS) - 1):
        def marches_of(cols):
            if n == 0:
                return [(one, zero, zero)] * 2
            return [tuple(shown_ref[3 * f + k, :, cols] for k in range(3)) for f in range(2)]

        interior_planes(range(GROUPS[n], GROUPS[n + 1]), marches_of,
                        s_ref, u_ref, next_ref, coefs_ref, uy_s, uz_s, w_s, shown_ref)
        if last and n < len(GROUPS) - 2:
            done = pl.ds(GROUPS[n], GROUPS[n + 1] - GROUPS[n])
            copies.append(pltpu.make_async_copy(s_ref.at[:, done], final_ref.at[:, done], sem.at[n]))
            copies[n].start()
    for copy in copies:
        copy.wait()


def outer_row(side, halos, rows_ref, own_ref, record):
    near, far, own = rows_ref[side], rows_ref[2 + side], own_ref[side]
    turn = 1.0 if side else -1.0
    near_place, far_place = NY + side, NY + 2 + side
    own_place = NY - 1 if side else 0

    def across(halo, place):
        return halo[place:place + 1]

    slope = turn * (far - own)
    slopes = [turn * (across(h, far_place) - across(h, own_place)) for h in halos]
    zs = [across(z_slope(h), near_place) for h in halos]
    mask = spread_y(record[GATES * NX:GATES * NX + 4], 0)
    coefs = [spread_y(record[GATES * NX + BLK * k:GATES * NX + BLK * (k + 1)], 0) for k in range(1, 7)]
    x_after, x_before = y_sides(near, across(halos[0], near_place), across(halos[1], near_place))
    z_after, z_before = z_sides(near)
    w = (
        0.52 * near
        + coefs[0] * (x_after + x_before)
        + coefs[1] * (own + far)
        + coefs[2] * (z_after + z_before)
        + coefs[3] * y_slope(slope, *slopes)
        + coefs[4] * y_slope(z_after - z_before, *zs)
        + coefs[5] * z_slope(slope)
    )
    gates = [record[NX * k:NX * (k + 1)] for k in range(GATES)]
    return mask * ionic(w, gates, jnp.zeros_like(w))[0]


def ends_body(last, refs):
    bases_ref, coefs_ref, depth_ev_ref, depth_od_ref, shown_ref = refs[:5]
    if last:
        earlier_ref, _, _, s_ref, final_ref, strips_ref, acc_s, uy_s, uz_s, sem = refs[5:]
        done = pl.ds(GROUPS[-2], GROUPS[-1] - GROUPS[-2])
        stores = [pltpu.make_async_copy(s_ref.at[:, done], final_ref.at[:, done], sem.at[2])]
        stores[0].start()
    else:
        (gates_ev_ref, gates_od_ref, rows_ref, own_ref, _, _,
         s_ref, next_ref, acc_s, ahead_ref, ev_ref, od_ref, uy_s, uz_s) = refs[5:]
    even = is_even("depth")
    halos = neighbours("depth", depth_ev_ref[...], depth_od_ref[...])
    if not last:
        records = neighbours("area", gates_ev_ref[...], gates_od_ref[...])
        for side in range(2):
            ahead_ref[side] = outer_row(side, halos, rows_ref, own_ref, records[side])
    for end, x, sign in ((0, 0, -1.0), (1, NX - 1, 1.0)):
        rows = slice(x // BLK * NY, x // BLK * NY + NY)
        halo = halos[end]
        u = halo[0:NY]
        uz_s[...] = sign * z_slope(u)
        uy_s[...] = sign * y_slope(u, halo[NY:NY + 1], halo[NY + 1:NY + 2])
        for j in range(NZ // CHUNK):
            cols = slice(j * CHUNK, (j + 1) * CHUNK)
            m = coefs_ref[0, rows, cols]
            w = (
                bases_ref[end, :, cols]
                + coefs_ref[1, rows, cols] * u[:, cols]
                + coefs_ref[4, rows, cols] * uy_s[:, cols]
                + coefs_ref[5, rows, cols] * uz_s[:, cols]
            )
            new = advance(w, [s_ref[k, x, :, cols] for k in range(8)], m > 0.5)
            for k in range(8):
                s_ref[k, x, :, cols] = new[k]
            if not last:
                next_ref[x, :, cols] = m * new[0]
            if end == 0:
                one = jnp.ones((NY, CHUNK), f32)
                zero = jnp.zeros((NY, CHUNK), f32)
                marches = show(new, m, [(one, zero, zero)] * 2)
            else:
                marches = [tuple(acc_s[3 * f + k, :, cols] for k in range(3)) for f in range(2)]
                marches = show(new, m, marches)
            for f in range(2):
                passed, red, green = marches[f]
                if end == 0:
                    red = red + passed * shown_ref[3 * f + 1, :, cols]
                    green = green + passed * shown_ref[3 * f + 2, :, cols]
                    passed = passed * shown_ref[3 * f, :, cols]
                for k, item in enumerate((passed, red, green)):
                    acc_s[3 * f + k, :, cols] = item
        if last:
            stores.append(pltpu.make_async_copy(s_ref.at[:, x], final_ref.at[:, x], sem.at[end]))
            stores[-1].start()
    if not last:
        depth_messages(even, next_ref, ahead_ref, ev_ref, od_ref)
    else:
        stacks = [jnp.concatenate([earlier_ref[k], earlier_ref[3 + k], acc_s[k], acc_s[3 + k]], axis=0)
                  for k in range(3)]
        turned = jnp.concatenate(stacks[:2], axis=0).T
        greens = jnp.concatenate([stacks[2], pltpu.roll(stacks[2], NZ - HALF, axis=1)], axis=0).T
        left = lax.broadcasted_iota(jnp.int32, (1, 128), 1) < 64
        for d in range(NZ // STRIP):
            start = STRIP * d
            a, b = turned[start:start + HALF], turned[start + HALF:start + STRIP]
            strips_ref[d, 0:HALF] = jnp.where(left, a, pltpu.roll(b, 64, axis=1))
            strips_ref[d, HALF:2 * HALF] = jnp.where(left, pltpu.roll(a, 64, axis=1), b)
            strips_ref[d, 2 * HALF:3 * HALF] = greens[start:start + HALF]
        for store in stores:
            store.wait()


def composite_kernel(strips_ref, out_ref):
    count = strips_ref.shape[0]
    passed = jnp.ones((HALF, 128), f32)
    red = jnp.zeros((HALF, 128), f32)
    green = jnp.zeros((HALF, 128), f32)
    for s in range(count):
        red = red + passed * strips_ref[s, HALF:2 * HALF]
        green = green + passed * strips_ref[s, 2 * HALF:3 * HALF]
        passed = passed * strips_ref[s, 0:HALF]
    solid = 1.0 - passed
    red = 0.5 * (solid + red)
    whole = jnp.concatenate([red, green, solid - red, solid, jnp.zeros((32, 128), f32)], axis=0)
    turned = whole.T
    first, second = turned[0:64], turned[64:128]
    lane = lax.broadcasted_iota(jnp.int32, (1, 128), 1)
    for c in range(4):
        a = pltpu.roll(first, (128 - HALF * c) % 128, axis=1) if c else first
        b = pltpu.roll(second, (128 + HALF - HALF * c) % 128, axis=1) if c != 1 else second
        o = jnp.where(lane < HALF, a, b)
        for k in range(4):
            out_ref[k // 2, k % 2, c] = o[NY * k:NY * (k + 1), 0:STRIP]


VOLUME = (8, NX, NY, NZ)
FIELD = (NX, NY, NZ)
PLANE = (NY, NZ)
SHOWN = (6, NY, NZ)
COPY = pltpu.SemaphoreType.DMA


def shapes_of(*shapes):
    return [jax.ShapeDtypeStruct(s, f32) for s in shapes]


def kept_in(space, *shapes):
    return [space(s, f32) for s in shapes]


def anywhere():
    return pl.BlockSpec(memory_space=pl.ANY)


def inside():
    return pl.BlockSpec(memory_space=pltpu.VMEM)


def cost():
    voxels = NX * NY * NZ
    return pl.CostEstimate(flops=400 * voxels, bytes_accessed=32 * voxels, transcendentals=12 * voxels)


def interior(last, states, u, coefs, rows):
    out_specs = [inside()] * 3
    out_shape = kept_in(pltpu.VMEM, VOLUME, SHOWN, (2, NY, NZ))
    scratch = [pltpu.VMEM(FIELD, f32)] * 3
    if last:
        out_specs += [anywhere()]
        out_shape += kept_in(pltpu.HBM, VOLUME)
        scratch += [COPY((len(GROUPS) - 2,))]
    else:
        out_specs += [inside()]
        out_shape += kept_in(pltpu.VMEM, FIELD)
    return pl.pallas_call(
        lambda *refs: interior_kernel(last, refs),
        in_specs=[inside()] * 4,
        out_specs=out_specs,
        out_shape=out_shape,
        scratch_shapes=scratch,
        input_output_aliases={0: 0},
        compiler_params=params(8),
        cost_estimate=cost(),
        name="interior_last" if last else "interior_first",
    )(states, u, coefs, rows)


def ends(last, bases, coefs, depth, shown, rest):
    args = [bases, coefs, *depth, shown, *rest]
    in_specs = [inside()] * len(args)
    aliases = {len(args) - 2: 0, len(args) - 1: 1}
    scratch = [pltpu.VMEM(PLANE, f32)] * 2
    if last:
        out_shape = kept_in(pltpu.VMEM, VOLUME) + kept_in(pltpu.HBM, VOLUME)
        out_shape += kept_in(pltpu.VMEM, (NZ // STRIP, 3 * HALF, 128))
        scratch = [pltpu.VMEM(SHOWN, f32), *scratch, COPY((3,))]
        in_specs[-1] = anywhere()
        out_specs = [inside(), anywhere(), inside()]
    else:
        out_shape = kept_in(pltpu.VMEM, VOLUME, FIELD, SHOWN, (2, NX, NZ), (NY + 2, NZ), (NY + 2, NZ))
        out_specs = [inside()] * 6
    return pl.pallas_call(
        lambda *refs: ends_body(last, refs),
        in_specs=in_specs,
        out_specs=out_specs,
        out_shape=out_shape,
        scratch_shapes=scratch,
        input_output_aliases=aliases,
        compiler_params=params(4),
        name="ends_last" if last else "ends_first",
    )(*args)


def swaps(axis):
    count = lax.axis_size(axis)
    return [(i, i ^ 1) for i in range(count)], [(i, (((i - 1) ^ 1) + 1) % count) for i in range(count)]


def swap(axis, which, message):
    return lax.ppermute(message, axis, swaps(axis)[which])


def per_device(states, tissue, fiber):
    blocks = (NX // BLK, NY // BLK, NZ // BLK)
    states = pltpu.with_memory_space_constraint(states, pltpu.HBM)
    tissue = pltpu.with_memory_space_constraint(tissue, pltpu.HBM)
    kept, u, ev, od, own = pl.pallas_call(
        faces_kernel,
        in_specs=[anywhere(), anywhere()],
        out_shape=kept_in(pltpu.VMEM, VOLUME, FIELD, (2 * NX, NZ), (2 * NX, NZ), (2, NX, NZ)),
        scratch_shapes=[pltpu.VMEM(blocks, jnp.int32), COPY((1 + NX // BLK,))],
        compiler_params=params(4),
        name="faces",
    )(tissue, states)
    area = swap("area", 0, ev), swap("area", 1, od)
    states, coefs, ev, od = pl.pallas_call(
        load_kernel,
        in_specs=[inside(), inside(), anywhere(), inside()],
        out_shape=kept_in(pltpu.VMEM, VOLUME, (7, 64, NZ), (RECORD, NZ), (RECORD, NZ)),
        scratch_shapes=[COPY((7,))],
        input_output_aliases={3: 0},
        compiler_params=params(4),
        cost_estimate=pl.CostEstimate(flops=10**7, bytes_accessed=8 * 10**6, transcendentals=0),
        name="load",
    )(tissue, fiber, states, kept)
    ev, od, rows, gates_ev, gates_od = pl.pallas_call(
        message_kernel,
        in_specs=[inside()] * 3 + [anywhere()] * 2,
        out_specs=[inside()] * 3 + [anywhere()] * 2,
        out_shape=kept_in(pltpu.VMEM, (NY + 4, NZ), (NY + 4, NZ), (4, NX, NZ), (RECORD, NZ), (RECORD, NZ)),
        input_output_aliases={3: 3, 4: 4},
        compiler_params=params(1),
        name="depth_message",
    )(*area, u, ev, od)
    gates = swap("area", 0, gates_ev), swap("area", 1, gates_od)
    depth = swap("depth", 0, ev), swap("depth", 1, od)
    states, shown, bases, after = interior(False, states, u, coefs, rows)
    states, u, images, rows, ev, od = ends(
        False, bases, coefs, depth, shown, (*gates, rows, own, states, after))
    depth = swap("depth", 0, ev), swap("depth", 1, od)
    states, shown, bases, final = interior(True, states, u, coefs, rows)
    _, states, strips = ends(True, bases, coefs, depth, shown, (images, states, final))
    strips = lax.all_to_all(strips, "depth", split_axis=0, concat_axis=0, tiled=True)
    images = pl.pallas_call(
        composite_kernel,
        out_shape=jax.ShapeDtypeStruct((2, 2, 4, NY, STRIP), f32),
        compiler_params=params(4),
        name="composite",
    )(strips)
    return states, images


def solution(mesh):
    return jax.shard_map(
        per_device,
        mesh=mesh,
        in_specs=(
            P(None, "depth", "area", None),
            P("depth", "area", None),
            P("depth", "area", None),
        ),
        out_specs=(P(None, "depth", "area", None), P(None, None, None, "area", "depth")),
        check_vma=False,
    )
```

```python
import math

import jax
import jax.numpy as jnp
from jax import lax
from jax.experimental import pallas as pl
from jax.experimental.pallas import tpu as pltpu
from jax.sharding import PartitionSpec as P

BLK = 4
CLASSES = 8
NX = 16
NY = 16
NZ = 768
STRIP = 48
HALF = STRIP // 2
CHUNK = 128
GROUPS = (1, 6, 9, 12, 15)
GATES = 6
RECORD = GATES * NX + 8 * (NX // BLK)

TIME_STEP = 0.15
SIGMA_LONG = 1.0
SIGMA_CROSS = 0.3
SLOPES = (8.0, -8.0, 6.0, 5.0, -5.0, -3.0)
MIDDLES = (0.2, 0.4, 0.3, 0.5, 0.6, 0.5)
RATES = (3.0, 0.5, 1.0, 0.8, 0.3, 0.1)
OPACITY = (0.012, 0.01)

f32 = jnp.float32


def params(mib):
    return pltpu.CompilerParams(vmem_limit_bytes=mib * 2**20)


def is_even(axis):
    return lax.rem(lax.axis_index(axis), 2) == 0


def lane_spread(count):
    row = lax.broadcasted_iota(jnp.int32, (count, count * BLK), 0)
    column = lax.broadcasted_iota(jnp.int32, (count, count * BLK), 1)
    return row == lax.shift_right_logical(column, 2)


def flat(ref):
    return jnp.concatenate([ref[k] for k in range(NX // BLK)], axis=0)


def spread_y(wide, start):
    row = lax.broadcasted_iota(jnp.int32, (NY, 1), 0)
    out = jnp.broadcast_to(wide[start:start + 1], (NY, wide.shape[1]))
    for k in range(1, NY // BLK):
        out = jnp.where(row >= BLK * k, wide[start + k:start + k + 1], out)
    return out


def choose(first, a, b):
    return jnp.where(first, a, b)


def neighbours(axis, ev, od):
    even = is_even(axis)
    place = lax.axis_index(axis)
    below = jnp.where(place == 0, 0.0, choose(even, od, ev))
    above = jnp.where(place == lax.axis_size(axis) - 1, 0.0, choose(even, ev, od))
    return below, above


def faces_kernel(tissue_ref, states_ref, s_ref, u_ref, ev_ref, od_ref, own_ref, tissue_s, sem):
    loads = [pltpu.make_async_copy(tissue_ref, tissue_s, sem.at[0])]
    for block in range(NX // BLK):
        part = pl.ds(BLK * block, BLK)
        loads.append(pltpu.make_async_copy(states_ref.at[0, part], s_ref.at[0, part], sem.at[1 + block]))
    for load in loads:
        load.start()
    onehot = lane_spread(NZ // BLK).astype(jnp.bfloat16)
    loads[0].wait()
    wide = jnp.dot(flat(tissue_s).astype(f32).astype(jnp.bfloat16), onehot, preferred_element_type=f32)
    masks = [spread_y(wide, BLK * block) for block in range(NX // BLK)]
    even = is_even("area")
    for x in range(NX):
        if x % BLK == 0:
            loads[1 + x // BLK].wait()
        u = s_ref[0, x] * masks[x // BLK]
        u_ref[x] = u
        own_ref[0, x:x + 1] = u[0:1]
        own_ref[1, x:x + 1] = u[NY - 1:NY]
        ev_ref[NX + x:NX + x + 1] = choose(even, u[NY - 2:NY - 1], u[1:2])
        od_ref[NX + x:NX + x + 1] = choose(even, u[1:2], u[NY - 2:NY - 1])
    ev_ref[0:NX] = choose(even, own_ref[1], own_ref[0])
    od_ref[0:NX] = choose(even, own_ref[0], own_ref[1])


def class_tables():
    spread = SIGMA_LONG - SIGMA_CROSS
    tables = [[] for _ in range(6)]
    for kind in range(CLASSES):
        polar = math.pi * (kind + 0.5) / CLASSES
        azimuth = 2.3 * kind
        f = (math.cos(polar), math.sin(polar) * math.cos(azimuth), math.sin(polar) * math.sin(azimuth))
        for k in range(3):
            tables[k].append(TIME_STEP * (SIGMA_CROSS + spread * f[k] * f[k]))
        for k, (a, b) in enumerate(((0, 1), (0, 2), (1, 2))):
            tables[3 + k].append(0.5 * TIME_STEP * spread * f[a] * f[b])
    return tables


def load_kernel(tissue_ref, fiber_ref, states_ref, _kept, s_ref, coefs_ref, ev_ref, od_ref, sem):
    loads = [pltpu.make_async_copy(states_ref.at[k + 1], s_ref.at[k + 1], sem.at[k]) for k in range(7)]
    for load in loads:
        load.start()
    kind = flat(fiber_ref)
    parts = [flat(tissue_ref).astype(f32)]
    for table in class_tables():
        part = jnp.full(kind.shape, table[0], f32)
        for c in range(1, CLASSES):
            part = jnp.where(kind == c, table[c], part)
        parts.append(part)
    rest = jnp.concatenate(parts, axis=0)
    onehot = lane_spread(NZ // BLK).astype(jnp.bfloat16)
    wide = None
    for _ in range(3):
        piece = rest.astype(jnp.bfloat16)
        rest = rest - piece.astype(f32)
        product = jnp.dot(piece, onehot, preferred_element_type=f32)
        wide = product if wide is None else wide + product
    for k in range(7):
        for block in range(4):
            coefs_ref[k, NY * block:NY * (block + 1)] = spread_y(wide, 16 * k + 4 * block)
    even = is_even("area")
    for part in range(7):
        place = GATES * NX + BLK * part
        for block in range(4):
            low = wide[16 * part + 4 * block:16 * part + 4 * block + 1]
            high = wide[16 * part + 4 * block + 3:16 * part + 4 * block + 4]
            ev_ref[place + block:place + block + 1] = choose(even, high, low)
            od_ref[place + block:place + block + 1] = choose(even, low, high)
    for k in range(GATES):
        loads[k].wait()
        for x in range(NX):
            place = NX * k + x
            low = s_ref[k + 1, x, 0:1]
            high = s_ref[k + 1, x, NY - 1:NY]
            ev_ref[place:place + 1] = choose(even, high, low)
            od_ref[place:place + 1] = choose(even, low, high)
    spare = pl.ds(GATES * NX + 7 * BLK, BLK)
    ev_ref[spare] = jnp.zeros((BLK, NZ), f32)
    od_ref[spare] = jnp.zeros((BLK, NZ), f32)
    loads[6].wait()


def message_kernel(area_ev_ref, area_od_ref, u_ref, _e, _o, ev_ref, od_ref, rows_ref, _gates_ev, _gates_od):
    even = is_even("depth")
    below, above = neighbours("area", area_ev_ref[...], area_od_ref[...])
    rows_ref[0], rows_ref[2] = below[0:NX], below[NX:2 * NX]
    rows_ref[1], rows_ref[3] = above[0:NX], above[NX:2 * NX]
    depth_messages(even, u_ref, rows_ref, ev_ref, od_ref)


def depth_messages(even, u_ref, rows_ref, ev_ref, od_ref):
    low, high = u_ref[0], u_ref[NX - 1]
    ev_ref[0:NY] = choose(even, high, low)
    od_ref[0:NY] = choose(even, low, high)
    for k in range(rows_ref.shape[0]):
        place = NY + k
        low, high = rows_ref[k, 0:1], rows_ref[k, NX - 1:NX]
        ev_ref[place:place + 1] = choose(even, high, low)
        od_ref[place:place + 1] = choose(even, low, high)


def z_sides(u):
    lane = lax.broadcasted_iota(jnp.int32, (1, NZ), 1)
    after = jnp.where(lane == NZ - 1, 0.0, pltpu.roll(u, NZ - 1, axis=1))
    before = jnp.where(lane == 0, 0.0, pltpu.roll(u, 1, axis=1))
    return after, before


def y_sides(u, row_lo, row_hi):
    row = lax.broadcasted_iota(jnp.int32, (NY, 1), 0)
    after = jnp.where(row == NY - 1, row_hi, pltpu.roll(u, NY - 1, axis=0))
    before = jnp.where(row == 0, row_lo, pltpu.roll(u, 1, axis=0))
    return after, before


def z_slope(u):
    after, before = z_sides(u)
    return after - before


def y_slope(u, row_lo, row_hi):
    after, before = y_sides(u, row_lo, row_hi)
    return after - before


def derive(planes, u_ref, coefs_ref, rows_ref, uy_ref, uz_ref, w_ref):
    row_lo = rows_ref[0]
    row_hi = rows_ref[1]
    rowz_lo = z_slope(row_lo)
    rowz_hi = z_slope(row_hi)
    for x in planes:
        rows = slice(x // BLK * NY, x // BLK * NY + NY)
        row = slice(x, x + 1)
        u = u_ref[x]
        after, before = z_sides(u)
        uz = after - before
        uz_ref[x] = uz
        w = 0.52 * u + coefs_ref[3, rows] * (after + before)
        after, before = y_sides(u, row_lo[row], row_hi[row])
        uy_ref[x] = after - before
        w = w + coefs_ref[2, rows] * (after + before)
        after, before = y_sides(uz, rowz_lo[row], rowz_hi[row])
        w_ref[x] = w + coefs_ref[6, rows] * (after - before)


def ionic(w, gates, calcium):
    fresh = []
    for k in range(6):
        keep = math.exp(-TIME_STEP * RATES[k])
        half = 0.5 * (1.0 - keep)
        t = jnp.tanh((0.5 * SLOPES[k]) * w - (0.5 * SLOPES[k] * MIDDLES[k]))
        fresh.append(half * t + (keep * gates[k] + half))
    both = fresh[3] * fresh[4]
    cube = fresh[0] * fresh[0] * fresh[0]
    loss = (
        (2.0 * TIME_STEP) * (cube * fresh[1]) * (w - 1.2)
        + TIME_STEP * (fresh[2] * fresh[2]) * (w + 0.1)
        + (0.6 * TIME_STEP) * both * (w - 0.9)
        + (0.2 * TIME_STEP) * (1.0 + fresh[5]) * (w - 0.05)
    )
    gain = (1.5 * TIME_STEP) * both
    calc_next = (1.0 - 0.8 * TIME_STEP) * calcium + gain * (1.0 - calcium)
    return w - loss, fresh, calc_next


def march(q, opaque, state):
    passed, red, green = state
    alpha = opaque * jnp.tanh(3.0 * q - 1.2) + opaque
    weight = passed * alpha
    off = q - 0.5
    red = red + weight * jnp.tanh(2.5 * off)
    green = green + weight * jnp.exp(-6.0 * (off * off))
    return passed - weight, red, green


def advance(w, old, inside):
    volt, fresh, calc = ionic(w, old[1:7], old[7])
    return [jnp.where(inside, a, b) for a, b in zip([volt] + fresh + [calc], old)]


def show(new, m, marches):
    return [march(q, (0.5 * OPACITY[f]) * m, marches[f]) for f, q in enumerate((new[0], new[7]))]


def interior_planes(planes, marches_of, s_ref, u_ref, next_ref, coefs_ref, uy_ref, uz_ref, w_ref, shown_ref):
    def chunk(j, carry):
        cols = pl.ds(pl.multiple_of(j * CHUNK, CHUNK), CHUNK)
        marches = marches_of(cols)
        for x in planes:
            rows = slice(x // BLK * NY, x // BLK * NY + NY)
            m = coefs_ref[0, rows, cols]
            w = (
                w_ref[x, :, cols]
                + coefs_ref[1, rows, cols] * (u_ref[x + 1, :, cols] + u_ref[x - 1, :, cols])
                + coefs_ref[4, rows, cols] * (uy_ref[x + 1, :, cols] - uy_ref[x - 1, :, cols])
                + coefs_ref[5, rows, cols] * (uz_ref[x + 1, :, cols] - uz_ref[x - 1, :, cols])
            )
            new = advance(w, [s_ref[k, x, :, cols] for k in range(8)], m > 0.5)
            for k in range(8):
                s_ref[k, x, :, cols] = new[k]
            if next_ref is not None:
                next_ref[x, :, cols] = m * new[0]
            marches = show(new, m, marches)
        for f in range(2):
            for k in range(3):
                shown_ref[3 * f + k, :, cols] = marches[f][k]
        return carry

    lax.fori_loop(0, NZ // CHUNK, chunk, 0)


def base_of(x, beside, sign, u_ref, coefs_ref, uy_ref, uz_ref, w_ref):
    rows = slice(x // BLK * NY, x // BLK * NY + NY)
    return (
        w_ref[x]
        + coefs_ref[1, rows] * u_ref[beside]
        + sign * (coefs_ref[4, rows] * uy_ref[beside] + coefs_ref[5, rows] * uz_ref[beside])
    )


def interior_kernel(last, refs):
    u_ref, coefs_ref, rows_ref = refs[1:4]
    if last:
        next_ref = None
        s_ref, shown_ref, base_ref, final_ref, uy_s, uz_s, w_s, sem = refs[4:]
    else:
        s_ref, shown_ref, base_ref, next_ref, uy_s, uz_s, w_s = refs[4:]
    derive(range(NX), u_ref, coefs_ref, rows_ref, uy_s, uz_s, w_s)
    base_ref[0] = base_of(0, 1, 1.0, u_ref, coefs_ref, uy_s, uz_s, w_s)
    base_ref[1] = base_of(NX - 1, NX - 2, -1.0, u_ref, coefs_ref, uy_s, uz_s, w_s)
    copies = []
    one = jnp.ones((NY, CHUNK), f32)
    zero = jnp.zeros((NY, CHUNK), f32)
    for n in range(len(GROUPS) - 1):
        def marches_of(cols):
            if n == 0:
                return [(one, zero, zero)] * 2
            return [tuple(shown_ref[3 * f + k, :, cols] for k in range(3)) for f in range(2)]

        interior_planes(range(GROUPS[n], GROUPS[n + 1]), marches_of,
                        s_ref, u_ref, next_ref, coefs_ref, uy_s, uz_s, w_s, shown_ref)
        if last and n < len(GROUPS) - 2:
            done = pl.ds(GROUPS[n], GROUPS[n + 1] - GROUPS[n])
            copies.append(pltpu.make_async_copy(s_ref.at[:, done], final_ref.at[:, done], sem.at[n]))
            copies[n].start()
    for copy in copies:
        copy.wait()


def outer_row(side, halos, rows_ref, own_ref, record):
    near, far, own = rows_ref[side], rows_ref[2 + side], own_ref[side]
    turn = 1.0 if side else -1.0
    near_place, far_place = NY + side, NY + 2 + side
    own_place = NY - 1 if side else 0

    def across(halo, place):
        return halo[place:place + 1]

    slope = turn * (far - own)
    slopes = [turn * (across(h, far_place) - across(h, own_place)) for h in halos]
    zs = [across(z_slope(h), near_place) for h in halos]
    mask = spread_y(record[GATES * NX:GATES * NX + 4], 0)
    coefs = [spread_y(record[GATES * NX + BLK * k:GATES * NX + BLK * (k + 1)], 0) for k in range(1, 7)]
    x_after, x_before = y_sides(near, across(halos[0], near_place), across(halos[1], near_place))
    z_after, z_before = z_sides(near)
    w = (
        0.52 * near
        + coefs[0] * (x_after + x_before)
        + coefs[1] * (own + far)
        + coefs[2] * (z_after + z_before)
        + coefs[3] * y_slope(slope, *slopes)
        + coefs[4] * y_slope(z_after - z_before, *zs)
        + coefs[5] * z_slope(slope)
    )
    gates = [record[NX * k:NX * (k + 1)] for k in range(GATES)]
    return mask * ionic(w, gates, jnp.zeros_like(w))[0]


def ends_body(last, refs):
    bases_ref, coefs_ref, depth_ev_ref, depth_od_ref, shown_ref = refs[:5]
    if last:
        earlier_ref, _, _, s_ref, final_ref, strips_ref, acc_s, uy_s, uz_s, sem = refs[5:]
        done = pl.ds(GROUPS[-2], GROUPS[-1] - GROUPS[-2])
        stores = [pltpu.make_async_copy(s_ref.at[:, done], final_ref.at[:, done], sem.at[2])]
        stores[0].start()
    else:
        (gates_ev_ref, gates_od_ref, rows_ref, own_ref, _, _,
         s_ref, next_ref, acc_s, ahead_ref, ev_ref, od_ref, uy_s, uz_s) = refs[5:]
    even = is_even("depth")
    halos = neighbours("depth", depth_ev_ref[...], depth_od_ref[...])
    if not last:
        records = neighbours("area", gates_ev_ref[...], gates_od_ref[...])
        for side in range(2):
            ahead_ref[side] = outer_row(side, halos, rows_ref, own_ref, records[side])
    for end, x, sign in ((0, 0, -1.0), (1, NX - 1, 1.0)):
        rows = slice(x // BLK * NY, x // BLK * NY + NY)
        halo = halos[end]
        u = halo[0:NY]
        uz_s[...] = sign * z_slope(u)
        uy_s[...] = sign * y_slope(u, halo[NY:NY + 1], halo[NY + 1:NY + 2])
        for j in range(NZ // CHUNK):
            cols = slice(j * CHUNK, (j + 1) * CHUNK)
            m = coefs_ref[0, rows, cols]
            w = (
                bases_ref[end, :, cols]
                + coefs_ref[1, rows, cols] * u[:, cols]
                + coefs_ref[4, rows, cols] * uy_s[:, cols]
                + coefs_ref[5, rows, cols] * uz_s[:, cols]
            )
            new = advance(w, [s_ref[k, x, :, cols] for k in range(8)], m > 0.5)
            for k in range(8):
                s_ref[k, x, :, cols] = new[k]
            if not last:
                next_ref[x, :, cols] = m * new[0]
            if end == 0:
                one = jnp.ones((NY, CHUNK), f32)
                zero = jnp.zeros((NY, CHUNK), f32)
                marches = show(new, m, [(one, zero, zero)] * 2)
            else:
                marches = [tuple(acc_s[3 * f + k, :, cols] for k in range(3)) for f in range(2)]
                marches = show(new, m, marches)
            for f in range(2):
                passed, red, green = marches[f]
                if end == 0:
                    red = red + passed * shown_ref[3 * f + 1, :, cols]
                    green = green + passed * shown_ref[3 * f + 2, :, cols]
                    passed = passed * shown_ref[3 * f, :, cols]
                for k, item in enumerate((passed, red, green)):
                    acc_s[3 * f + k, :, cols] = item
        if last:
            stores.append(pltpu.make_async_copy(s_ref.at[:, x], final_ref.at[:, x], sem.at[end]))
            stores[-1].start()
    if not last:
        depth_messages(even, next_ref, ahead_ref, ev_ref, od_ref)
    else:
        stacks = [jnp.concatenate([earlier_ref[k], earlier_ref[3 + k], acc_s[k], acc_s[3 + k]], axis=0)
                  for k in range(3)]
        turned = jnp.concatenate(stacks[:2], axis=0).T
        greens = jnp.concatenate([stacks[2], pltpu.roll(stacks[2], NZ - HALF, axis=1)], axis=0).T
        left = lax.broadcasted_iota(jnp.int32, (1, 128), 1) < 64
        for d in range(NZ // STRIP):
            start = STRIP * d
            a, b = turned[start:start + HALF], turned[start + HALF:start + STRIP]
            strips_ref[d, 0:HALF] = jnp.where(left, a, pltpu.roll(b, 64, axis=1))
            strips_ref[d, HALF:2 * HALF] = jnp.where(left, pltpu.roll(a, 64, axis=1), b)
            strips_ref[d, 2 * HALF:3 * HALF] = greens[start:start + HALF]
        for store in stores:
            store.wait()


def composite_kernel(strips_ref, out_ref):
    count = strips_ref.shape[0]
    passed = jnp.ones((HALF, 128), f32)
    red = jnp.zeros((HALF, 128), f32)
    green = jnp.zeros((HALF, 128), f32)
    for s in range(count):
        red = red + passed * strips_ref[s, HALF:2 * HALF]
        green = green + passed * strips_ref[s, 2 * HALF:3 * HALF]
        passed = passed * strips_ref[s, 0:HALF]
    solid = 1.0 - passed
    red = 0.5 * (solid + red)
    whole = jnp.concatenate([red, green, solid - red, solid, jnp.zeros((32, 128), f32)], axis=0)
    turned = whole.T
    first, second = turned[0:64], turned[64:128]
    lane = lax.broadcasted_iota(jnp.int32, (1, 128), 1)
    for c in range(4):
        a = pltpu.roll(first, (128 - HALF * c) % 128, axis=1) if c else first
        b = pltpu.roll(second, (128 + HALF - HALF * c) % 128, axis=1) if c != 1 else second
        o = jnp.where(lane < HALF, a, b)
        for k in range(4):
            out_ref[k // 2, k % 2, c] = o[NY * k:NY * (k + 1), 0:STRIP]


VOLUME = (8, NX, NY, NZ)
FIELD = (NX, NY, NZ)
PLANE = (NY, NZ)
SHOWN = (6, NY, NZ)
COPY = pltpu.SemaphoreType.DMA


def shapes_of(*shapes):
    return [jax.ShapeDtypeStruct(s, f32) for s in shapes]


def kept_in(space, *shapes):
    return [space(s, f32) for s in shapes]


def anywhere():
    return pl.BlockSpec(memory_space=pl.ANY)


def inside():
    return pl.BlockSpec(memory_space=pltpu.VMEM)


def cost():
    voxels = NX * NY * NZ
    return pl.CostEstimate(flops=400 * voxels, bytes_accessed=32 * voxels, transcendentals=12 * voxels)


def interior(last, states, u, coefs, rows):
    out_specs = [inside()] * 3
    out_shape = kept_in(pltpu.VMEM, VOLUME, SHOWN, (2, NY, NZ))
    scratch = [pltpu.VMEM(FIELD, f32)] * 3
    if last:
        out_specs += [anywhere()]
        out_shape += kept_in(pltpu.HBM, VOLUME)
        scratch += [COPY((len(GROUPS) - 2,))]
    else:
        out_specs += [inside()]
        out_shape += kept_in(pltpu.VMEM, FIELD)
    return pl.pallas_call(
        lambda *refs: interior_kernel(last, refs),
        in_specs=[inside()] * 4,
        out_specs=out_specs,
        out_shape=out_shape,
        scratch_shapes=scratch,
        input_output_aliases={0: 0},
        compiler_params=params(8),
        cost_estimate=cost(),
        name="interior_last" if last else "interior_first",
    )(states, u, coefs, rows)


def ends(last, bases, coefs, depth, shown, rest):
    args = [bases, coefs, *depth, shown, *rest]
    in_specs = [inside()] * len(args)
    aliases = {len(args) - 2: 0, len(args) - 1: 1}
    scratch = [pltpu.VMEM(PLANE, f32)] * 2
    if last:
        out_shape = kept_in(pltpu.VMEM, VOLUME) + kept_in(pltpu.HBM, VOLUME)
        out_shape += kept_in(pltpu.VMEM, (NZ // STRIP, 3 * HALF, 128))
        scratch = [pltpu.VMEM(SHOWN, f32), *scratch, COPY((3,))]
        in_specs[-1] = anywhere()
        out_specs = [inside(), anywhere(), inside()]
    else:
        out_shape = kept_in(pltpu.VMEM, VOLUME, FIELD, SHOWN, (2, NX, NZ), (NY + 2, NZ), (NY + 2, NZ))
        out_specs = [inside()] * 6
    return pl.pallas_call(
        lambda *refs: ends_body(last, refs),
        in_specs=in_specs,
        out_specs=out_specs,
        out_shape=out_shape,
        scratch_shapes=scratch,
        input_output_aliases=aliases,
        compiler_params=params(4),
        name="ends_last" if last else "ends_first",
    )(*args)


def swaps(axis):
    count = lax.axis_size(axis)
    return [(i, i ^ 1) for i in range(count)], [(i, (((i - 1) ^ 1) + 1) % count) for i in range(count)]


def swap(axis, which, message):
    return lax.ppermute(message, axis, swaps(axis)[which])


def per_device(states, tissue, fiber):
    blocks = (NX // BLK, NY // BLK, NZ // BLK)
    states = pltpu.with_memory_space_constraint(states, pltpu.HBM)
    tissue = pltpu.with_memory_space_constraint(tissue, pltpu.HBM)
    kept, u, ev, od, own = pl.pallas_call(
        faces_kernel,
        in_specs=[anywhere(), anywhere()],
        out_shape=kept_in(pltpu.VMEM, VOLUME, FIELD, (2 * NX, NZ), (2 * NX, NZ), (2, NX, NZ)),
        scratch_shapes=[pltpu.VMEM(blocks, jnp.int32), COPY((1 + NX // BLK,))],
        compiler_params=params(4),
        name="faces",
    )(tissue, states)
    area = swap("area", 0, ev), swap("area", 1, od)
    states, coefs, ev, od = pl.pallas_call(
        load_kernel,
        in_specs=[inside(), inside(), anywhere(), inside()],
        out_shape=kept_in(pltpu.VMEM, VOLUME, (7, 64, NZ), (RECORD, NZ), (RECORD, NZ)),
        scratch_shapes=[COPY((7,))],
        input_output_aliases={3: 0},
        compiler_params=params(4),
        cost_estimate=pl.CostEstimate(flops=10**7, bytes_accessed=8 * 10**6, transcendentals=0),
        name="load",
    )(tissue, fiber, states, kept)
    ev, od, rows, gates_ev, gates_od = pl.pallas_call(
        message_kernel,
        in_specs=[inside()] * 3 + [anywhere()] * 2,
        out_specs=[inside()] * 3 + [anywhere()] * 2,
        out_shape=kept_in(pltpu.VMEM, (NY + 4, NZ), (NY + 4, NZ), (4, NX, NZ), (RECORD, NZ), (RECORD, NZ)),
        input_output_aliases={3: 3, 4: 4},
        compiler_params=params(1),
        name="depth_message",
    )(*area, u, ev, od)
    gates = swap("area", 0, gates_ev), swap("area", 1, gates_od)
    depth = swap("depth", 0, ev), swap("depth", 1, od)
    states, shown, bases, after = interior(False, states, u, coefs, rows)
    states, u, images, rows, ev, od = ends(
        False, bases, coefs, depth, shown, (*gates, rows, own, states, after))
    depth = swap("depth", 0, ev), swap("depth", 1, od)
    states, shown, bases, final = interior(True, states, u, coefs, rows)
    _, states, strips = ends(True, bases, coefs, depth, shown, (images, states, final))
    strips = lax.all_to_all(strips, "depth", split_axis=0, concat_axis=0, tiled=True)
    images = pl.pallas_call(
        composite_kernel,
        out_shape=jax.ShapeDtypeStruct((2, 2, 4, NY, STRIP), f32),
        compiler_params=params(4),
        name="composite",
    )(strips)
    return states, images


def solution(mesh):
    return jax.shard_map(
        per_device,
        mesh=mesh,
        in_specs=(
            P(None, "depth", "area", None),
            P("depth", "area", None),
            P("depth", "area", None),
        ),
        out_specs=(P(None, "depth", "area", None), P(None, None, None, "area", "depth")),
        check_vma=False,
    )
```
